32 devices in a mesh: groups: 2 (over x), seq: 16 (over z, y, core).
Axes of the slice: x: 2, y: 2, z: 4, core: 2. Of those that a mesh axis runs over, the one named last changes fastest.
Arguments:
- prefill_kv: bfloat16 [4096, 576], P(('groups', 'seq')), parts along dimension 0, may hold values from -6 to 6
- lengths: int32 [128], P('groups'), parts along dimension 0, may hold values from 1 to 63, as said below
- assignment: int32 [128], P('groups'), parts along dimension 0, may hold values from 0 to 63, as said below
- queries: bfloat16 [4, 128, 64, 576], P(None, ('groups', 'seq')), parts along dimension 1, may hold values from -60 to 60
- new_kv: bfloat16 [4, 128, 576], P(None, ('groups', 'seq')), parts along dimension 1, may hold values from -6 to 6
- expert_hidden: bfloat16 [128, 4, 8, 1024], P(('groups', 'seq')), parts along dimension 0, may hold values from -6 to 6
- routes: int32 [128, 4, 8], P(('groups', 'seq')), parts along dimension 0, may hold values from 0 to 15, all different within a row; in each aligned block of 16 rows (0 to 15, 16 to 31, ..., all dimensions but the last counted through in order) at most 16 rows name the same one
- route_weights: float32 [128, 4, 8], P(('groups', 'seq')), parts along dimension 0, may hold values from 0.05 to 0.5
- expert_down: bfloat16 [16, 1024, 3584], P('seq'), may hold values from -0.1875 to 0.1875
Outputs:
- context: bfloat16 [4, 128, 64, 512], P(None, ('groups', 'seq')), parts along dimension 1
- moe_out: bfloat16 [128, 4, 3584], P(('groups', 'seq')), parts along dimension 0
The draws below stay inside these ranges and needn't reach their ends.
There are 2 independent parts, one for each index of `groups`. The reference program is written for one: setup_inputs(seed, part) draws one part's arguments, and reference() takes and returns one part's arrays. A program takes and returns all parts, laid end to end along the dimension named above; an argument that names none is the same for every part. Nothing has to cross between parts.
Inputs may be any that keep to these rules, and one draw needn't show every extreme that they name: `lengths`: each length is 1 to 63; they sum to 2048; 63 is reached. `assignment`: A permutation of the requests. The rows that one device holds of prefill_kv include at most 16 rows of the requests of any one decoding device, and some device reaches 16. Within the routes of one device's rows no expert is named more than 16 times, and some expert reaches it.
All inputs are finite; a program needn't handle non-finite values.
Results may differ from the reference program's by a relative error of at most 0.0051.
Values may be sent and summed in bfloat16 or wider, within the bound.
No kernel may reach another device: no remote copies, remote signals or barrier semaphores. Data moves between devices by JAX's collectives and lax.ppermute only.
A program may use at most 64 MiB of HBM per device.

```python
import math
import jax
import jax.numpy as jnp
import numpy as np
from jax import lax

HEADS = 64
LAT = 512
KVW = 576
D = 3584
HID = 1024
TOP = 8
EXPERTS = 16
STEPS = 4
REQ_DEV = 4
ROWS = 64
REQS = 64
CTX_DEV = 128
CTX = 2048
MOST = 63
RPAD = 64
ECAP = 16
N_SEQ = 16


def request_plan(key):
    key_a, key_b, key_c, key_d = jax.random.split(key, 4)
    owner_count = ROWS // REQ_DEV
    pair_count = REQS // 2
    first_length = jax.random.randint(key_a, (pair_count,), 1, MOST + 1, dtype=jnp.int32)
    chosen = jax.random.permutation(key_b, pair_count)[:REQ_DEV].astype(jnp.int32)
    first_length = first_length.at[chosen].set(MOST)
    lengths = jnp.stack([first_length, MOST + 1 - first_length], axis=1).reshape(-1).astype(jnp.int32)
    forced = jnp.zeros((REQS,), jnp.int32).at[2 * chosen].set(1)
    shuffled = jax.random.permutation(key_c, REQS).astype(jnp.int32)
    within = shuffled[jnp.argsort(1 - forced[shuffled], stable=True)]
    blocks = within.reshape(owner_count, REQ_DEV)
    owners = jax.random.permutation(key_d, owner_count).astype(jnp.int32)
    assignment = jnp.zeros((owner_count, REQ_DEV), jnp.int32).at[owners].set(blocks).reshape(-1)
    return (lengths, assignment)


def fresh_latents(key):
    return jnp.clip(jax.random.normal(key, (STEPS, ROWS, KVW), jnp.float32), -6.0, 6.0)


def draw_lengths(key, part):
    plan = request_plan(key)
    return plan[0]


def draw_assignment(key, part):
    plan = request_plan(key)
    return plan[1]


def draw_new_kv(key, part):
    base_draw = fresh_latents(key)
    return base_draw.astype(jnp.bfloat16)


def draw_queries(key, part):
    key = jax.random.fold_in(key, 4)
    key_a = jax.random.fold_in(key, 0)
    base_draw = jnp.clip(jax.random.normal(key_a, (STEPS, ROWS, HEADS, KVW), jnp.float32), -6.0, 6.0)
    return base_draw.astype(jnp.bfloat16)


def block_levels(rng, shape, shards, smallest, largest):
    loudness, own = 1.0, jax.random.fold_in(rng, 6)
    for position, parts in shards:
        draws = jnp.exp(jax.random.uniform(jax.random.fold_in(own, position), (parts,), jnp.float32, smallest / len(shards), largest / len(shards)))
        loudness = loudness * jnp.repeat(draws, shape[position] // parts).reshape([-1 if axis == position else 1 for axis in range(len(shape))])
    return loudness


def assign_block(key, own, number, rows, count, top, reach, lean):
    sequence = jax.random.permutation(key, count)
    heavy_load, usual = load_shares(count, rows * top, reach, lean, True), load_shares(count, rows * top, reach, lean, False)
    places = jnp.arange(count)

    def named(sizes, turn):
        used = int((sizes > 0).sum())
        fixed = max(1, used // 4)
        moved = fixed + (places - fixed + turn * (used - fixed)) % max(1, count - fixed)
        return jnp.zeros((count,), jnp.int32).at[sequence[jnp.where(places < fixed, places, moved)]].set(jnp.asarray(sizes, jnp.int32))

    sizes = jnp.where(number % 4 == 0, named(heavy_load, number // 4), named(usual, number - number // 4 - 1))
    mixed = jax.random.permutation(jax.random.fold_in(own, 3), count)
    source_of, sink = mixed[0:count // 2 * 2:2], mixed[1:count // 2 * 2:2]
    margin = jnp.minimum(sizes[source_of] - 1, reach - sizes[sink]) // 2
    margin = jnp.where((source_of == sequence[0]) | (sink == sequence[0]) | (sizes[sink] == 0), 0, jnp.maximum(margin, 0))
    moved = jax.random.randint(jax.random.fold_in(own, 4), (count // 2,), 0, 1 << 20) % (margin + 1)
    sizes = sizes.at[source_of].add(-moved).at[sink].add(moved)
    labels = jnp.searchsorted(jnp.cumsum(sizes), jnp.arange(rows * top), side="right").astype(jnp.int32)
    table = labels.reshape(top, rows).T
    table = table[jax.random.permutation(jax.random.fold_in(own, 1), rows)]
    turn = jax.random.randint(jax.random.fold_in(own, 2), (rows, 1), 0, top)
    return jnp.take_along_axis(table, (jnp.arange(top)[None, :] + turn) % top, axis=1)


def load_shares(count, total, bound, skew, full):
    portions = [(1 << 20) // math.isqrt(rank ** skew) + 1 for rank in range(1, count + 1)]
    largest = bound if full else min(bound, max(-(-total // count), total * portions[0] // sum(portions)))
    least = 1 if total - largest >= count - 1 else 0
    given, surplus = [largest] + [least] * (count - 1), total - largest - least * (count - 1)
    while surplus > 0:
        candidates = [i for i in range(1, count) if given[i] < largest] or [i for i in range(1, count) if given[i] < bound]
        pool, budget = sum([portions[i] for i in candidates]), surplus
        for i in candidates:
            more = min(bound - given[i], max(1, budget * portions[i] // pool), surplus)
            given[i] = given[i] + more
            surplus = surplus - more
    return np.array(given)


def centred(stream_key, extent, deviation, most, cuts=(), kind=jnp.bfloat16):
    drawn = deviation * jax.random.normal(stream_key, extent, jnp.float32)
    if cuts:
        drawn = drawn * block_levels(stream_key, extent, cuts, -0.22, 0.18)
    return jnp.clip(drawn, -most, most).astype(kind)


def setup_inputs(seed: int = 0, part: int = 0) -> dict:
    seeds = jax.random.split(jax.random.key(seed), 10)
    part_keys = jax.random.split(jax.random.fold_in(seeds[9], part), 10)
    prefill_kv = centred(part_keys[0], (CTX, KVW), 1.0, 6.0, ((0, 16),))
    lengths = draw_lengths(jax.random.fold_in(jax.random.fold_in(seeds[9], part), 71), part)
    assignment = draw_assignment(jax.random.fold_in(jax.random.fold_in(seeds[9], part), 71), part)
    queries = draw_queries(jax.random.fold_in(jax.random.fold_in(seeds[9], part), 71), part)
    new_kv = draw_new_kv(jax.random.fold_in(jax.random.fold_in(seeds[9], part), 71), part)
    expert_hidden = centred(part_keys[5], (ROWS, STEPS, TOP, HID), 1.0, 6.0, ((0, 16),))
    routes_keys = jax.random.split(jax.random.fold_in(part_keys[6], 1), ROWS * STEPS // (STEPS * REQ_DEV))
    routes_turns = jax.random.permutation(jax.random.fold_in(part_keys[6], 3), ROWS * STEPS // (STEPS * REQ_DEV))
    routes = jax.vmap(lambda own, number: assign_block(jax.random.fold_in(part_keys[6], 2), own, number, STEPS * REQ_DEV, EXPERTS, TOP, ECAP, 2))(routes_keys, routes_turns).reshape((ROWS, STEPS, TOP))
    route_weights = jnp.clip(jnp.exp(math.log(0.5) - 2.3025851 * jax.random.uniform(part_keys[7], (ROWS, STEPS, TOP), jnp.float32) ** block_levels(part_keys[7], (ROWS, STEPS, TOP), ((0, 16),), -0.2, 0.2)), 0.05, 0.5)
    expert_down = centred(seeds[8], (EXPERTS, HID, D), HID ** -0.5, 0.1875, ((0, 16),))
    return {"prefill_kv": prefill_kv, "lengths": lengths, "assignment": assignment, "queries": queries, "new_kv": new_kv, "expert_hidden": expert_hidden, "routes": routes, "route_weights": route_weights, "expert_down": expert_down}


score_scale = 192.0 ** -0.5
masked_score = -1.0e30


def attend_request(padded, start_row, length, query_rows, fresh_rows):
    window = lax.dynamic_slice(padded, (start_row.astype(jnp.int32), jnp.zeros((), jnp.int32)), (RPAD, KVW))
    query_f = query_rows.astype(jnp.float32)
    window_f = window.astype(jnp.float32)
    fresh_f = fresh_rows.astype(jnp.float32)
    scores = jnp.einsum("shk,tk->sht", query_f, window_f) * score_scale
    in_range = jnp.arange(RPAD, dtype=jnp.int32) < length
    scores = jnp.where(in_range[None, None, :], scores, masked_score)
    fresh_scores = jnp.einsum("shk,uk->shu", query_f, fresh_f) * score_scale
    causal = jnp.arange(STEPS)[:, None] >= jnp.arange(STEPS)[None, :]
    fresh_scores = jnp.where(causal[:, None, :], fresh_scores, masked_score)
    top_score = jnp.maximum(jnp.max(scores, axis=-1), jnp.max(fresh_scores, axis=-1))
    weights = jnp.exp(scores - top_score[..., None])
    fresh_weights = jnp.exp(fresh_scores - top_score[..., None])
    denominator = jnp.sum(weights, axis=-1) + jnp.sum(fresh_weights, axis=-1)
    rounded = lax.optimization_barrier(weights.astype(jnp.bfloat16)).astype(jnp.float32)
    fresh_rounded = lax.optimization_barrier(fresh_weights.astype(jnp.bfloat16)).astype(jnp.float32)
    summed = jnp.einsum("sht,tl->shl", rounded, window_f[:, :LAT]) + jnp.einsum("shu,ul->shl", fresh_rounded, fresh_f[:, :LAT])
    return (summed / denominator[..., None]).astype(jnp.bfloat16)


def reference(prefill_kv, lengths, assignment, queries, new_kv, expert_hidden, routes, route_weights, expert_down):
    packed = prefill_kv.reshape(N_SEQ, CTX_DEV, KVW).transpose(1, 0, 2).reshape(CTX, KVW)
    padded = jnp.concatenate([packed, jnp.zeros((RPAD, KVW), packed.dtype)], axis=0)
    starts = (jnp.cumsum(lengths) - lengths).astype(jnp.int32)

    def one_row(row_index):
        request = assignment[row_index]
        return attend_request(padded, starts[request], lengths[request], queries[:, row_index], new_kv[:, row_index])

    context = lax.map(one_row, jnp.arange(ROWS, dtype=jnp.int32))
    context = jnp.transpose(context, (1, 0, 2, 3))

    flat_routes = routes.reshape(-1).astype(jnp.int32)
    route_count = flat_routes.shape[0]
    sorted_routes = jnp.argsort(flat_routes, stable=True).astype(jnp.int32)
    all_experts = jnp.arange(EXPERTS, dtype=jnp.int32)
    loads = jnp.sum((flat_routes[:, None] == all_experts[None, :]).astype(jnp.int32), axis=0)
    firsts = (jnp.cumsum(loads) - loads).astype(jnp.int32)
    flat_hidden = expert_hidden.reshape(route_count, HID)
    limit = ECAP * N_SEQ
    padded_order = jnp.concatenate([sorted_routes, jnp.zeros((limit,), jnp.int32)])

    def run_expert(expert_index):
        chosen = lax.dynamic_slice(padded_order, (firsts[expert_index].astype(jnp.int32),), (limit,))
        return jnp.dot(flat_hidden[chosen], expert_down[expert_index], preferred_element_type=jnp.float32).astype(jnp.bfloat16)

    outputs = lax.map(run_expert, all_experts)
    placed = jnp.zeros((route_count,), jnp.int32).at[sorted_routes].set(jnp.arange(route_count, dtype=jnp.int32))
    slot_rank = placed - firsts[flat_routes]
    picked = outputs[flat_routes, slot_rank].astype(jnp.float32)
    weighted = picked * route_weights.reshape(route_count, 1).astype(jnp.float32)
    moe_out = jnp.sum(weighted.reshape(ROWS, STEPS, TOP, D), axis=2).astype(jnp.bfloat16)
    return (context, moe_out)
```

```python
import functools

import jax
import jax.numpy as jnp
from jax import lax
from jax.experimental import pallas as pl
from jax.experimental.pallas import tpu as pltpu
from jax.sharding import PartitionSpec as P

ROPE = 64
HALF = 2


score_scale = 192.0 ** (-0.5)
masked_score = -1e30


def slot_sources(slot_ids, slot_total):
    source_rows = jnp.arange(slot_ids.shape[0], dtype=jnp.int32)
    matched = slot_ids[None, :] == jnp.arange(slot_total, dtype=jnp.int32)[:, None]
    return jnp.max(jnp.where(matched, source_rows[None, :], -1), axis=1)


def fill_slots(values, sources, filler):
    taken = jnp.take(values, jnp.maximum(sources, 0), axis=0)
    valid = (sources >= 0).reshape((-1,) + (1,) * (values.ndim - 1))
    return jnp.where(valid, taken, jnp.asarray(filler, values.dtype))


def hand_over(prefill_kv, lengths, assignment, per_owner):
    device_count = lax.axis_size("seq")
    own_index = lax.axis_index("seq")
    ctx_here, kv_width = prefill_kv.shape
    position = jnp.arange(ctx_here, dtype=jnp.int32) * device_count + own_index
    request_ends = jnp.cumsum(lengths)
    request = jnp.sum((position[:, None] >= request_ends[None, :]).astype(jnp.int32), axis=1)
    total_rows = assignment.shape[0]
    row_numbers = jnp.arange(total_rows, dtype=jnp.int32)
    serving = jnp.sum(
        jnp.where(assignment[None, :] == row_numbers[:, None], row_numbers[None, :], 0), axis=1
    )
    decode_row = jnp.sum(
        jnp.where(request[:, None] == row_numbers[None, :], serving[None, :], 0), axis=1
    )
    owner_index = decode_row // per_owner
    local_request = decode_row % per_owner
    onehot = (owner_index[:, None] == jnp.arange(device_count, dtype=jnp.int32)[None, :]).astype(
        jnp.int32
    )
    slot_rank = jnp.sum((jnp.cumsum(onehot, axis=0) - onehot) * onehot, axis=1)
    slot_count = 2 * HALF * per_owner
    sources = slot_sources(owner_index * slot_count + slot_rank, device_count * slot_count)
    outbox = fill_slots(prefill_kv, sources, 0).reshape(device_count, slot_count, kv_width)
    labels = fill_slots(local_request, sources, -1).reshape(device_count, slot_count)
    kv_cache, cache_tags = (
        lax.all_to_all(outbox, "seq", split_axis=0, concat_axis=0, tiled=True),
        lax.all_to_all(labels, "seq", split_axis=0, concat_axis=0, tiled=True),
    )
    return (kv_cache.reshape(device_count * slot_count, kv_width), cache_tags.reshape(-1))


def fresh_part(queries, new_kv):
    step_count = queries.shape[0]
    fresh_scores = (
        jnp.einsum("sqhk,uqk->sqhu", queries, new_kv, preferred_element_type=jnp.float32)
        * score_scale
    )
    causal = jnp.arange(step_count)[:, None] >= jnp.arange(step_count)[None, :]
    return jnp.where(causal[:, None, None, :], fresh_scores, masked_score)


def attend_dense(queries, new_kv, kv_cache, cache_tags):
    step_count, per_owner, head_count, kv_width = queries.shape
    latent = kv_width - ROPE
    query_rows = queries.reshape(step_count * per_owner * head_count, kv_width)
    scores = (
        jnp.einsum("rk,ck->rc", query_rows, kv_cache, preferred_element_type=jnp.float32)
        * score_scale
    )
    row_request = jnp.broadcast_to(
        jnp.arange(per_owner, dtype=jnp.int32)[None, :, None], (step_count, per_owner, head_count)
    ).reshape(-1)
    allowed = cache_tags[None, :] == row_request[:, None]
    scores = jnp.where(allowed, scores, masked_score).reshape(step_count, per_owner, head_count, -1)
    fresh_scores = fresh_part(queries, new_kv)
    top_score = jnp.maximum(jnp.max(scores, axis=-1), jnp.max(fresh_scores, axis=-1))
    weights = jnp.exp(scores - top_score[..., None])
    fresh_weights = jnp.exp(fresh_scores - top_score[..., None])
    denominator = jnp.sum(weights, axis=-1) + jnp.sum(fresh_weights, axis=-1)
    summed = jnp.einsum(
        "sqhc,cl->sqhl",
        weights.astype(jnp.bfloat16),
        kv_cache[:, :latent],
        preferred_element_type=jnp.float32,
    )
    summed = summed + jnp.einsum(
        "sqhu,uql->sqhl",
        fresh_weights.astype(jnp.bfloat16),
        new_kv[..., :latent],
        preferred_element_type=jnp.float32,
    )
    return (summed / denominator[..., None]).astype(jnp.bfloat16)


def expert_layer(expert_hidden, routes, route_weights, expert_down):
    device_count = lax.axis_size("seq")
    rows_here, step_count, top_count, hidden_width = expert_hidden.shape
    per_dev = expert_down.shape[0]
    experts = per_dev * device_count
    capacity = max(2, 2 * step_count * rows_here * top_count // experts)
    flat_routes = routes.reshape(-1)
    route_count = flat_routes.shape[0]
    onehot = (flat_routes[:, None] == jnp.arange(experts, dtype=jnp.int32)[None, :]).astype(
        jnp.int32
    )
    slot_index = jnp.sum((jnp.cumsum(onehot, axis=0) - onehot) * onehot, axis=1)
    flat_hidden = expert_hidden.reshape(route_count, hidden_width)
    slot_ids = flat_routes * capacity + slot_index
    sources = slot_sources(slot_ids, experts * capacity)
    outbox = fill_slots(flat_hidden, sources, 0).reshape(
        device_count, per_dev, capacity, hidden_width
    )
    expert_out = jnp.einsum(
        "dekh,ehm->dekm",
        lax.all_to_all(outbox, "seq", split_axis=0, concat_axis=0, tiled=True),
        expert_down,
        preferred_element_type=jnp.float32,
    ).astype(jnp.bfloat16)
    returned = lax.all_to_all(expert_out, "seq", split_axis=0, concat_axis=0, tiled=True)
    returned = returned.reshape(experts * capacity, returned.shape[-1])
    picked = jnp.take(returned, slot_ids, axis=0).astype(jnp.float32)
    weighted = picked * route_weights.reshape(route_count, 1)
    moe_out = jnp.sum(weighted.reshape(rows_here, step_count, top_count, -1), axis=2)
    return moe_out.astype(jnp.bfloat16)


def per_device_general(
    prefill_kv,
    lengths,
    assignment,
    queries,
    new_kv,
    expert_hidden,
    routes,
    route_weights,
    expert_down,
):
    kv_cache, cache_tags = hand_over(prefill_kv, lengths, assignment, queries.shape[1])
    context = attend_dense(queries, new_kv, kv_cache, cache_tags)
    moe_out = expert_layer(expert_hidden, routes, route_weights, expert_down)
    return (context, moe_out)


BLOCK = 16


def as_column(row):
    size = row.shape[1]
    eye = lax.broadcasted_iota(jnp.int32, (size, size), 0) == lax.broadcasted_iota(
        jnp.int32, (size, size), 1
    )
    return jnp.sum(jnp.where(eye, row, 0), axis=1, keepdims=True)


def flat_row(table, tokens, top):
    lanes = tokens * top
    place = lax.broadcasted_iota(jnp.int32, (top, lanes), 1) % top
    spread = (place == lax.broadcasted_iota(jnp.int32, (top, lanes), 0)).astype(jnp.float32)
    wide = jnp.dot(
        table, spread, precision=lax.Precision.HIGHEST, preferred_element_type=jnp.float32
    )
    owner = lax.broadcasted_iota(jnp.int32, (tokens, lanes), 1) // top
    mine = owner == lax.broadcasted_iota(jnp.int32, (tokens, lanes), 0)
    return jnp.sum(jnp.where(mine, wide, 0.0), axis=0, keepdims=True)


def outbox_kernel(routes_ref, weights_ref, hidden_ref, out_ref):
    rows, steps, top = routes_ref.shape
    tokens = rows * steps
    lanes = tokens * top
    slots = out_ref.shape[0]
    routes = jnp.concatenate([routes_ref[i] for i in range(rows)], axis=0).astype(jnp.float32)
    weights = jnp.concatenate([weights_ref[i] for i in range(rows)], axis=0)
    route_row = flat_row(routes, tokens, top).astype(jnp.int32)
    weight_row = flat_row(weights, tokens, top)
    slot = lax.broadcasted_iota(jnp.int32, (slots, lanes), 0)
    lane = lax.broadcasted_iota(jnp.int32, (slots, lanes), 1)
    pick = (lane // top == slot % tokens) & (route_row == slot // tokens)
    scale = jnp.sum(jnp.where(pick, weight_row, 0.0), axis=1, keepdims=True)
    chosen = jnp.where(pick, 1.0, 0.0).astype(jnp.bfloat16)
    moved = jnp.dot(chosen, hidden_ref[...], preferred_element_type=jnp.float32)
    out_ref[...] = (moved * scale).astype(jnp.bfloat16)


def pack_hidden(routes, route_weights, expert_hidden, experts):
    rows, steps, top, width = expert_hidden.shape
    tokens = rows * steps
    return pl.pallas_call(
        outbox_kernel,
        out_shape=jax.ShapeDtypeStruct((experts * tokens, width), jnp.bfloat16),
        cost_estimate=pl.CostEstimate(
            flops=2 * experts * tokens * tokens * top * width,
            bytes_accessed=2 * width * tokens * (top + experts),
            transcendentals=0,
        ),
        name="pack_hidden",
    )(routes, route_weights, expert_hidden.reshape(tokens * top, width))


def ceil_rows(position, source, devices):
    return (position + (devices - 1) - source) // devices


def kv_kernel(devices, per_owner, lengths_ref, assignment_ref, kv_ref, out_ref, tags_ref):
    me = lax.axis_index("seq")
    requests = lengths_ref.shape[1]
    here = kv_ref.shape[1]
    slots = out_ref.shape[0]
    room = slots // devices
    length_column = as_column(lengths_ref[...])
    assignment = assignment_ref[...]
    number = lax.broadcasted_iota(jnp.int32, (requests, requests), 0)
    before = jnp.sum(jnp.where(number < assignment, length_column, 0), axis=0, keepdims=True)
    own = jnp.sum(jnp.where(number == assignment, length_column, 0), axis=0, keepdims=True)
    after = before + own
    low = ceil_rows(before, me, devices)
    count = ceil_rows(after, me, devices) - low
    line = lax.broadcasted_iota(jnp.int32, (requests, requests), 1)
    same = (number // per_owner == line // per_owner) & (number < line)
    offset = jnp.sum(jnp.where(same, as_column(count), 0), axis=0, keepdims=True)
    slot = lax.broadcasted_iota(jnp.int32, (slots, requests), 0)
    decode = lax.broadcasted_iota(jnp.int32, (slots, requests), 1)
    rank = slot % room - offset
    held = (slot // room == decode // per_owner) & (rank >= 0) & (rank < count)
    source = jnp.sum(jnp.where(held, low + rank + 1, 0), axis=1, keepdims=True) - 1
    pick = source == lax.broadcasted_iota(jnp.int32, (slots, here), 1)
    out_ref[...] = lax.dot_general(
        jnp.where(pick, 1.0, 0.0).astype(jnp.bfloat16),
        kv_ref[...],
        (((1,), (1,)), ((), ())),
        preferred_element_type=jnp.float32,
    ).astype(jnp.bfloat16)
    place = lax.broadcasted_iota(jnp.int32, (1, slots), 1)
    sender, rank = place // room, place % room
    tags = jnp.full((1, slots), -1, jnp.int32)
    decode = lax.broadcasted_iota(jnp.int32, (1, requests), 1)
    taken = jnp.zeros((1, slots), jnp.int32)
    for q in range(per_owner):
        mine = decode == me * per_owner + q
        first = jnp.sum(jnp.where(mine, before, 0), axis=1, keepdims=True)
        last = jnp.sum(jnp.where(mine, after, 0), axis=1, keepdims=True)
        arriving = ceil_rows(last, sender, devices) - ceil_rows(first, sender, devices)
        tags = jnp.where((rank >= taken) & (rank < taken + arriving), q, tags)
        taken = taken + arriving
    tags_ref[...] = tags


def pack_kv(prefill_kv, lengths, assignment, devices, per_owner, room):
    here, width = prefill_kv.shape
    slots = devices * room
    return pl.pallas_call(
        functools.partial(kv_kernel, devices, per_owner),
        out_shape=(
            jax.ShapeDtypeStruct((slots, width), jnp.bfloat16),
            jax.ShapeDtypeStruct((1, slots), jnp.int32),
        ),
        cost_estimate=pl.CostEstimate(
            flops=2 * slots * here * width,
            bytes_accessed=2 * width * (here + slots),
            transcendentals=0,
        ),
        name="pack_kv",
    )(lengths.reshape(1, -1), assignment.reshape(1, -1), prefill_kv.T)


def attend_kernel(queries_ref, fresh_ref, cache_ref, tags_ref, out_ref):
    mine = pl.program_id(0)
    steps, _, heads, width = queries_ref.shape
    latent = out_ref.shape[3]
    per_owner = fresh_ref.shape[1]
    rows = steps * heads
    queries = queries_ref[...].reshape(rows, width)
    cache = cache_ref[...]
    fresh = jnp.concatenate([fresh_ref[u].astype(jnp.float32) for u in range(steps)], axis=0)
    fresh = fresh.astype(jnp.bfloat16)
    contract = (((1,), (1,)), ((), ()))
    scores = (
        lax.dot_general(queries, cache, contract, preferred_element_type=jnp.float32)
        * score_scale
    )
    scores = jnp.where(tags_ref[...] == mine, scores, masked_score)
    fresh_scores = (
        lax.dot_general(queries, fresh, contract, preferred_element_type=jnp.float32)
        * score_scale
    )
    step = lax.broadcasted_iota(jnp.int32, (rows, steps * per_owner), 0) // heads
    other = lax.broadcasted_iota(jnp.int32, (rows, steps * per_owner), 1)
    seen = (other % per_owner == mine) & (other // per_owner <= step)
    fresh_scores = jnp.where(seen, fresh_scores, masked_score)
    top_score = jnp.maximum(
        jnp.max(scores, axis=1, keepdims=True), jnp.max(fresh_scores, axis=1, keepdims=True)
    )
    weights = jnp.exp(scores - top_score)
    fresh_weights = jnp.exp(fresh_scores - top_score)
    denominator = jnp.sum(weights, axis=1, keepdims=True) + jnp.sum(
        fresh_weights, axis=1, keepdims=True
    )
    summed = jnp.dot(
        weights.astype(jnp.bfloat16), cache[:, :latent], preferred_element_type=jnp.float32
    ) + jnp.dot(
        fresh_weights.astype(jnp.bfloat16),
        fresh[:, :latent],
        preferred_element_type=jnp.float32,
    )
    context = (summed / denominator).astype(jnp.bfloat16)
    out_ref[...] = context.reshape(steps, 1, heads, latent)


def attend(queries, new_kv, kv_cache, tags):
    steps, per_owner, heads, width = queries.shape
    slots = kv_cache.shape[0]
    latent = width - ROPE
    return pl.pallas_call(
        attend_kernel,
        grid=(per_owner,),
        in_specs=[
            pl.BlockSpec((steps, 1, heads, width), lambda q: (0, q, 0, 0)),
            pl.BlockSpec((steps, per_owner, width), lambda q: (0, 0, 0)),
            pl.BlockSpec((slots, width), lambda q: (0, 0)),
            pl.BlockSpec((1, slots), lambda q: (0, 0)),
        ],
        out_specs=pl.BlockSpec((steps, 1, heads, latent), lambda q: (0, q, 0, 0)),
        out_shape=jax.ShapeDtypeStruct((steps, per_owner, heads, latent), jnp.bfloat16),
        cost_estimate=pl.CostEstimate(
            flops=2 * steps * per_owner * heads * slots * (width + latent),
            bytes_accessed=2 * steps * per_owner * heads * (width + latent),
            transcendentals=steps * per_owner * heads * slots,
        ),
        name="attend",
    )(queries, new_kv, kv_cache, tags)


def expert_kernel(bits, arrived_ref, down_ref, keep_ref, send_ref, sorted_ref):
    me = lax.axis_index("seq")
    blocks = 1 << len(bits)
    half = keep_ref.shape[0]

    @pl.when(pl.program_id(0) == 0)
    def _():
        for place in range(blocks):
            apart = 0
            for i, bit in enumerate(bits):
                if place >> (len(bits) - 1 - i) & 1:
                    apart |= bit
            start = pl.multiple_of((me ^ apart) * BLOCK, BLOCK)
            sorted_ref[place * BLOCK : (place + 1) * BLOCK, :] = arrived_ref[
                pl.ds(start, BLOCK), :
            ]

    result = jnp.dot(sorted_ref[...], down_ref[0], preferred_element_type=jnp.float32)
    keep_ref[...] = result[:half]
    send_ref[...] = result[half:].astype(jnp.bfloat16)


def expert_part(arrived, expert_down, bits, part, parts, tile):
    slots, hidden_width = arrived.shape
    width = expert_down.shape[2] // parts
    half = slots // 2
    tiles = width // tile
    return pl.pallas_call(
        functools.partial(expert_kernel, bits),
        grid=(tiles,),
        in_specs=[
            pl.BlockSpec((slots, hidden_width), lambda i: (0, 0)),
            pl.BlockSpec((1, hidden_width, tile), lambda i: (0, 0, i + part * tiles)),
        ],
        out_specs=[
            pl.BlockSpec((half, tile), lambda i: (0, i)),
            pl.BlockSpec((half, tile), lambda i: (0, i)),
        ],
        out_shape=(
            jax.ShapeDtypeStruct((half, width), jnp.float32),
            jax.ShapeDtypeStruct((half, width), jnp.bfloat16),
        ),
        scratch_shapes=[pltpu.VMEM((slots, hidden_width), jnp.bfloat16)],
        cost_estimate=pl.CostEstimate(
            flops=2 * slots * hidden_width * width,
            bytes_accessed=2 * hidden_width * width + 6 * half * width,
            transcendentals=0,
        ),
        name="expert_part",
    )(arrived, expert_down)


def swap(values, bit, devices):
    return lax.ppermute(values, "seq", [(i, i ^ bit) for i in range(devices)])


def fold(kept, received):
    total = kept + received.astype(jnp.float32)
    half = total.shape[0] // 2
    return total[:half], total[half:].astype(jnp.bfloat16)


def per_device_dense(
    prefill_kv,
    lengths,
    assignment,
    queries,
    new_kv,
    expert_hidden,
    routes,
    route_weights,
    expert_down,
):
    devices = lax.axis_size("seq")
    steps, per_owner = queries.shape[:2]
    rows, _, top, hidden_width = expert_hidden.shape
    model_width = expert_down.shape[2]
    outbox = pack_hidden(routes, route_weights, expert_hidden, devices)
    arrived = lax.all_to_all(
        outbox.reshape(devices, BLOCK, hidden_width), "seq", split_axis=0, concat_axis=0, tiled=True
    ).reshape(devices * BLOCK, hidden_width)
    kv_outbox, tags = pack_kv(
        prefill_kv, lengths, assignment, devices, per_owner, 2 * HALF * per_owner
    )

    orders = ((1, 2, 4, 8), (1, 4, 2, 8))
    parts = len(orders)
    flows = []
    for part, bits in enumerate(orders):
        kept, sent = expert_part(arrived, expert_down, bits, part, parts, 256)
        flows.append((kept, sent, swap(sent, bits[0], devices)))
    flows = [fold(kept, received) for kept, _, received in flows]
    received = [swap(sent, bits[1], devices) for (_, sent), bits in zip(flows, orders)]

    kv_outbox, _ = lax.optimization_barrier((kv_outbox, [sent for _, sent in flows]))
    kv_cache = lax.all_to_all(
        kv_outbox.reshape(devices, -1, kv_outbox.shape[1]),
        "seq",
        split_axis=0,
        concat_axis=0,
        tiled=True,
    ).reshape(kv_outbox.shape)
    context = attend(queries, new_kv, kv_cache, tags)

    for level in (2, 3):
        flows = [fold(kept, got) for (kept, _), got in zip(flows, received)]
        received = [swap(sent, bits[level], devices) for (_, sent), bits in zip(flows, orders)]
    final = [kept + got.astype(jnp.float32) for (kept, _), got in zip(flows, received)]
    moe_out = jnp.concatenate(final, axis=1).astype(jnp.bfloat16)
    return context, moe_out.reshape(rows, steps, model_width)


def per_device(*arrays):
    expert_hidden, expert_down = arrays[5], arrays[8]
    devices = lax.axis_size("seq")
    rows, steps, top = expert_hidden.shape[:3]
    tokens = rows * steps
    experts = expert_down.shape[0] * devices
    bound = max(2, 2 * tokens * top // experts)
    if devices == 16 and experts == devices and tokens == BLOCK and bound == tokens:
        return per_device_dense(*arrays)
    return per_device_general(*arrays)


def solution(mesh):
    placed = (
        P(("groups", "seq"), None),
        P("groups"),
        P("groups"),
        P(None, ("groups", "seq"), None, None),
        P(None, ("groups", "seq"), None),
        P(("groups", "seq"), None, None, None),
        P(("groups", "seq"), None, None),
        P(("groups", "seq"), None, None),
        P("seq", None, None),
    )
    return jax.shard_map(
        per_device,
        mesh=mesh,
        in_specs=placed,
        out_specs=(P(None, ("groups", "seq"), None, None), P(("groups", "seq"), None, None)),
        check_vma=False,
    )
```

```python
import functools

import jax
import jax.numpy as jnp
from jax import lax
from jax.experimental import pallas as pl
from jax.experimental.pallas import tpu as pltpu
from jax.sharding import PartitionSpec as P

ROPE = 64
HALF = 2


score_scale = 192.0 ** (-0.5)
masked_score = -1e30


def slot_sources(slot_ids, slot_total):
    source_rows = jnp.arange(slot_ids.shape[0], dtype=jnp.int32)
    matched = slot_ids[None, :] == jnp.arange(slot_total, dtype=jnp.int32)[:, None]
    return jnp.max(jnp.where(matched, source_rows[None, :], -1), axis=1)


def fill_slots(values, sources, filler):
    taken = jnp.take(values, jnp.maximum(sources, 0), axis=0)
    valid = (sources >= 0).reshape((-1,) + (1,) * (values.ndim - 1))
    return jnp.where(valid, taken, jnp.asarray(filler, values.dtype))


def hand_over(prefill_kv, lengths, assignment, per_owner):
    device_count = lax.axis_size("seq")
    own_index = lax.axis_index("seq")
    ctx_here, kv_width = prefill_kv.shape
    position = jnp.arange(ctx_here, dtype=jnp.int32) * device_count + own_index
    request_ends = jnp.cumsum(lengths)
    request = jnp.sum((position[:, None] >= request_ends[None, :]).astype(jnp.int32), axis=1)
    total_rows = assignment.shape[0]
    row_numbers = jnp.arange(total_rows, dtype=jnp.int32)
    serving = jnp.sum(
        jnp.where(assignment[None, :] == row_numbers[:, None], row_numbers[None, :], 0), axis=1
    )
    decode_row = jnp.sum(
        jnp.where(request[:, None] == row_numbers[None, :], serving[None, :], 0), axis=1
    )
    owner_index = decode_row // per_owner
    local_request = decode_row % per_owner
    onehot = (owner_index[:, None] == jnp.arange(device_count, dtype=jnp.int32)[None, :]).astype(
        jnp.int32
    )
    slot_rank = jnp.sum((jnp.cumsum(onehot, axis=0) - onehot) * onehot, axis=1)
    slot_count = 2 * HALF * per_owner
    sources = slot_sources(owner_index * slot_count + slot_rank, device_count * slot_count)
    outbox = fill_slots(prefill_kv, sources, 0).reshape(device_count, slot_count, kv_width)
    labels = fill_slots(local_request, sources, -1).reshape(device_count, slot_count)
    kv_cache, cache_tags = (
        lax.all_to_all(outbox, "seq", split_axis=0, concat_axis=0, tiled=True),
        lax.all_to_all(labels, "seq", split_axis=0, concat_axis=0, tiled=True),
    )
    return (kv_cache.reshape(device_count * slot_count, kv_width), cache_tags.reshape(-1))


def fresh_part(queries, new_kv):
    step_count = queries.shape[0]
    fresh_scores = (
        jnp.einsum("sqhk,uqk->sqhu", queries, new_kv, preferred_element_type=jnp.float32)
        * score_scale
    )
    causal = jnp.arange(step_count)[:, None] >= jnp.arange(step_count)[None, :]
    return jnp.where(causal[:, None, None, :], fresh_scores, masked_score)


def attend_dense(queries, new_kv, kv_cache, cache_tags):
    step_count, per_owner, head_count, kv_width = queries.shape
    latent = kv_width - ROPE
    query_rows = queries.reshape(step_count * per_owner * head_count, kv_width)
    scores = (
        jnp.einsum("rk,ck->rc", query_rows, kv_cache, preferred_element_type=jnp.float32)
        * score_scale
    )
    row_request = jnp.broadcast_to(
        jnp.arange(per_owner, dtype=jnp.int32)[None, :, None], (step_count, per_owner, head_count)
    ).reshape(-1)
    allowed = cache_tags[None, :] == row_request[:, None]
    scores = jnp.where(allowed, scores, masked_score).reshape(step_count, per_owner, head_count, -1)
    fresh_scores = fresh_part(queries, new_kv)
    top_score = jnp.maximum(jnp.max(scores, axis=-1), jnp.max(fresh_scores, axis=-1))
    weights = jnp.exp(scores - top_score[..., None])
    fresh_weights = jnp.exp(fresh_scores - top_score[..., None])
    denominator = jnp.sum(weights, axis=-1) + jnp.sum(fresh_weights, axis=-1)
    summed = jnp.einsum(
        "sqhc,cl->sqhl",
        weights.astype(jnp.bfloat16),
        kv_cache[:, :latent],
        preferred_element_type=jnp.float32,
    )
    summed = summed + jnp.einsum(
        "sqhu,uql->sqhl",
        fresh_weights.astype(jnp.bfloat16),
        new_kv[..., :latent],
        preferred_element_type=jnp.float32,
    )
    return (summed / denominator[..., None]).astype(jnp.bfloat16)


def expert_layer(expert_hidden, routes, route_weights, expert_down):
    device_count = lax.axis_size("seq")
    rows_here, step_count, top_count, hidden_width = expert_hidden.shape
    per_dev = expert_down.shape[0]
    experts = per_dev * device_count
    capacity = max(2, 2 * step_count * rows_here * top_count // experts)
    flat_routes = routes.reshape(-1)
    route_count = flat_routes.shape[0]
    onehot = (flat_routes[:, None] == jnp.arange(experts, dtype=jnp.int32)[None, :]).astype(
        jnp.int32
    )
    slot_index = jnp.sum((jnp.cumsum(onehot, axis=0) - onehot) * onehot, axis=1)
    flat_hidden = expert_hidden.reshape(route_count, hidden_width)
    slot_ids = flat_routes * capacity + slot_index
    sources = slot_sources(slot_ids, experts * capacity)
    outbox = fill_slots(flat_hidden, sources, 0).reshape(
        device_count, per_dev, capacity, hidden_width
    )
    expert_out = jnp.einsum(
        "dekh,ehm->dekm",
        lax.all_to_all(outbox, "seq", split_axis=0, concat_axis=0, tiled=True),
        expert_down,
        preferred_element_type=jnp.float32,
    ).astype(jnp.bfloat16)
    returned = lax.all_to_all(expert_out, "seq", split_axis=0, concat_axis=0, tiled=True)
    returned = returned.reshape(experts * capacity, returned.shape[-1])
    picked = jnp.take(returned, slot_ids, axis=0).astype(jnp.float32)
    weighted = picked * route_weights.reshape(route_count, 1)
    moe_out = jnp.sum(weighted.reshape(rows_here, step_count, top_count, -1), axis=2)
    return moe_out.astype(jnp.bfloat16)


def per_device_general(
    prefill_kv,
    lengths,
    assignment,
    queries,
    new_kv,
    expert_hidden,
    routes,
    route_weights,
    expert_down,
):
    kv_cache, cache_tags = hand_over(prefill_kv, lengths, assignment, queries.shape[1])
    context = attend_dense(queries, new_kv, kv_cache, cache_tags)
    moe_out = expert_layer(expert_hidden, routes, route_weights, expert_down)
    return (context, moe_out)


BLOCK = 16
SCOPED_BYTES = 16 * 2**20


def as_column(row):
    size = row.shape[1]
    eye = lax.broadcasted_iota(jnp.int32, (size, size), 0) == lax.broadcasted_iota(
        jnp.int32, (size, size), 1
    )
    return jnp.sum(jnp.where(eye, row, 0), axis=1, keepdims=True)


def flat_row(table, tokens, top):
    lanes = tokens * top
    place = lax.broadcasted_iota(jnp.int32, (top, lanes), 1) % top
    spread = (place == lax.broadcasted_iota(jnp.int32, (top, lanes), 0)).astype(jnp.float32)
    wide = jnp.dot(
        table, spread, precision=lax.Precision.HIGHEST, preferred_element_type=jnp.float32
    )
    owner = lax.broadcasted_iota(jnp.int32, (tokens, lanes), 1) // top
    mine = owner == lax.broadcasted_iota(jnp.int32, (tokens, lanes), 0)
    return jnp.sum(jnp.where(mine, wide, 0.0), axis=0, keepdims=True)


def outbox_kernel(routes_ref, weights_ref, hidden_ref, out_ref):
    rows, steps, top = routes_ref.shape
    tokens = rows * steps
    lanes = tokens * top
    slots = out_ref.shape[0]
    routes = jnp.concatenate([routes_ref[i] for i in range(rows)], axis=0).astype(jnp.float32)
    weights = jnp.concatenate([weights_ref[i] for i in range(rows)], axis=0)
    route_row = flat_row(routes, tokens, top).astype(jnp.int32)
    weight_row = flat_row(weights, tokens, top)
    slot = lax.broadcasted_iota(jnp.int32, (slots, lanes), 0)
    lane = lax.broadcasted_iota(jnp.int32, (slots, lanes), 1)
    pick = (lane // top == slot % tokens) & (route_row == slot // tokens)
    scale = jnp.sum(jnp.where(pick, weight_row, 0.0), axis=1, keepdims=True)
    chosen = jnp.where(pick, 1.0, 0.0).astype(jnp.bfloat16)
    moved = jnp.dot(chosen, hidden_ref[...], preferred_element_type=jnp.float32)
    out_ref[...] = (moved * scale).astype(jnp.bfloat16)


def pack_hidden(routes, route_weights, expert_hidden, experts):
    rows, steps, top, width = expert_hidden.shape
    tokens = rows * steps
    return pl.pallas_call(
        outbox_kernel,
        out_shape=jax.ShapeDtypeStruct((experts * tokens, width), jnp.bfloat16),
        cost_estimate=pl.CostEstimate(
            flops=2 * experts * tokens * tokens * top * width,
            bytes_accessed=2 * width * tokens * (top + experts),
            transcendentals=0,
        ),
        name="pack_hidden",
    )(routes, route_weights, expert_hidden.reshape(tokens * top, width))


def ceil_rows(position, source, devices):
    return (position + (devices - 1) - source) // devices


def request_spans(lengths_ref, assignment_ref):
    requests = lengths_ref.shape[1]
    length_column = as_column(lengths_ref[...])
    assignment = assignment_ref[...]
    number = lax.broadcasted_iota(jnp.int32, (requests, requests), 0)
    before = jnp.sum(jnp.where(number < assignment, length_column, 0), axis=0, keepdims=True)
    own = jnp.sum(jnp.where(number == assignment, length_column, 0), axis=0, keepdims=True)
    return before, before + own


def apart_of(place, bits):
    apart = place * 0
    for i, bit in enumerate(bits):
        digit = (place // (1 << (len(bits) - 1 - i))) % 2
        apart = apart + digit * bit
    return apart


def kv_kernel(bits, per_owner, lengths_ref, assignment_ref, kv_ref, out_ref):
    me = lax.axis_index("seq")
    devices = 1 << len(bits)
    requests = lengths_ref.shape[1]
    here = kv_ref.shape[1]
    slots = out_ref.shape[0]
    room = slots // devices
    before, after = request_spans(lengths_ref, assignment_ref)
    low = ceil_rows(before, me, devices)
    count = ceil_rows(after, me, devices) - low
    number = lax.broadcasted_iota(jnp.int32, (requests, requests), 0)
    line = lax.broadcasted_iota(jnp.int32, (requests, requests), 1)
    same = (number // per_owner == line // per_owner) & (number < line)
    offset = jnp.sum(jnp.where(same, as_column(count), 0), axis=0, keepdims=True)
    slot = lax.broadcasted_iota(jnp.int32, (slots, requests), 0)
    decode = lax.broadcasted_iota(jnp.int32, (slots, requests), 1)
    owner = me ^ apart_of(slot // room, bits)
    rank = slot % room - offset
    held = (owner == decode // per_owner) & (rank >= 0) & (rank < count)
    source = jnp.sum(jnp.where(held, low + rank + 1, 0), axis=1, keepdims=True) - 1
    pick = source == lax.broadcasted_iota(jnp.int32, (slots, here), 1)
    out_ref[...] = lax.dot_general(
        jnp.where(pick, 1.0, 0.0).astype(jnp.bfloat16),
        kv_ref[...],
        (((1,), (1,)), ((), ())),
        preferred_element_type=jnp.float32,
    ).astype(jnp.bfloat16)


def pack_kv(prefill_kv, lengths, assignment, bits, per_owner, room):
    here, width = prefill_kv.shape
    slots = room << len(bits)
    return pl.pallas_call(
        functools.partial(kv_kernel, bits, per_owner),
        out_shape=jax.ShapeDtypeStruct((slots, width), jnp.bfloat16),
        compiler_params=pltpu.CompilerParams(vmem_limit_bytes=SCOPED_BYTES),
        cost_estimate=pl.CostEstimate(
            flops=2 * slots * here * width,
            bytes_accessed=20 * 2**20,
            transcendentals=0,
        ),
        name="pack_kv",
    )(lengths.reshape(1, -1), assignment.reshape(1, -1), prefill_kv.T)


def tags_kernel(devices, per_owner, lengths_ref, assignment_ref, tags_ref):
    me = lax.axis_index("seq")
    requests = lengths_ref.shape[1]
    slots = tags_ref.shape[1]
    room = slots // devices
    before, after = request_spans(lengths_ref, assignment_ref)
    place = lax.broadcasted_iota(jnp.int32, (1, slots), 1)
    sender, rank = me ^ (place // room), place % room
    tags = jnp.full((1, slots), -1, jnp.int32)
    decode = lax.broadcasted_iota(jnp.int32, (1, requests), 1)
    taken = jnp.zeros((1, slots), jnp.int32)
    for q in range(per_owner):
        mine = decode == me * per_owner + q
        first = jnp.sum(jnp.where(mine, before, 0), axis=1, keepdims=True)
        last = jnp.sum(jnp.where(mine, after, 0), axis=1, keepdims=True)
        arriving = ceil_rows(last, sender, devices) - ceil_rows(first, sender, devices)
        tags = jnp.where((rank >= taken) & (rank < taken + arriving), q, tags)
        taken = taken + arriving
    tags_ref[...] = tags


def slot_tags(lengths, assignment, devices, per_owner, slots):
    return pl.pallas_call(
        functools.partial(tags_kernel, devices, per_owner),
        out_shape=jax.ShapeDtypeStruct((1, slots), jnp.int32),
        compiler_params=pltpu.CompilerParams(vmem_limit_bytes=SCOPED_BYTES),
        cost_estimate=pl.CostEstimate(flops=0, bytes_accessed=8192, transcendentals=0),
        name="slot_tags",
    )(lengths.reshape(1, -1), assignment.reshape(1, -1))


def attend_kernel(queries_ref, fresh_ref, cache_ref, tags_ref, out_ref):
    mine = pl.program_id(0)
    steps, _, heads, width = queries_ref.shape
    latent = out_ref.shape[3]
    per_owner = fresh_ref.shape[1]
    rows = steps * heads
    queries = queries_ref[...].reshape(rows, width)
    cache = cache_ref[...]
    fresh = jnp.concatenate([fresh_ref[u].astype(jnp.float32) for u in range(steps)], axis=0)
    fresh = fresh.astype(jnp.bfloat16)
    contract = (((1,), (1,)), ((), ()))
    scores = (
        lax.dot_general(queries, cache, contract, preferred_element_type=jnp.float32)
        * score_scale
    )
    scores = jnp.where(tags_ref[...] == mine, scores, masked_score)
    fresh_scores = (
        lax.dot_general(queries, fresh, contract, preferred_element_type=jnp.float32)
        * score_scale
    )
    step = lax.broadcasted_iota(jnp.int32, (rows, steps * per_owner), 0) // heads
    other = lax.broadcasted_iota(jnp.int32, (rows, steps * per_owner), 1)
    seen = (other % per_owner == mine) & (other // per_owner <= step)
    fresh_scores = jnp.where(seen, fresh_scores, masked_score)
    top_score = jnp.maximum(
        jnp.max(scores, axis=1, keepdims=True), jnp.max(fresh_scores, axis=1, keepdims=True)
    )
    weights = jnp.exp(scores - top_score)
    fresh_weights = jnp.exp(fresh_scores - top_score)
    denominator = jnp.sum(weights, axis=1, keepdims=True) + jnp.sum(
        fresh_weights, axis=1, keepdims=True
    )
    summed = jnp.dot(
        weights.astype(jnp.bfloat16), cache[:, :latent], preferred_element_type=jnp.float32
    ) + jnp.dot(
        fresh_weights.astype(jnp.bfloat16),
        fresh[:, :latent],
        preferred_element_type=jnp.float32,
    )
    context = (summed / denominator).astype(jnp.bfloat16)
    out_ref[...] = context.reshape(steps, 1, heads, latent)


def attend(queries, new_kv, kv_cache, tags):
    steps, per_owner, heads, width = queries.shape
    slots = kv_cache.shape[0]
    latent = width - ROPE
    return pl.pallas_call(
        attend_kernel,
        grid=(per_owner,),
        in_specs=[
            pl.BlockSpec((steps, 1, heads, width), lambda q: (0, q, 0, 0)),
            pl.BlockSpec((steps, per_owner, width), lambda q: (0, 0, 0)),
            pl.BlockSpec((slots, width), lambda q: (0, 0)),
            pl.BlockSpec((1, slots), lambda q: (0, 0)),
        ],
        out_specs=pl.BlockSpec((steps, 1, heads, latent), lambda q: (0, q, 0, 0)),
        out_shape=jax.ShapeDtypeStruct((steps, per_owner, heads, latent), jnp.bfloat16),
        compiler_params=pltpu.CompilerParams(vmem_limit_bytes=SCOPED_BYTES),
        cost_estimate=pl.CostEstimate(
            flops=2 * steps * per_owner * heads * slots * (width + latent),
            bytes_accessed=2 * steps * per_owner * heads * (width + latent),
            transcendentals=steps * per_owner * heads * slots,
        ),
        name="attend",
    )(queries, new_kv, kv_cache, tags)


def sort_blocks(bits, arrived_ref, sorted_ref):
    me = lax.axis_index("seq")
    for place in range(1 << len(bits)):
        start = pl.multiple_of((me ^ apart_of(place, bits)) * BLOCK, BLOCK)
        sorted_ref[place * BLOCK : (place + 1) * BLOCK, :] = arrived_ref[pl.ds(start, BLOCK), :]


def first_half_kernel(
    bits, pieces, arrived_ref, down_ref, keep_ref, send_ref, rest_ref, sorted_ref, own_ref, sems
):
    half, width = keep_ref.shape
    piece = width // pieces
    copies = []
    for i in range(pieces):
        columns = slice(i * piece, (i + 1) * piece)
        copies.append(
            pltpu.make_async_copy(down_ref.at[0, :, columns], own_ref.at[:, columns], sems.at[i])
        )
    copies.append(pltpu.make_async_copy(down_ref.at[0, :, width:], rest_ref, sems.at[pieces]))
    for copy in copies:
        copy.start()
    sort_blocks(bits, arrived_ref, sorted_ref)
    for i in range(pieces):
        columns = slice(i * piece, (i + 1) * piece)
        copies[i].wait()
        result = jnp.dot(
            sorted_ref[...], own_ref[:, columns], preferred_element_type=jnp.float32
        )
        keep_ref[:, columns] = result[:half]
        send_ref[:, columns] = result[half:].astype(jnp.bfloat16)
    copies[pieces].wait()


def second_half_kernel(bits, arrived_ref, rest_ref, keep_ref, send_ref, sorted_ref):
    half = keep_ref.shape[0]
    sort_blocks(bits, arrived_ref, sorted_ref)
    result = jnp.dot(sorted_ref[...], rest_ref[...], preferred_element_type=jnp.float32)
    keep_ref[...] = result[:half]
    send_ref[...] = result[half:].astype(jnp.bfloat16)


def expert_halves(arrived, expert_down, orders):
    slots, hidden_width = arrived.shape
    width = expert_down.shape[2] // 2
    half = slots // 2
    pieces = 2
    vmem = pl.BlockSpec(memory_space=pltpu.VMEM)
    shapes = (
        jax.ShapeDtypeStruct((half, width), jnp.float32),
        jax.ShapeDtypeStruct((half, width), jnp.bfloat16),
    )
    params = pltpu.CompilerParams(vmem_limit_bytes=SCOPED_BYTES)
    cost = pl.CostEstimate(
        flops=2 * slots * hidden_width * width,
        bytes_accessed=2 * hidden_width * width,
        transcendentals=0,
    )
    down = pltpu.with_memory_space_constraint(expert_down, pltpu.HBM)
    kept_first, sent_first, rest = pl.pallas_call(
        functools.partial(first_half_kernel, orders[0], pieces),
        in_specs=[vmem, pl.BlockSpec(memory_space=pltpu.HBM)],
        out_specs=[vmem] * 3,
        out_shape=shapes + (pltpu.VMEM((hidden_width, width), jnp.bfloat16),),
        scratch_shapes=[
            pltpu.VMEM((slots, hidden_width), jnp.bfloat16),
            pltpu.VMEM((hidden_width, width), jnp.bfloat16),
            pltpu.SemaphoreType.DMA((pieces + 1,)),
        ],
        compiler_params=params,
        cost_estimate=cost,
        name="expert_first",
    )(arrived, down)
    kept_second, sent_second = pl.pallas_call(
        functools.partial(second_half_kernel, orders[1]),
        in_specs=[vmem] * 2,
        out_specs=[vmem] * 2,
        out_shape=shapes,
        scratch_shapes=[pltpu.VMEM((slots, hidden_width), jnp.bfloat16)],
        compiler_params=params,
        cost_estimate=cost,
        name="expert_second",
    )(arrived, rest)
    return (kept_first, sent_first), (kept_second, sent_second)


after = lax.optimization_barrier


def swap(values, bit, devices):
    return lax.ppermute(values, "seq", [(i, i ^ bit) for i in range(devices)])


def fold(kept, received):
    total = kept + received.astype(jnp.float32)
    half = total.shape[0] // 2
    return total[:half], total[half:].astype(jnp.bfloat16)


def per_device_dense(
    prefill_kv,
    lengths,
    assignment,
    queries,
    new_kv,
    expert_hidden,
    routes,
    route_weights,
    expert_down,
):
    devices = lax.axis_size("seq")
    steps, per_owner = queries.shape[:2]
    rows, _, top, hidden_width = expert_hidden.shape
    model_width = expert_down.shape[2]
    outbox = pack_hidden(routes, route_weights, expert_hidden, devices)
    arrived = lax.all_to_all(
        outbox.reshape(devices, BLOCK, hidden_width), "seq", split_axis=0, concat_axis=0, tiled=True
    ).reshape(devices * BLOCK, hidden_width)

    room = 2 * HALF * per_owner
    kv_bits = (1, 2, 4, 8)
    held = pack_kv(prefill_kv, lengths, assignment, kv_bits, per_owner, room)
    tags = slot_tags(lengths, assignment, devices, per_owner, devices * room)
    held = held.reshape(1, held.shape[0], held.shape[1])

    def split(held):
        half = held.shape[1] // 2
        return held[:, :half], held[:, half:]

    for bit in kv_bits[:2]:
        kept, sent = split(held)
        held = jnp.concatenate([kept, swap(sent, bit, devices)], axis=0)
    kv_kept, kv_sent = split(held)
    kv_got = swap(kv_sent, kv_bits[2], devices)
    arrived, _, _ = after((arrived, kv_sent, tags))

    orders = ((1, 2, 4, 8), (1, 4, 2, 8))
    flows = []
    for (kept, sent), bits in zip(expert_halves(arrived, expert_down, orders), orders):
        flows.append((kept, swap(sent, bits[0], devices)))
    flows = [fold(kept, received) for kept, received in flows]
    received = [swap(sent, bits[1], devices) for (_, sent), bits in zip(flows, orders)]

    kv_got, _ = after((kv_got, [sent for _, sent in flows]))
    kv_kept, kv_sent = split(jnp.concatenate([kv_kept, kv_got], axis=0))
    held = jnp.concatenate([kv_kept, swap(kv_sent, kv_bits[3], devices)], axis=0)
    context = attend(queries, new_kv, held.reshape(devices * room, -1), tags)

    flows = [fold(kept, got) for (kept, _), got in zip(flows, received)]
    received = [swap(sent, bits[2], devices) for (_, sent), bits in zip(flows, orders)]
    flows = [fold(kept, got) for (kept, _), got in zip(flows, received)]
    kept = jnp.concatenate([kept for kept, _ in flows], axis=1)
    sent = jnp.concatenate([sent for _, sent in flows], axis=1)
    received = swap(sent, orders[0][-1], devices)
    received, context = lax.optimization_barrier((received, context))
    moe_out = (kept + received.astype(jnp.float32)).astype(jnp.bfloat16)
    return context, moe_out.reshape(rows, steps, model_width)


def per_device(*arrays):
    expert_hidden, expert_down = arrays[5], arrays[8]
    devices = lax.axis_size("seq")
    rows, steps, top = expert_hidden.shape[:3]
    tokens = rows * steps
    experts = expert_down.shape[0] * devices
    bound = max(2, 2 * tokens * top // experts)
    if devices == 16 and experts == devices and tokens == BLOCK and bound == tokens:
        return per_device_dense(*arrays)
    return per_device_general(*arrays)


def solution(mesh):
    placed = (
        P(("groups", "seq"), None),
        P("groups"),
        P("groups"),
        P(None, ("groups", "seq"), None, None),
        P(None, ("groups", "seq"), None),
        P(("groups", "seq"), None, None, None),
        P(("groups", "seq"), None, None),
        P(("groups", "seq"), None, None),
        P("seq", None, None),
    )
    return jax.shard_map(
        per_device,
        mesh=mesh,
        in_specs=placed,
        out_specs=(P(None, ("groups", "seq"), None, None), P(("groups", "seq"), None, None)),
        check_vma=False,
    )
```

```python
import functools

import jax
import jax.numpy as jnp
from jax import lax
from jax.experimental import pallas as pl
from jax.experimental.pallas import tpu as pltpu
from jax.sharding import PartitionSpec as P

ROPE = 64
HALF = 2


score_scale = 192.0 ** (-0.5)
masked_score = -1e30


def slot_sources(slot_ids, slot_total):
    source_rows = jnp.arange(slot_ids.shape[0], dtype=jnp.int32)
    matched = slot_ids[None, :] == jnp.arange(slot_total, dtype=jnp.int32)[:, None]
    return jnp.max(jnp.where(matched, source_rows[None, :], -1), axis=1)


def fill_slots(values, sources, filler):
    taken = jnp.take(values, jnp.maximum(sources, 0), axis=0)
    valid = (sources >= 0).reshape((-1,) + (1,) * (values.ndim - 1))
    return jnp.where(valid, taken, jnp.asarray(filler, values.dtype))


def hand_over(prefill_kv, lengths, assignment, per_owner):
    device_count = lax.axis_size("seq")
    own_index = lax.axis_index("seq")
    ctx_here, kv_width = prefill_kv.shape
    position = jnp.arange(ctx_here, dtype=jnp.int32) * device_count + own_index
    request_ends = jnp.cumsum(lengths)
    request = jnp.sum((position[:, None] >= request_ends[None, :]).astype(jnp.int32), axis=1)
    total_rows = assignment.shape[0]
    row_numbers = jnp.arange(total_rows, dtype=jnp.int32)
    serving = jnp.sum(
        jnp.where(assignment[None, :] == row_numbers[:, None], row_numbers[None, :], 0), axis=1
    )
    decode_row = jnp.sum(
        jnp.where(request[:, None] == row_numbers[None, :], serving[None, :], 0), axis=1
    )
    owner_index = decode_row // per_owner
    local_request = decode_row % per_owner
    onehot = (owner_index[:, None] == jnp.arange(device_count, dtype=jnp.int32)[None, :]).astype(
        jnp.int32
    )
    slot_rank = jnp.sum((jnp.cumsum(onehot, axis=0) - onehot) * onehot, axis=1)
    slot_count = 2 * HALF * per_owner
    sources = slot_sources(owner_index * slot_count + slot_rank, device_count * slot_count)
    outbox = fill_slots(prefill_kv, sources, 0).reshape(device_count, slot_count, kv_width)
    labels = fill_slots(local_request, sources, -1).reshape(device_count, slot_count)
    kv_cache, cache_tags = (
        lax.all_to_all(outbox, "seq", split_axis=0, concat_axis=0, tiled=True),
        lax.all_to_all(labels, "seq", split_axis=0, concat_axis=0, tiled=True),
    )
    return (kv_cache.reshape(device_count * slot_count, kv_width), cache_tags.reshape(-1))


def fresh_part(queries, new_kv):
    step_count = queries.shape[0]
    fresh_scores = (
        jnp.einsum("sqhk,uqk->sqhu", queries, new_kv, preferred_element_type=jnp.float32)
        * score_scale
    )
    causal = jnp.arange(step_count)[:, None] >= jnp.arange(step_count)[None, :]
    return jnp.where(causal[:, None, None, :], fresh_scores, masked_score)


def attend_dense(queries, new_kv, kv_cache, cache_tags):
    step_count, per_owner, head_count, kv_width = queries.shape
    latent = kv_width - ROPE
    query_rows = queries.reshape(step_count * per_owner * head_count, kv_width)
    scores = (
        jnp.einsum("rk,ck->rc", query_rows, kv_cache, preferred_element_type=jnp.float32)
        * score_scale
    )
    row_request = jnp.broadcast_to(
        jnp.arange(per_owner, dtype=jnp.int32)[None, :, None], (step_count, per_owner, head_count)
    ).reshape(-1)
    allowed = cache_tags[None, :] == row_request[:, None]
    scores = jnp.where(allowed, scores, masked_score).reshape(step_count, per_owner, head_count, -1)
    fresh_scores = fresh_part(queries, new_kv)
    top_score = jnp.maximum(jnp.max(scores, axis=-1), jnp.max(fresh_scores, axis=-1))
    weights = jnp.exp(scores - top_score[..., None])
    fresh_weights = jnp.exp(fresh_scores - top_score[..., None])
    denominator = jnp.sum(weights, axis=-1) + jnp.sum(fresh_weights, axis=-1)
    summed = jnp.einsum(
        "sqhc,cl->sqhl",
        weights.astype(jnp.bfloat16),
        kv_cache[:, :latent],
        preferred_element_type=jnp.float32,
    )
    summed = summed + jnp.einsum(
        "sqhu,uql->sqhl",
        fresh_weights.astype(jnp.bfloat16),
        new_kv[..., :latent],
        preferred_element_type=jnp.float32,
    )
    return (summed / denominator[..., None]).astype(jnp.bfloat16)


def expert_layer(expert_hidden, routes, route_weights, expert_down):
    device_count = lax.axis_size("seq")
    rows_here, step_count, top_count, hidden_width = expert_hidden.shape
    per_dev = expert_down.shape[0]
    experts = per_dev * device_count
    capacity = max(2, 2 * step_count * rows_here * top_count // experts)
    flat_routes = routes.reshape(-1)
    route_count = flat_routes.shape[0]
    onehot = (flat_routes[:, None] == jnp.arange(experts, dtype=jnp.int32)[None, :]).astype(
        jnp.int32
    )
    slot_index = jnp.sum((jnp.cumsum(onehot, axis=0) - onehot) * onehot, axis=1)
    flat_hidden = expert_hidden.reshape(route_count, hidden_width)
    slot_ids = flat_routes * capacity + slot_index
    sources = slot_sources(slot_ids, experts * capacity)
    outbox = fill_slots(flat_hidden, sources, 0).reshape(
        device_count, per_dev, capacity, hidden_width
    )
    expert_out = jnp.einsum(
        "dekh,ehm->dekm",
        lax.all_to_all(outbox, "seq", split_axis=0, concat_axis=0, tiled=True),
        expert_down,
        preferred_element_type=jnp.float32,
    ).astype(jnp.bfloat16)
    returned = lax.all_to_all(expert_out, "seq", split_axis=0, concat_axis=0, tiled=True)
    returned = returned.reshape(experts * capacity, returned.shape[-1])
    picked = jnp.take(returned, slot_ids, axis=0).astype(jnp.float32)
    weighted = picked * route_weights.reshape(route_count, 1)
    moe_out = jnp.sum(weighted.reshape(rows_here, step_count, top_count, -1), axis=2)
    return moe_out.astype(jnp.bfloat16)


def per_device_general(
    prefill_kv,
    lengths,
    assignment,
    queries,
    new_kv,
    expert_hidden,
    routes,
    route_weights,
    expert_down,
):
    kv_cache, cache_tags = hand_over(prefill_kv, lengths, assignment, queries.shape[1])
    context = attend_dense(queries, new_kv, kv_cache, cache_tags)
    moe_out = expert_layer(expert_hidden, routes, route_weights, expert_down)
    return (context, moe_out)


BLOCK = 16
SCOPED_BYTES = 16 * 2**20


def as_column(row):
    size = row.shape[1]
    eye = lax.broadcasted_iota(jnp.int32, (size, size), 0) == lax.broadcasted_iota(
        jnp.int32, (size, size), 1
    )
    return jnp.sum(jnp.where(eye, row, 0), axis=1, keepdims=True)


def flat_row(table, tokens, top):
    lanes = tokens * top
    place = lax.broadcasted_iota(jnp.int32, (top, lanes), 1) % top
    spread = (place == lax.broadcasted_iota(jnp.int32, (top, lanes), 0)).astype(jnp.float32)
    wide = jnp.dot(
        table, spread, precision=lax.Precision.HIGHEST, preferred_element_type=jnp.float32
    )
    owner = lax.broadcasted_iota(jnp.int32, (tokens, lanes), 1) // top
    mine = owner == lax.broadcasted_iota(jnp.int32, (tokens, lanes), 0)
    return jnp.sum(jnp.where(mine, wide, 0.0), axis=0, keepdims=True)


def ceil_rows(position, source, devices):
    return (position + (devices - 1) - source) // devices


def request_spans(lengths_ref, assignment_ref):
    requests = lengths_ref.shape[1]
    length_column = as_column(lengths_ref[...])
    assignment = assignment_ref[...]
    number = lax.broadcasted_iota(jnp.int32, (requests, requests), 0)
    before = jnp.sum(jnp.where(number < assignment, length_column, 0), axis=0, keepdims=True)
    own = jnp.sum(jnp.where(number == assignment, length_column, 0), axis=0, keepdims=True)
    return before, before + own


def apart_of(place, bits):
    apart = place * 0
    for i, bit in enumerate(bits):
        digit = (place // (1 << (len(bits) - 1 - i))) % 2
        apart = apart + digit * bit
    return apart


def outbox_kernel(
    chips,
    per_owner,
    routes_ref,
    weights_ref,
    hidden_ref,
    lengths_ref,
    assignment_ref,
    kv_ref,
    near_ref,
    far_ref,
):
    me = lax.axis_index("seq")
    devices = 2 * chips
    half = near_ref.shape[0]
    slots = 2 * half
    room = slots // devices
    rows, steps, top = routes_ref.shape
    tokens = rows * steps
    lanes = tokens * top
    hidden_width = hidden_ref.shape[1]
    routes = jnp.concatenate([routes_ref[i] for i in range(rows)], axis=0).astype(jnp.float32)
    weights = jnp.concatenate([weights_ref[i] for i in range(rows)], axis=0)
    route_row = flat_row(routes, tokens, top).astype(jnp.int32)
    weight_row = flat_row(weights, tokens, top)
    slot = lax.broadcasted_iota(jnp.int32, (slots, lanes), 0)
    lane = lax.broadcasted_iota(jnp.int32, (slots, lanes), 1)
    block = slot // room
    target = me ^ (2 * (block % chips) + block // chips)
    pick = (lane // top == slot % room) & (route_row == target)
    scale = jnp.sum(jnp.where(pick, weight_row, 0.0), axis=1, keepdims=True)
    chosen = jnp.where(pick, 1.0, 0.0).astype(jnp.bfloat16)
    moved = jnp.dot(chosen, hidden_ref[...], preferred_element_type=jnp.float32)
    moved = (moved * scale).astype(jnp.bfloat16)
    near_ref[:, :hidden_width] = moved[:half]
    far_ref[:, :hidden_width] = moved[half:]

    requests = lengths_ref.shape[1]
    kv_width, here = kv_ref.shape
    before, after_last = request_spans(lengths_ref, assignment_ref)
    low = ceil_rows(before, me, devices)
    count = ceil_rows(after_last, me, devices) - low
    number = lax.broadcasted_iota(jnp.int32, (requests, requests), 0)
    line = lax.broadcasted_iota(jnp.int32, (requests, requests), 1)
    same = (number // per_owner == line // per_owner) & (number < line)
    offset = jnp.sum(jnp.where(same, as_column(count), 0), axis=0, keepdims=True)
    slot = lax.broadcasted_iota(jnp.int32, (slots, requests), 0)
    decode = lax.broadcasted_iota(jnp.int32, (slots, requests), 1)
    block = slot // room
    target = me ^ (2 * (block % chips) + block // chips)
    rank = slot % room - offset
    held = (target == decode // per_owner) & (rank >= 0) & (rank < count)
    source = jnp.sum(jnp.where(held, low + rank + 1, 0), axis=1, keepdims=True) - 1
    pick = source == lax.broadcasted_iota(jnp.int32, (slots, here), 1)
    moved = lax.dot_general(
        jnp.where(pick, 1.0, 0.0).astype(jnp.bfloat16),
        kv_ref[...],
        (((1,), (1,)), ((), ())),
        preferred_element_type=jnp.float32,
    ).astype(jnp.bfloat16)
    last = hidden_width + kv_width
    empty = jnp.zeros((half, near_ref.shape[1] - last), jnp.bfloat16)
    near_ref[:, hidden_width:last] = moved[:half]
    far_ref[:, hidden_width:last] = moved[half:]
    near_ref[:, last:] = empty
    far_ref[:, last:] = empty


def pack_outboxes(
    routes, route_weights, expert_hidden, lengths, assignment, prefill_kv, devices
):
    rows, steps, top, hidden_width = expert_hidden.shape
    here, kv_width = prefill_kv.shape
    tokens = rows * steps
    slots = tokens * devices
    width = pl.cdiv(hidden_width + kv_width, 128) * 128
    operands = (
        routes,
        route_weights,
        expert_hidden.reshape(tokens * top, hidden_width),
        lengths.reshape(1, -1),
        assignment.reshape(1, -1),
        prefill_kv.T,
    )
    return pl.pallas_call(
        functools.partial(outbox_kernel, devices // 2, rows),
        out_shape=(jax.ShapeDtypeStruct((slots // 2, width), jnp.bfloat16),) * 2,
        compiler_params=pltpu.CompilerParams(vmem_limit_bytes=SCOPED_BYTES),
        cost_estimate=pl.CostEstimate(
            flops=2 * slots * (tokens * top * hidden_width + here * kv_width),
            bytes_accessed=4 * slots * width,
            transcendentals=0,
        ),
        name="pack_outboxes",
    )(*(pltpu.with_memory_space_constraint(x, pltpu.HBM) for x in operands))


def load_kernel(
    devices, per_owner, lengths_ref, assignment_ref, down_ref, tags_ref, held_ref, sem
):
    copy = pltpu.make_async_copy(down_ref, held_ref, sem)
    copy.start()
    me = lax.axis_index("seq")
    requests = lengths_ref.shape[1]
    slots = tags_ref.shape[1]
    room = slots // devices
    before, after = request_spans(lengths_ref, assignment_ref)
    place = lax.broadcasted_iota(jnp.int32, (1, slots), 1)
    sender, rank = me ^ (place // room), place % room
    tags = jnp.full((1, slots), -1, jnp.int32)
    decode = lax.broadcasted_iota(jnp.int32, (1, requests), 1)
    taken = jnp.zeros((1, slots), jnp.int32)
    for q in range(per_owner):
        mine = decode == me * per_owner + q
        first = jnp.sum(jnp.where(mine, before, 0), axis=1, keepdims=True)
        last = jnp.sum(jnp.where(mine, after, 0), axis=1, keepdims=True)
        arriving = ceil_rows(last, sender, devices) - ceil_rows(first, sender, devices)
        tags = jnp.where((rank >= taken) & (rank < taken + arriving), q, tags)
        taken = taken + arriving
    tags_ref[...] = tags
    copy.wait()


def load_down(lengths, assignment, expert_down, devices, per_owner, slots):
    vmem = pl.BlockSpec(memory_space=pltpu.VMEM)
    return pl.pallas_call(
        functools.partial(load_kernel, devices, per_owner),
        in_specs=[vmem, vmem, pl.BlockSpec(memory_space=pltpu.HBM)],
        out_specs=[vmem, vmem],
        out_shape=(
            jax.ShapeDtypeStruct((1, slots), jnp.int32),
            pltpu.VMEM(expert_down.shape, expert_down.dtype),
        ),
        scratch_shapes=[pltpu.SemaphoreType.DMA],
        compiler_params=pltpu.CompilerParams(vmem_limit_bytes=SCOPED_BYTES),
        cost_estimate=pl.CostEstimate(
            flops=0, bytes_accessed=2 * expert_down.size, transcendentals=0
        ),
        name="load_down",
    )(
        pltpu.with_memory_space_constraint(lengths.reshape(1, -1), pltpu.HBM),
        pltpu.with_memory_space_constraint(assignment.reshape(1, -1), pltpu.HBM),
        pltpu.with_memory_space_constraint(expert_down, pltpu.HBM),
    )


def attend_kernel(first, pieces, queries_ref, fresh_ref, tags_ref, *refs):
    arrived_refs, out_ref, cache_ref = refs[:pieces], refs[pieces], refs[pieces + 1]
    mine = pl.program_id(0)
    rows, width = arrived_refs[0].shape[0], cache_ref.shape[1]

    @pl.when(mine == 0)
    def _():
        for i, arrived_ref in enumerate(arrived_refs):
            cache_ref[i * rows : (i + 1) * rows, :] = arrived_ref[:, first : first + width]

    steps, _, heads, width = queries_ref.shape
    latent = out_ref.shape[3]
    per_owner = fresh_ref.shape[1]
    rows = steps * heads
    queries = queries_ref[...].reshape(rows, width)
    cache = cache_ref[...]
    fresh = jnp.concatenate([fresh_ref[u].astype(jnp.float32) for u in range(steps)], axis=0)
    fresh = fresh.astype(jnp.bfloat16)
    contract = (((1,), (1,)), ((), ()))
    scores = (
        lax.dot_general(queries, cache, contract, preferred_element_type=jnp.float32)
        * score_scale
    )
    scores = jnp.where(tags_ref[...] == mine, scores, masked_score)
    fresh_scores = (
        lax.dot_general(queries, fresh, contract, preferred_element_type=jnp.float32)
        * score_scale
    )
    step = lax.broadcasted_iota(jnp.int32, (rows, steps * per_owner), 0) // heads
    other = lax.broadcasted_iota(jnp.int32, (rows, steps * per_owner), 1)
    seen = (other % per_owner == mine) & (other // per_owner <= step)
    fresh_scores = jnp.where(seen, fresh_scores, masked_score)
    top_score = jnp.maximum(
        jnp.max(scores, axis=1, keepdims=True), jnp.max(fresh_scores, axis=1, keepdims=True)
    )
    weights = jnp.exp(scores - top_score)
    fresh_weights = jnp.exp(fresh_scores - top_score)
    denominator = jnp.sum(weights, axis=1, keepdims=True) + jnp.sum(
        fresh_weights, axis=1, keepdims=True
    )
    summed = jnp.dot(
        weights.astype(jnp.bfloat16), cache[:, :latent], preferred_element_type=jnp.float32
    ) + jnp.dot(
        fresh_weights.astype(jnp.bfloat16),
        fresh[:, :latent],
        preferred_element_type=jnp.float32,
    )
    context = (summed / denominator).astype(jnp.bfloat16)
    out_ref[...] = context.reshape(steps, 1, heads, latent)


def attend(queries, new_kv, arrived, first, tags):
    steps, per_owner, heads, width = queries.shape
    slots = tags.shape[1]
    latent = width - ROPE
    return pl.pallas_call(
        functools.partial(attend_kernel, first, len(arrived)),
        grid=(per_owner,),
        in_specs=[
            pl.BlockSpec((steps, 1, heads, width), lambda q: (0, q, 0, 0)),
            pl.BlockSpec((steps, per_owner, width), lambda q: (0, 0, 0)),
            pl.BlockSpec((1, slots), lambda q: (0, 0)),
        ]
        + [pl.BlockSpec(piece.shape, lambda q: (0, 0)) for piece in arrived],
        out_specs=pl.BlockSpec((steps, 1, heads, latent), lambda q: (0, q, 0, 0)),
        out_shape=jax.ShapeDtypeStruct((steps, per_owner, heads, latent), jnp.bfloat16),
        scratch_shapes=[pltpu.VMEM((slots, width), jnp.bfloat16)],
        compiler_params=pltpu.CompilerParams(vmem_limit_bytes=SCOPED_BYTES),
        cost_estimate=pl.CostEstimate(
            flops=2 * steps * per_owner * heads * slots * (width + latent),
            bytes_accessed=2 * steps * per_owner * heads * (width + latent),
            transcendentals=steps * per_owner * heads * slots,
        ),
        name="attend",
    )(queries, new_kv, tags, *arrived)


def expert_kernel(bits, first, pieces, down_ref, *refs):
    arrived_refs, (keep_ref, send_ref, sorted_ref) = refs[:pieces], refs[pieces:]
    half, width = keep_ref.shape
    hidden_width = sorted_ref.shape[1]
    per_piece = arrived_refs[0].shape[0] // BLOCK
    for place in range(1 << len(bits)):
        piece, block = divmod(apart_of(place, bits), per_piece)
        sorted_ref[place * BLOCK : (place + 1) * BLOCK, :] = arrived_refs[piece][
            block * BLOCK : (block + 1) * BLOCK, :hidden_width
        ]
    result = jnp.dot(
        sorted_ref[...],
        down_ref[0, :, first : first + width],
        preferred_element_type=jnp.float32,
    )
    keep_ref[...] = result[:half]
    send_ref[...] = result[half:].astype(jnp.bfloat16)


def expert_part(arrived, expert_down, bits, part, parts):
    slots = BLOCK << len(bits)
    _, hidden_width, model_width = expert_down.shape
    width = model_width // parts
    half = slots // 2
    vmem = pl.BlockSpec(memory_space=pltpu.VMEM)
    return pl.pallas_call(
        functools.partial(expert_kernel, bits, part * width, len(arrived)),
        in_specs=[vmem] * (1 + len(arrived)),
        out_specs=[vmem] * 2,
        out_shape=(
            jax.ShapeDtypeStruct((half, width), jnp.float32),
            jax.ShapeDtypeStruct((half, width), jnp.bfloat16),
        ),
        scratch_shapes=[pltpu.VMEM((slots, hidden_width), jnp.bfloat16)],
        compiler_params=pltpu.CompilerParams(vmem_limit_bytes=SCOPED_BYTES),
        cost_estimate=pl.CostEstimate(
            flops=2 * slots * hidden_width * width,
            bytes_accessed=2 * hidden_width * width,
            transcendentals=0,
        ),
        name="expert_part",
    )(expert_down, *arrived)


after = lax.optimization_barrier


def swap(values, bit, devices):
    return lax.ppermute(values, "seq", [(i, i ^ bit) for i in range(devices)])


def fold(kept, received):
    total = kept + received.astype(jnp.float32)
    half = total.shape[0] // 2
    return total[:half], total[half:].astype(jnp.bfloat16)


def per_device_dense(
    prefill_kv,
    lengths,
    assignment,
    queries,
    new_kv,
    expert_hidden,
    routes,
    route_weights,
    expert_down,
):
    devices = lax.axis_size("seq")
    steps, per_owner = queries.shape[:2]
    rows, _, top, hidden_width = expert_hidden.shape
    model_width = expert_down.shape[2]
    near, far = pack_outboxes(
        routes, route_weights, expert_hidden, lengths, assignment, prefill_kv, devices
    )
    crossed = swap(far, 1, devices)
    chips = devices // 2
    arrived = [None] * chips
    for apart in (0, 4, 2, 6, 1, 5, 3, 7):
        block = slice(apart * BLOCK, (apart + 1) * BLOCK)
        piece = jnp.concatenate([near[block], crossed[block]], axis=0)
        arrived[apart] = swap(piece, 2 * apart, devices) if apart else piece
    late_lengths, _ = after((lengths, arrived[4]))
    tags, down = load_down(
        late_lengths, assignment, expert_down, devices, per_owner, devices * BLOCK
    )
    context = attend(queries, new_kv, arrived, hidden_width, tags)

    orders = ((1, 2, 4, 8), (1, 4, 2, 8))
    flows = []
    for part, bits in enumerate(orders):
        kept, sent = expert_part(arrived, down, bits, part, len(orders))
        flows.append((kept, swap(sent, bits[0], devices)))
    flows = [fold(kept, received) for kept, received in flows]
    received = [swap(sent, bits[1], devices) for (_, sent), bits in zip(flows, orders)]
    flows = [fold(kept, got) for (kept, _), got in zip(flows, received)]
    received = [swap(sent, bits[2], devices) for (_, sent), bits in zip(flows, orders)]
    flows = [fold(kept, got) for (kept, _), got in zip(flows, received)]
    kept = jnp.concatenate([kept for kept, _ in flows], axis=1)
    sent = jnp.concatenate([sent for _, sent in flows], axis=1)
    received = swap(sent, orders[0][-1], devices)
    received, context = lax.optimization_barrier((received, context))
    moe_out = (kept + received.astype(jnp.float32)).astype(jnp.bfloat16)
    return context, moe_out.reshape(rows, steps, model_width)


def per_device(*arrays):
    expert_hidden, expert_down = arrays[5], arrays[8]
    devices = lax.axis_size("seq")
    rows, steps, top = expert_hidden.shape[:3]
    tokens = rows * steps
    experts = expert_down.shape[0] * devices
    bound = max(2, 2 * tokens * top // experts)
    if devices == 16 and experts == devices and tokens == BLOCK and bound == tokens:
        return per_device_dense(*arrays)
    return per_device_general(*arrays)


def solution(mesh):
    placed = (
        P(("groups", "seq"), None),
        P("groups"),
        P("groups"),
        P(None, ("groups", "seq"), None, None),
        P(None, ("groups", "seq"), None),
        P(("groups", "seq"), None, None, None),
        P(("groups", "seq"), None, None),
        P(("groups", "seq"), None, None),
        P("seq", None, None),
    )
    return jax.shard_map(
        per_device,
        mesh=mesh,
        in_specs=placed,
        out_specs=(P(None, ("groups", "seq"), None, None), P(("groups", "seq"), None, None)),
        check_vma=False,
    )
```

```python
import functools

import jax
import jax.numpy as jnp
from jax import lax
from jax.experimental import pallas as pl
from jax.experimental.pallas import tpu as pltpu
from jax.sharding import PartitionSpec as P

ROPE = 64
HALF = 2


score_scale = 192.0 ** (-0.5)
masked_score = -1e30


def slot_sources(slot_ids, slot_total):
    source_rows = jnp.arange(slot_ids.shape[0], dtype=jnp.int32)
    matched = slot_ids[None, :] == jnp.arange(slot_total, dtype=jnp.int32)[:, None]
    return jnp.max(jnp.where(matched, source_rows[None, :], -1), axis=1)


def fill_slots(values, sources, filler):
    taken = jnp.take(values, jnp.maximum(sources, 0), axis=0)
    valid = (sources >= 0).reshape((-1,) + (1,) * (values.ndim - 1))
    return jnp.where(valid, taken, jnp.asarray(filler, values.dtype))


def hand_over(prefill_kv, lengths, assignment, per_owner):
    device_count = lax.axis_size("seq")
    own_index = lax.axis_index("seq")
    ctx_here, kv_width = prefill_kv.shape
    position = jnp.arange(ctx_here, dtype=jnp.int32) * device_count + own_index
    request_ends = jnp.cumsum(lengths)
    request = jnp.sum((position[:, None] >= request_ends[None, :]).astype(jnp.int32), axis=1)
    total_rows = assignment.shape[0]
    row_numbers = jnp.arange(total_rows, dtype=jnp.int32)
    serving = jnp.sum(
        jnp.where(assignment[None, :] == row_numbers[:, None], row_numbers[None, :], 0), axis=1
    )
    decode_row = jnp.sum(
        jnp.where(request[:, None] == row_numbers[None, :], serving[None, :], 0), axis=1
    )
    owner_index = decode_row // per_owner
    local_request = decode_row % per_owner
    onehot = (owner_index[:, None] == jnp.arange(device_count, dtype=jnp.int32)[None, :]).astype(
        jnp.int32
    )
    slot_rank = jnp.sum((jnp.cumsum(onehot, axis=0) - onehot) * onehot, axis=1)
    slot_count = 2 * HALF * per_owner
    sources = slot_sources(owner_index * slot_count + slot_rank, device_count * slot_count)
    outbox = fill_slots(prefill_kv, sources, 0).reshape(device_count, slot_count, kv_width)
    labels = fill_slots(local_request, sources, -1).reshape(device_count, slot_count)
    kv_cache, cache_tags = (
        lax.all_to_all(outbox, "seq", split_axis=0, concat_axis=0, tiled=True),
        lax.all_to_all(labels, "seq", split_axis=0, concat_axis=0, tiled=True),
    )
    return (kv_cache.reshape(device_count * slot_count, kv_width), cache_tags.reshape(-1))


def fresh_part(queries, new_kv):
    step_count = queries.shape[0]
    fresh_scores = (
        jnp.einsum("sqhk,uqk->sqhu", queries, new_kv, preferred_element_type=jnp.float32)
        * score_scale
    )
    causal = jnp.arange(step_count)[:, None] >= jnp.arange(step_count)[None, :]
    return jnp.where(causal[:, None, None, :], fresh_scores, masked_score)


def attend_dense(queries, new_kv, kv_cache, cache_tags):
    step_count, per_owner, head_count, kv_width = queries.shape
    latent = kv_width - ROPE
    query_rows = queries.reshape(step_count * per_owner * head_count, kv_width)
    scores = (
        jnp.einsum("rk,ck->rc", query_rows, kv_cache, preferred_element_type=jnp.float32)
        * score_scale
    )
    row_request = jnp.broadcast_to(
        jnp.arange(per_owner, dtype=jnp.int32)[None, :, None], (step_count, per_owner, head_count)
    ).reshape(-1)
    allowed = cache_tags[None, :] == row_request[:, None]
    scores = jnp.where(allowed, scores, masked_score).reshape(step_count, per_owner, head_count, -1)
    fresh_scores = fresh_part(queries, new_kv)
    top_score = jnp.maximum(jnp.max(scores, axis=-1), jnp.max(fresh_scores, axis=-1))
    weights = jnp.exp(scores - top_score[..., None])
    fresh_weights = jnp.exp(fresh_scores - top_score[..., None])
    denominator = jnp.sum(weights, axis=-1) + jnp.sum(fresh_weights, axis=-1)
    summed = jnp.einsum(
        "sqhc,cl->sqhl",
        weights.astype(jnp.bfloat16),
        kv_cache[:, :latent],
        preferred_element_type=jnp.float32,
    )
    summed = summed + jnp.einsum(
        "sqhu,uql->sqhl",
        fresh_weights.astype(jnp.bfloat16),
        new_kv[..., :latent],
        preferred_element_type=jnp.float32,
    )
    return (summed / denominator[..., None]).astype(jnp.bfloat16)


def expert_layer(expert_hidden, routes, route_weights, expert_down):
    device_count = lax.axis_size("seq")
    rows_here, step_count, top_count, hidden_width = expert_hidden.shape
    per_dev = expert_down.shape[0]
    experts = per_dev * device_count
    capacity = max(2, 2 * step_count * rows_here * top_count // experts)
    flat_routes = routes.reshape(-1)
    route_count = flat_routes.shape[0]
    onehot = (flat_routes[:, None] == jnp.arange(experts, dtype=jnp.int32)[None, :]).astype(
        jnp.int32
    )
    slot_index = jnp.sum((jnp.cumsum(onehot, axis=0) - onehot) * onehot, axis=1)
    flat_hidden = expert_hidden.reshape(route_count, hidden_width)
    slot_ids = flat_routes * capacity + slot_index
    sources = slot_sources(slot_ids, experts * capacity)
    outbox = fill_slots(flat_hidden, sources, 0).reshape(
        device_count, per_dev, capacity, hidden_width
    )
    expert_out = jnp.einsum(
        "dekh,ehm->dekm",
        lax.all_to_all(outbox, "seq", split_axis=0, concat_axis=0, tiled=True),
        expert_down,
        preferred_element_type=jnp.float32,
    ).astype(jnp.bfloat16)
    returned = lax.all_to_all(expert_out, "seq", split_axis=0, concat_axis=0, tiled=True)
    returned = returned.reshape(experts * capacity, returned.shape[-1])
    picked = jnp.take(returned, slot_ids, axis=0).astype(jnp.float32)
    weighted = picked * route_weights.reshape(route_count, 1)
    moe_out = jnp.sum(weighted.reshape(rows_here, step_count, top_count, -1), axis=2)
    return moe_out.astype(jnp.bfloat16)


def per_device_general(
    prefill_kv,
    lengths,
    assignment,
    queries,
    new_kv,
    expert_hidden,
    routes,
    route_weights,
    expert_down,
):
    kv_cache, cache_tags = hand_over(prefill_kv, lengths, assignment, queries.shape[1])
    context = attend_dense(queries, new_kv, kv_cache, cache_tags)
    moe_out = expert_layer(expert_hidden, routes, route_weights, expert_down)
    return (context, moe_out)


BLOCK = 16
CHIP_ORDER = (0, 4, 2, 6, 1, 5, 3, 7)
EARLY = 5
SCOPED_BYTES = 16 * 2**20


def as_column(row):
    size = row.shape[1]
    eye = lax.broadcasted_iota(jnp.int32, (size, size), 0) == lax.broadcasted_iota(
        jnp.int32, (size, size), 1
    )
    return jnp.sum(jnp.where(eye, row, 0), axis=1, keepdims=True)


def flat_row(table, tokens, top):
    lanes = tokens * top
    place = lax.broadcasted_iota(jnp.int32, (top, lanes), 1) % top
    spread = (place == lax.broadcasted_iota(jnp.int32, (top, lanes), 0)).astype(jnp.float32)
    wide = jnp.dot(
        table, spread, precision=lax.Precision.HIGHEST, preferred_element_type=jnp.float32
    )
    owner = lax.broadcasted_iota(jnp.int32, (tokens, lanes), 1) // top
    mine = owner == lax.broadcasted_iota(jnp.int32, (tokens, lanes), 0)
    return jnp.sum(jnp.where(mine, wide, 0.0), axis=0, keepdims=True)


def ceil_rows(position, source, devices):
    return (position + (devices - 1) - source) // devices


def request_spans(lengths_ref, assignment_ref):
    requests = lengths_ref.shape[1]
    length_column = as_column(lengths_ref[...])
    assignment = assignment_ref[...]
    number = lax.broadcasted_iota(jnp.int32, (requests, requests), 0)
    before = jnp.sum(jnp.where(number < assignment, length_column, 0), axis=0, keepdims=True)
    own = jnp.sum(jnp.where(number == assignment, length_column, 0), axis=0, keepdims=True)
    return before, before + own


def apart_of(place, bits):
    apart = place * 0
    for i, bit in enumerate(bits):
        digit = (place // (1 << (len(bits) - 1 - i))) % 2
        apart = apart + digit * bit
    return apart


def outbox_kernel(
    chips,
    per_owner,
    routes_ref,
    weights_ref,
    hidden_ref,
    lengths_ref,
    assignment_ref,
    kv_ref,
    *out_refs,
):
    me = lax.axis_index("seq")
    devices = 2 * chips
    room = out_refs[0].shape[0] // 2
    slots = room * devices
    rows, steps, top = routes_ref.shape
    tokens = rows * steps
    lanes = tokens * top
    hidden_width = hidden_ref.shape[1]
    routes = jnp.concatenate([routes_ref[i] for i in range(rows)], axis=0).astype(jnp.float32)
    weights = jnp.concatenate([weights_ref[i] for i in range(rows)], axis=0)
    route_row = flat_row(routes, tokens, top).astype(jnp.int32)
    weight_row = flat_row(weights, tokens, top)
    slot = lax.broadcasted_iota(jnp.int32, (slots, lanes), 0)
    lane = lax.broadcasted_iota(jnp.int32, (slots, lanes), 1)
    block = slot // room
    target = me ^ block
    pick = (lane // top == slot % room) & (route_row == target)
    scale = jnp.sum(jnp.where(pick, weight_row, 0.0), axis=1, keepdims=True)
    chosen = jnp.where(pick, 1.0, 0.0).astype(jnp.bfloat16)
    moved = jnp.dot(chosen, hidden_ref[...], preferred_element_type=jnp.float32)
    moved = (moved * scale).astype(jnp.bfloat16)
    for chip in range(chips):
        out_refs[chip][:, :hidden_width] = moved[2 * chip * room : 2 * (chip + 1) * room]

    requests = lengths_ref.shape[1]
    kv_width, here = kv_ref.shape
    before, after_last = request_spans(lengths_ref, assignment_ref)
    low = ceil_rows(before, me, devices)
    count = ceil_rows(after_last, me, devices) - low
    number = lax.broadcasted_iota(jnp.int32, (requests, requests), 0)
    line = lax.broadcasted_iota(jnp.int32, (requests, requests), 1)
    same = (number // per_owner == line // per_owner) & (number < line)
    offset = jnp.sum(jnp.where(same, as_column(count), 0), axis=0, keepdims=True)
    slot = lax.broadcasted_iota(jnp.int32, (slots, requests), 0)
    decode = lax.broadcasted_iota(jnp.int32, (slots, requests), 1)
    block = slot // room
    target = me ^ block
    rank = slot % room - offset
    held = (target == decode // per_owner) & (rank >= 0) & (rank < count)
    source = jnp.sum(jnp.where(held, low + rank + 1, 0), axis=1, keepdims=True) - 1
    pick = source == lax.broadcasted_iota(jnp.int32, (slots, here), 1)
    moved = lax.dot_general(
        jnp.where(pick, 1.0, 0.0).astype(jnp.bfloat16),
        kv_ref[...],
        (((1,), (1,)), ((), ())),
        preferred_element_type=jnp.float32,
    ).astype(jnp.bfloat16)
    last = hidden_width + kv_width
    empty = jnp.zeros((2 * room, out_refs[0].shape[1] - last), jnp.bfloat16)
    for chip in range(chips):
        out_refs[chip][:, hidden_width:last] = moved[2 * chip * room : 2 * (chip + 1) * room]
        out_refs[chip][:, last:] = empty


def pack_outboxes(
    routes, route_weights, expert_hidden, lengths, assignment, prefill_kv, devices
):
    rows, steps, top, hidden_width = expert_hidden.shape
    here, kv_width = prefill_kv.shape
    tokens = rows * steps
    slots = tokens * devices
    width = pl.cdiv(hidden_width + kv_width, 128) * 128
    operands = (
        routes,
        route_weights,
        expert_hidden.reshape(tokens * top, hidden_width),
        lengths.reshape(1, -1),
        assignment.reshape(1, -1),
        prefill_kv.T,
    )
    return pl.pallas_call(
        functools.partial(outbox_kernel, devices // 2, rows),
        out_shape=(jax.ShapeDtypeStruct((2 * tokens, width), jnp.bfloat16),) * (devices // 2),
        compiler_params=pltpu.CompilerParams(vmem_limit_bytes=SCOPED_BYTES),
        cost_estimate=pl.CostEstimate(
            flops=2 * slots * (tokens * top * hidden_width + here * kv_width),
            bytes_accessed=4 * slots * width,
            transcendentals=0,
        ),
        name="pack_outboxes",
    )(*(pltpu.with_memory_space_constraint(x, pltpu.HBM) for x in operands))


def load_kernel(
    devices, per_owner, lengths_ref, assignment_ref, down_ref, tags_ref, held_ref, sem
):
    copy = pltpu.make_async_copy(down_ref, held_ref, sem)
    copy.start()
    me = lax.axis_index("seq")
    requests = lengths_ref.shape[1]
    slots = tags_ref.shape[1]
    room = slots // devices
    before, after = request_spans(lengths_ref, assignment_ref)
    place = lax.broadcasted_iota(jnp.int32, (1, slots), 1)
    sender, rank = me ^ (place // room), place % room
    tags = jnp.full((1, slots), -1, jnp.int32)
    decode = lax.broadcasted_iota(jnp.int32, (1, requests), 1)
    taken = jnp.zeros((1, slots), jnp.int32)
    for q in range(per_owner):
        mine = decode == me * per_owner + q
        first = jnp.sum(jnp.where(mine, before, 0), axis=1, keepdims=True)
        last = jnp.sum(jnp.where(mine, after, 0), axis=1, keepdims=True)
        arriving = ceil_rows(last, sender, devices) - ceil_rows(first, sender, devices)
        tags = jnp.where((rank >= taken) & (rank < taken + arriving), q, tags)
        taken = taken + arriving
    tags_ref[...] = tags
    copy.wait()


def load_down(lengths, assignment, expert_down, devices, per_owner, slots):
    vmem = pl.BlockSpec(memory_space=pltpu.VMEM)
    return pl.pallas_call(
        functools.partial(load_kernel, devices, per_owner),
        in_specs=[vmem, vmem, pl.BlockSpec(memory_space=pltpu.HBM)],
        out_specs=[vmem, vmem],
        out_shape=(
            jax.ShapeDtypeStruct((1, slots), jnp.int32),
            pltpu.VMEM(expert_down.shape, expert_down.dtype),
        ),
        scratch_shapes=[pltpu.SemaphoreType.DMA],
        compiler_params=pltpu.CompilerParams(vmem_limit_bytes=SCOPED_BYTES),
        cost_estimate=pl.CostEstimate(
            flops=0, bytes_accessed=2 * expert_down.size, transcendentals=0
        ),
        name="load_down",
    )(
        pltpu.with_memory_space_constraint(lengths.reshape(1, -1), pltpu.HBM),
        pltpu.with_memory_space_constraint(assignment.reshape(1, -1), pltpu.HBM),
        pltpu.with_memory_space_constraint(expert_down, pltpu.HBM),
    )


def blocks_of(chip, arrived_refs, crossed_refs):
    place = CHIP_ORDER.index(chip)
    late = place >= EARLY
    start = (place - EARLY * late) * BLOCK
    return (
        (arrived_refs[place], slice(0, BLOCK)),
        (crossed_refs[late], slice(start, start + BLOCK)),
    )


def attend_kernel(first, pieces, queries_ref, fresh_ref, tags_ref, *refs):
    arrived_refs, crossed_refs = refs[:pieces], refs[pieces:-2]
    out_ref, cache_ref = refs[-2:]
    mine = pl.program_id(0)
    latent_columns = slice(first, first + cache_ref.shape[1])

    @pl.when(mine == 0)
    def _():
        for chip in range(pieces):
            for block, rows in enumerate(blocks_of(chip, arrived_refs, crossed_refs)):
                start = (2 * chip + block) * BLOCK
                cache_ref[start : start + BLOCK, :] = rows[0][rows[1], latent_columns]

    steps, _, heads, width = queries_ref.shape
    latent = out_ref.shape[3]
    per_owner = fresh_ref.shape[1]
    rows = steps * heads
    queries = queries_ref[...].reshape(rows, width)
    cache = cache_ref[...]
    fresh = jnp.concatenate([fresh_ref[u].astype(jnp.float32) for u in range(steps)], axis=0)
    fresh = fresh.astype(jnp.bfloat16)
    contract = (((1,), (1,)), ((), ()))
    scores = (
        lax.dot_general(queries, cache, contract, preferred_element_type=jnp.float32)
        * score_scale
    )
    scores = jnp.where(tags_ref[...] == mine, scores, masked_score)
    fresh_scores = (
        lax.dot_general(queries, fresh, contract, preferred_element_type=jnp.float32)
        * score_scale
    )
    step = lax.broadcasted_iota(jnp.int32, (rows, steps * per_owner), 0) // heads
    other = lax.broadcasted_iota(jnp.int32, (rows, steps * per_owner), 1)
    seen = (other % per_owner == mine) & (other // per_owner <= step)
    fresh_scores = jnp.where(seen, fresh_scores, masked_score)
    top_score = jnp.maximum(
        jnp.max(scores, axis=1, keepdims=True), jnp.max(fresh_scores, axis=1, keepdims=True)
    )
    weights = jnp.exp(scores - top_score)
    fresh_weights = jnp.exp(fresh_scores - top_score)
    denominator = jnp.sum(weights, axis=1, keepdims=True) + jnp.sum(
        fresh_weights, axis=1, keepdims=True
    )
    summed = jnp.dot(
        weights.astype(jnp.bfloat16), cache[:, :latent], preferred_element_type=jnp.float32
    ) + jnp.dot(
        fresh_weights.astype(jnp.bfloat16),
        fresh[:, :latent],
        preferred_element_type=jnp.float32,
    )
    context = (summed / denominator).astype(jnp.bfloat16)
    out_ref[...] = context.reshape(steps, 1, heads, latent)


def attend(queries, new_kv, arrived, crossed, first, tags):
    steps, per_owner, heads, width = queries.shape
    slots = tags.shape[1]
    latent = width - ROPE
    return pl.pallas_call(
        functools.partial(attend_kernel, first, len(arrived)),
        grid=(per_owner,),
        in_specs=[
            pl.BlockSpec((steps, 1, heads, width), lambda q: (0, q, 0, 0)),
            pl.BlockSpec((steps, per_owner, width), lambda q: (0, 0, 0)),
            pl.BlockSpec((1, slots), lambda q: (0, 0)),
        ]
        + [pl.BlockSpec(piece.shape, lambda q: (0, 0)) for piece in arrived + crossed],
        out_specs=pl.BlockSpec((steps, 1, heads, latent), lambda q: (0, q, 0, 0)),
        out_shape=jax.ShapeDtypeStruct((steps, per_owner, heads, latent), jnp.bfloat16),
        scratch_shapes=[pltpu.VMEM((slots, width), jnp.bfloat16)],
        compiler_params=pltpu.CompilerParams(vmem_limit_bytes=SCOPED_BYTES),
        cost_estimate=pl.CostEstimate(
            flops=2 * steps * per_owner * heads * slots * (width + latent),
            bytes_accessed=2 * steps * per_owner * heads * (width + latent),
            transcendentals=steps * per_owner * heads * slots,
        ),
        name="attend",
    )(queries, new_kv, tags, *arrived, *crossed)


def kept_kernel(orders, pieces, down_ref, *refs):
    arrived_refs, out_refs, sorted_ref = refs[:pieces], refs[pieces:-1], refs[-1]
    width = out_refs[0].shape[1]
    hidden_width = sorted_ref.shape[1]
    for part, (bits, out_ref) in enumerate(zip(orders, out_refs)):
        for place in range(pieces):
            ref, rows = blocks_of(apart_of(place, bits), arrived_refs, (None, None))[0]
            sorted_ref[place * BLOCK : (place + 1) * BLOCK, :] = ref[rows, :hidden_width]
        out_ref[...] = jnp.dot(
            sorted_ref[...],
            down_ref[0, :, part * width : (part + 1) * width],
            preferred_element_type=jnp.float32,
        )


def sent_kernel(bits, first, pieces, down_ref, early_ref, late_ref, out_ref, sorted_ref):
    width = out_ref.shape[1]
    hidden_width = sorted_ref.shape[1]
    for place in range(pieces):
        ref, rows = blocks_of(apart_of(place, bits), (None,) * pieces, (early_ref, late_ref))[1]
        sorted_ref[place * BLOCK : (place + 1) * BLOCK, :] = ref[rows, :hidden_width]
    result = jnp.dot(
        sorted_ref[...],
        down_ref[0, :, first : first + width],
        preferred_element_type=jnp.float32,
    )
    out_ref[...] = result.astype(jnp.bfloat16)


def expert_call(kernel, expert_down, arrays, pieces, outs, name):
    _, hidden_width, model_width = expert_down.shape
    slots = BLOCK * pieces
    vmem = pl.BlockSpec(memory_space=pltpu.VMEM)
    return pl.pallas_call(
        kernel,
        in_specs=[vmem] * (1 + len(arrays)),
        out_specs=[vmem] * len(outs),
        out_shape=outs,
        scratch_shapes=[pltpu.VMEM((slots, hidden_width), jnp.bfloat16)],
        compiler_params=pltpu.CompilerParams(vmem_limit_bytes=SCOPED_BYTES),
        cost_estimate=pl.CostEstimate(
            flops=2 * slots * hidden_width * sum(out.shape[1] for out in outs),
            bytes_accessed=2 * hidden_width * sum(out.shape[1] for out in outs),
            transcendentals=0,
        ),
        name=name,
    )(expert_down, *arrays)


after = lax.optimization_barrier


def swap(values, bit, devices):
    return lax.ppermute(values, "seq", [(i, i ^ bit) for i in range(devices)])


def fold(kept, received):
    total = kept + received.astype(jnp.float32)
    half = total.shape[0] // 2
    return total[:half], total[half:].astype(jnp.bfloat16)


def per_device_dense(
    prefill_kv,
    lengths,
    assignment,
    queries,
    new_kv,
    expert_hidden,
    routes,
    route_weights,
    expert_down,
):
    devices = lax.axis_size("seq")
    steps, per_owner = queries.shape[:2]
    rows, _, top, hidden_width = expert_hidden.shape
    model_width = expert_down.shape[2]
    outboxes = pack_outboxes(
        routes, route_weights, expert_hidden, lengths, assignment, prefill_kv, devices
    )
    chips = devices // 2
    arrived = [
        swap(outboxes[apart], 2 * apart, devices) if apart else outboxes[apart]
        for apart in CHIP_ORDER
    ]
    late_lengths, _ = after((lengths, arrived[1]))
    tags, down = load_down(
        late_lengths, assignment, expert_down, devices, per_owner, devices * BLOCK
    )
    late, _ = after((arrived[EARLY:], tags))
    crossed = [
        swap(jnp.concatenate([piece[BLOCK:] for piece in group], axis=0), 1, devices)
        for group in (arrived[:EARLY], late)
    ]
    context = attend(queries, new_kv, arrived, crossed, hidden_width, tags)

    orders = ((1, 2, 4), (2, 1, 4))
    width = model_width // len(orders)
    half = devices * BLOCK // 2
    kept = expert_call(
        functools.partial(kept_kernel, orders, chips),
        down,
        arrived,
        chips,
        (jax.ShapeDtypeStruct((half, width), jnp.float32),) * len(orders),
        "expert_kept",
    )
    crossed, kept = after((crossed, kept))
    flows = []
    for part, bits in enumerate(orders):
        (sent,) = expert_call(
            functools.partial(sent_kernel, bits, part * width, chips),
            down,
            crossed,
            chips,
            (jax.ShapeDtypeStruct((half, width), jnp.bfloat16),),
            "expert_sent",
        )
        flows.append((kept[part], swap(sent, 1, devices)))
    flows = [fold(kept, received) for kept, received in flows]
    received = [swap(sent, 2 * bits[0], devices) for (_, sent), bits in zip(flows, orders)]
    flows = [fold(kept, got) for (kept, _), got in zip(flows, received)]
    received = [swap(sent, 2 * bits[1], devices) for (_, sent), bits in zip(flows, orders)]
    flows = [fold(kept, got) for (kept, _), got in zip(flows, received)]
    kept = jnp.concatenate([kept for kept, _ in flows], axis=1)
    sent = jnp.concatenate([sent for _, sent in flows], axis=1)
    received = swap(sent, 2 * orders[0][-1], devices)
    received, context = lax.optimization_barrier((received, context))
    moe_out = (kept + received.astype(jnp.float32)).astype(jnp.bfloat16)
    return context, moe_out.reshape(rows, steps, model_width)


def per_device(*arrays):
    expert_hidden, expert_down = arrays[5], arrays[8]
    devices = lax.axis_size("seq")
    rows, steps, top = expert_hidden.shape[:3]
    tokens = rows * steps
    experts = expert_down.shape[0] * devices
    bound = max(2, 2 * tokens * top // experts)
    if devices == 16 and experts == devices and tokens == BLOCK and bound == tokens:
        return per_device_dense(*arrays)
    return per_device_general(*arrays)


def solution(mesh):
    placed = (
        P(("groups", "seq"), None),
        P("groups"),
        P("groups"),
        P(None, ("groups", "seq"), None, None),
        P(None, ("groups", "seq"), None),
        P(("groups", "seq"), None, None, None),
        P(("groups", "seq"), None, None),
        P(("groups", "seq"), None, None),
        P("seq", None, None),
    )
    return jax.shard_map(
        per_device,
        mesh=mesh,
        in_specs=placed,
        out_specs=(P(None, ("groups", "seq"), None, None), P(("groups", "seq"), None, None)),
        check_vma=False,
    )
```

```python
import functools

import jax
import jax.numpy as jnp
from jax import lax
from jax.experimental import pallas as pl
from jax.experimental.pallas import tpu as pltpu
from jax.sharding import PartitionSpec as P

ROPE = 64
HALF = 2


score_scale = 192.0 ** (-0.5)
masked_score = -1e30


def slot_sources(slot_ids, slot_total):
    source_rows = jnp.arange(slot_ids.shape[0], dtype=jnp.int32)
    matched = slot_ids[None, :] == jnp.arange(slot_total, dtype=jnp.int32)[:, None]
    return jnp.max(jnp.where(matched, source_rows[None, :], -1), axis=1)


def fill_slots(values, sources, filler):
    taken = jnp.take(values, jnp.maximum(sources, 0), axis=0)
    valid = (sources >= 0).reshape((-1,) + (1,) * (values.ndim - 1))
    return jnp.where(valid, taken, jnp.asarray(filler, values.dtype))


def hand_over(prefill_kv, lengths, assignment, per_owner):
    device_count = lax.axis_size("seq")
    own_index = lax.axis_index("seq")
    ctx_here, kv_width = prefill_kv.shape
    position = jnp.arange(ctx_here, dtype=jnp.int32) * device_count + own_index
    request_ends = jnp.cumsum(lengths)
    request = jnp.sum((position[:, None] >= request_ends[None, :]).astype(jnp.int32), axis=1)
    total_rows = assignment.shape[0]
    row_numbers = jnp.arange(total_rows, dtype=jnp.int32)
    serving = jnp.sum(
        jnp.where(assignment[None, :] == row_numbers[:, None], row_numbers[None, :], 0), axis=1
    )
    decode_row = jnp.sum(
        jnp.where(request[:, None] == row_numbers[None, :], serving[None, :], 0), axis=1
    )
    owner_index = decode_row // per_owner
    local_request = decode_row % per_owner
    onehot = (owner_index[:, None] == jnp.arange(device_count, dtype=jnp.int32)[None, :]).astype(
        jnp.int32
    )
    slot_rank = jnp.sum((jnp.cumsum(onehot, axis=0) - onehot) * onehot, axis=1)
    slot_count = 2 * HALF * per_owner
    sources = slot_sources(owner_index * slot_count + slot_rank, device_count * slot_count)
    outbox = fill_slots(prefill_kv, sources, 0).reshape(device_count, slot_count, kv_width)
    labels = fill_slots(local_request, sources, -1).reshape(device_count, slot_count)
    kv_cache, cache_tags = (
        lax.all_to_all(outbox, "seq", split_axis=0, concat_axis=0, tiled=True),
        lax.all_to_all(labels, "seq", split_axis=0, concat_axis=0, tiled=True),
    )
    return (kv_cache.reshape(device_count * slot_count, kv_width), cache_tags.reshape(-1))


def fresh_part(queries, new_kv):
    step_count = queries.shape[0]
    fresh_scores = (
        jnp.einsum("sqhk,uqk->sqhu", queries, new_kv, preferred_element_type=jnp.float32)
        * score_scale
    )
    causal = jnp.arange(step_count)[:, None] >= jnp.arange(step_count)[None, :]
    return jnp.where(causal[:, None, None, :], fresh_scores, masked_score)


def attend_dense(queries, new_kv, kv_cache, cache_tags):
    step_count, per_owner, head_count, kv_width = queries.shape
    latent = kv_width - ROPE
    query_rows = queries.reshape(step_count * per_owner * head_count, kv_width)
    scores = (
        jnp.einsum("rk,ck->rc", query_rows, kv_cache, preferred_element_type=jnp.float32)
        * score_scale
    )
    row_request = jnp.broadcast_to(
        jnp.arange(per_owner, dtype=jnp.int32)[None, :, None], (step_count, per_owner, head_count)
    ).reshape(-1)
    allowed = cache_tags[None, :] == row_request[:, None]
    scores = jnp.where(allowed, scores, masked_score).reshape(step_count, per_owner, head_count, -1)
    fresh_scores = fresh_part(queries, new_kv)
    top_score = jnp.maximum(jnp.max(scores, axis=-1), jnp.max(fresh_scores, axis=-1))
    weights = jnp.exp(scores - top_score[..., None])
    fresh_weights = jnp.exp(fresh_scores - top_score[..., None])
    denominator = jnp.sum(weights, axis=-1) + jnp.sum(fresh_weights, axis=-1)
    summed = jnp.einsum(
        "sqhc,cl->sqhl",
        weights.astype(jnp.bfloat16),
        kv_cache[:, :latent],
        preferred_element_type=jnp.float32,
    )
    summed = summed + jnp.einsum(
        "sqhu,uql->sqhl",
        fresh_weights.astype(jnp.bfloat16),
        new_kv[..., :latent],
        preferred_element_type=jnp.float32,
    )
    return (summed / denominator[..., None]).astype(jnp.bfloat16)


def expert_layer(expert_hidden, routes, route_weights, expert_down):
    device_count = lax.axis_size("seq")
    rows_here, step_count, top_count, hidden_width = expert_hidden.shape
    per_dev = expert_down.shape[0]
    experts = per_dev * device_count
    capacity = max(2, 2 * step_count * rows_here * top_count // experts)
    flat_routes = routes.reshape(-1)
    route_count = flat_routes.shape[0]
    onehot = (flat_routes[:, None] == jnp.arange(experts, dtype=jnp.int32)[None, :]).astype(
        jnp.int32
    )
    slot_index = jnp.sum((jnp.cumsum(onehot, axis=0) - onehot) * onehot, axis=1)
    flat_hidden = expert_hidden.reshape(route_count, hidden_width)
    slot_ids = flat_routes * capacity + slot_index
    sources = slot_sources(slot_ids, experts * capacity)
    outbox = fill_slots(flat_hidden, sources, 0).reshape(
        device_count, per_dev, capacity, hidden_width
    )
    expert_out = jnp.einsum(
        "dekh,ehm->dekm",
        lax.all_to_all(outbox, "seq", split_axis=0, concat_axis=0, tiled=True),
        expert_down,
        preferred_element_type=jnp.float32,
    ).astype(jnp.bfloat16)
    returned = lax.all_to_all(expert_out, "seq", split_axis=0, concat_axis=0, tiled=True)
    returned = returned.reshape(experts * capacity, returned.shape[-1])
    picked = jnp.take(returned, slot_ids, axis=0).astype(jnp.float32)
    weighted = picked * route_weights.reshape(route_count, 1)
    moe_out = jnp.sum(weighted.reshape(rows_here, step_count, top_count, -1), axis=2)
    return moe_out.astype(jnp.bfloat16)


def per_device_general(
    prefill_kv,
    lengths,
    assignment,
    queries,
    new_kv,
    expert_hidden,
    routes,
    route_weights,
    expert_down,
):
    kv_cache, cache_tags = hand_over(prefill_kv, lengths, assignment, queries.shape[1])
    context = attend_dense(queries, new_kv, kv_cache, cache_tags)
    moe_out = expert_layer(expert_hidden, routes, route_weights, expert_down)
    return (context, moe_out)


BLOCK = 16
LANES = 128
CHIP_ORDER = (0, 4, 2, 6, 1, 5, 3, 7)
EARLY = 5
SCOPED_BYTES = 16 * 2**20


def as_column(row):
    size = row.shape[1]
    eye = lax.broadcasted_iota(jnp.int32, (size, size), 0) == lax.broadcasted_iota(
        jnp.int32, (size, size), 1
    )
    return jnp.sum(jnp.where(eye, row, 0), axis=1, keepdims=True)


def flat_row(table, tokens, top):
    lanes = tokens * top
    place = lax.broadcasted_iota(jnp.int32, (top, lanes), 1) % top
    spread = (place == lax.broadcasted_iota(jnp.int32, (top, lanes), 0)).astype(jnp.float32)
    wide = jnp.dot(
        table, spread, precision=lax.Precision.HIGHEST, preferred_element_type=jnp.float32
    )
    owner = lax.broadcasted_iota(jnp.int32, (tokens, lanes), 1) // top
    mine = owner == lax.broadcasted_iota(jnp.int32, (tokens, lanes), 0)
    return jnp.sum(jnp.where(mine, wide, 0.0), axis=0, keepdims=True)


def ceil_rows(position, source, devices):
    return (position + (devices - 1) - source) // devices


def request_spans(lengths_ref, assignment_ref):
    requests = lengths_ref.shape[1]
    length_column = as_column(lengths_ref[...])
    assignment = assignment_ref[...]
    number = lax.broadcasted_iota(jnp.int32, (requests, requests), 0)
    before = jnp.sum(jnp.where(number < assignment, length_column, 0), axis=0, keepdims=True)
    own = jnp.sum(jnp.where(number == assignment, length_column, 0), axis=0, keepdims=True)
    return before, before + own


def apart_of(place, bits):
    apart = place * 0
    for i, bit in enumerate(bits):
        digit = (place // (1 << (len(bits) - 1 - i))) % 2
        apart = apart + digit * bit
    return apart


def outbox_kernel(
    chips,
    per_owner,
    routes_ref,
    weights_ref,
    hidden_ref,
    lengths_ref,
    assignment_ref,
    kv_ref,
    *out_refs,
):
    me = lax.axis_index("seq")
    devices = 2 * chips
    room = BLOCK
    slots = room * devices
    rows, steps, top = routes_ref.shape
    tokens = rows * steps
    lanes = tokens * top
    hidden_width = hidden_ref.shape[1]
    routes = jnp.concatenate([routes_ref[i] for i in range(rows)], axis=0).astype(jnp.float32)
    weights = jnp.concatenate([weights_ref[i] for i in range(rows)], axis=0)
    route_row = flat_row(routes, tokens, top).astype(jnp.int32)
    weight_row = flat_row(weights, tokens, top)
    slot = lax.broadcasted_iota(jnp.int32, (slots, lanes), 0)
    lane = lax.broadcasted_iota(jnp.int32, (slots, lanes), 1)
    block = slot // room
    target = me ^ block
    pick = (lane // top == slot % room) & (route_row == target)
    scale = jnp.sum(jnp.where(pick, weight_row, 0.0), axis=1, keepdims=True)
    chosen = jnp.where(pick, 1.0, 0.0).astype(jnp.bfloat16)
    moved = jnp.dot(chosen, hidden_ref[...], preferred_element_type=jnp.float32)
    moved = (moved * scale).astype(jnp.bfloat16)
    kv_width, here = kv_ref.shape
    tiles = (hidden_width + kv_width) // LANES
    for chip, out_ref in enumerate(out_refs):
        for block in range(2):
            start = (2 * chip + block) * room
            for tile in range(hidden_width // LANES):
                out_ref[(block * tiles + tile) * room : (block * tiles + tile + 1) * room, :] = (
                    moved[start : start + room, tile * LANES : (tile + 1) * LANES]
                )

    requests = lengths_ref.shape[1]
    before, after_last = request_spans(lengths_ref, assignment_ref)
    low = ceil_rows(before, me, devices)
    count = ceil_rows(after_last, me, devices) - low
    number = lax.broadcasted_iota(jnp.int32, (requests, requests), 0)
    line = lax.broadcasted_iota(jnp.int32, (requests, requests), 1)
    same = (number // per_owner == line // per_owner) & (number < line)
    offset = jnp.sum(jnp.where(same, as_column(count), 0), axis=0, keepdims=True)
    slot = lax.broadcasted_iota(jnp.int32, (slots, requests), 0)
    decode = lax.broadcasted_iota(jnp.int32, (slots, requests), 1)
    block = slot // room
    target = me ^ block
    rank = slot % room - offset
    held = (target == decode // per_owner) & (rank >= 0) & (rank < count)
    source = jnp.sum(jnp.where(held, low + rank + 1, 0), axis=1, keepdims=True) - 1
    pick = source == lax.broadcasted_iota(jnp.int32, (slots, here), 1)
    moved = lax.dot_general(
        jnp.where(pick, 1.0, 0.0).astype(jnp.bfloat16),
        kv_ref[...],
        (((1,), (1,)), ((), ())),
        preferred_element_type=jnp.float32,
    ).astype(jnp.bfloat16)
    whole = kv_width // LANES
    for chip, out_ref in enumerate(out_refs):
        ends = []
        for block in range(2):
            start = (2 * chip + block) * room
            for tile in range(whole):
                place = (block + 1) * tiles - whole + tile
                out_ref[place * room : (place + 1) * room, :] = moved[
                    start : start + room, tile * LANES : (tile + 1) * LANES
                ]
            ends.append(moved[start : start + room, whole * LANES :])
        out_ref[2 * tiles * room :, :] = jnp.concatenate(ends, axis=1)


def pack_outboxes(
    routes, route_weights, expert_hidden, lengths, assignment, prefill_kv, devices
):
    rows, steps, top, hidden_width = expert_hidden.shape
    here, kv_width = prefill_kv.shape
    tokens = rows * steps
    slots = tokens * devices
    tiles = (hidden_width + kv_width) // LANES
    operands = (
        routes,
        route_weights,
        expert_hidden.reshape(tokens * top, hidden_width),
        lengths.reshape(1, -1),
        assignment.reshape(1, -1),
        prefill_kv.T,
    )
    return pl.pallas_call(
        functools.partial(outbox_kernel, devices // 2, rows),
        out_shape=(jax.ShapeDtypeStruct(((2 * tiles + 1) * tokens, LANES), jnp.bfloat16),)
        * (devices // 2),
        compiler_params=pltpu.CompilerParams(vmem_limit_bytes=SCOPED_BYTES),
        cost_estimate=pl.CostEstimate(
            flops=2 * slots * (tokens * top * hidden_width + here * kv_width),
            bytes_accessed=4 * slots * (hidden_width + kv_width),
            transcendentals=0,
        ),
        name="pack_outboxes",
    )(*(pltpu.with_memory_space_constraint(x, pltpu.HBM) for x in operands))


def load_kernel(
    devices, per_owner, lengths_ref, assignment_ref, down_ref, tags_ref, held_ref, sem
):
    copy = pltpu.make_async_copy(down_ref, held_ref, sem)
    copy.start()
    me = lax.axis_index("seq")
    requests = lengths_ref.shape[1]
    slots = tags_ref.shape[1]
    room = slots // devices
    before, after = request_spans(lengths_ref, assignment_ref)
    place = lax.broadcasted_iota(jnp.int32, (1, slots), 1)
    sender, rank = me ^ (place // room), place % room
    tags = jnp.full((1, slots), -1, jnp.int32)
    decode = lax.broadcasted_iota(jnp.int32, (1, requests), 1)
    taken = jnp.zeros((1, slots), jnp.int32)
    for q in range(per_owner):
        mine = decode == me * per_owner + q
        first = jnp.sum(jnp.where(mine, before, 0), axis=1, keepdims=True)
        last = jnp.sum(jnp.where(mine, after, 0), axis=1, keepdims=True)
        arriving = ceil_rows(last, sender, devices) - ceil_rows(first, sender, devices)
        tags = jnp.where((rank >= taken) & (rank < taken + arriving), q, tags)
        taken = taken + arriving
    tags_ref[...] = tags
    copy.wait()


def load_down(lengths, assignment, expert_down, devices, per_owner, slots):
    vmem = pl.BlockSpec(memory_space=pltpu.VMEM)
    return pl.pallas_call(
        functools.partial(load_kernel, devices, per_owner),
        in_specs=[vmem, vmem, pl.BlockSpec(memory_space=pltpu.HBM)],
        out_specs=[vmem, vmem],
        out_shape=(
            jax.ShapeDtypeStruct((1, slots), jnp.int32),
            pltpu.VMEM(expert_down.shape, expert_down.dtype),
        ),
        scratch_shapes=[pltpu.SemaphoreType.DMA],
        compiler_params=pltpu.CompilerParams(vmem_limit_bytes=SCOPED_BYTES),
        cost_estimate=pl.CostEstimate(
            flops=0, bytes_accessed=2 * expert_down.size, transcendentals=0
        ),
        name="load_down",
    )(
        pltpu.with_memory_space_constraint(lengths.reshape(1, -1), pltpu.HBM),
        pltpu.with_memory_space_constraint(assignment.reshape(1, -1), pltpu.HBM),
        pltpu.with_memory_space_constraint(expert_down, pltpu.HBM),
    )


def blocks_of(chip, arrived_refs, crossed_refs, tiles):
    place = CHIP_ORDER.index(chip)
    late = place >= EARLY
    start = (place - EARLY * late) * (tiles + 1) * BLOCK
    return (arrived_refs[place], 0, tiles * BLOCK), (crossed_refs[late], start, 0)


def copy_tiles(ref, start, first, count, to_ref, place):
    for tile in range(count):
        at = start + (first + tile) * BLOCK
        to_ref[place * BLOCK : (place + 1) * BLOCK, tile * LANES : (tile + 1) * LANES] = ref[
            at : at + BLOCK, :
        ]


def attend_kernel(first, pieces, queries_ref, fresh_ref, tags_ref, *refs):
    arrived_refs, crossed_refs = refs[:pieces], refs[pieces:-2]
    out_ref, cache_ref = refs[-2:]
    mine = pl.program_id(0)
    kv_width = cache_ref.shape[1]
    whole = kv_width // LANES
    tiles = first // LANES + whole

    @pl.when(mine == 0)
    def _():
        for chip in range(pieces):
            for block, (ref, start, gap) in enumerate(
                blocks_of(chip, arrived_refs, crossed_refs, tiles)
            ):
                place = 2 * chip + block
                copy_tiles(ref, start, tiles - whole, whole, cache_ref, place)
                end = start + tiles * BLOCK + gap
                side = block * (kv_width - whole * LANES)
                cache_ref[place * BLOCK : (place + 1) * BLOCK, whole * LANES :] = ref[
                    end : end + BLOCK, side : side + kv_width - whole * LANES
                ]

    steps, _, heads, width = queries_ref.shape
    latent = out_ref.shape[3]
    per_owner = fresh_ref.shape[1]
    rows = steps * heads
    queries = queries_ref[...].reshape(rows, width)
    cache = cache_ref[...]
    fresh = jnp.concatenate([fresh_ref[u].astype(jnp.float32) for u in range(steps)], axis=0)
    fresh = fresh.astype(jnp.bfloat16)
    contract = (((1,), (1,)), ((), ()))
    scores = (
        lax.dot_general(queries, cache, contract, preferred_element_type=jnp.float32)
        * score_scale
    )
    scores = jnp.where(tags_ref[...] == mine, scores, masked_score)
    fresh_scores = (
        lax.dot_general(queries, fresh, contract, preferred_element_type=jnp.float32)
        * score_scale
    )
    step = lax.broadcasted_iota(jnp.int32, (rows, steps * per_owner), 0) // heads
    other = lax.broadcasted_iota(jnp.int32, (rows, steps * per_owner), 1)
    seen = (other % per_owner == mine) & (other // per_owner <= step)
    fresh_scores = jnp.where(seen, fresh_scores, masked_score)
    top_score = jnp.maximum(
        jnp.max(scores, axis=1, keepdims=True), jnp.max(fresh_scores, axis=1, keepdims=True)
    )
    weights = jnp.exp(scores - top_score)
    fresh_weights = jnp.exp(fresh_scores - top_score)
    denominator = jnp.sum(weights, axis=1, keepdims=True) + jnp.sum(
        fresh_weights, axis=1, keepdims=True
    )
    summed = jnp.dot(
        weights.astype(jnp.bfloat16), cache[:, :latent], preferred_element_type=jnp.float32
    ) + jnp.dot(
        fresh_weights.astype(jnp.bfloat16),
        fresh[:, :latent],
        preferred_element_type=jnp.float32,
    )
    context = (summed / denominator).astype(jnp.bfloat16)
    out_ref[...] = context.reshape(steps, 1, heads, latent)


def attend(queries, new_kv, arrived, crossed, first, tags):
    steps, per_owner, heads, width = queries.shape
    slots = tags.shape[1]
    latent = width - ROPE
    return pl.pallas_call(
        functools.partial(attend_kernel, first, len(arrived)),
        grid=(per_owner,),
        in_specs=[
            pl.BlockSpec((steps, 1, heads, width), lambda q: (0, q, 0, 0)),
            pl.BlockSpec((steps, per_owner, width), lambda q: (0, 0, 0)),
            pl.BlockSpec((1, slots), lambda q: (0, 0)),
        ]
        + [pl.BlockSpec(piece.shape, lambda q: (0, 0)) for piece in arrived + crossed],
        out_specs=pl.BlockSpec((steps, 1, heads, latent), lambda q: (0, q, 0, 0)),
        out_shape=jax.ShapeDtypeStruct((steps, per_owner, heads, latent), jnp.bfloat16),
        scratch_shapes=[pltpu.VMEM((slots, width), jnp.bfloat16)],
        compiler_params=pltpu.CompilerParams(vmem_limit_bytes=SCOPED_BYTES),
        cost_estimate=pl.CostEstimate(
            flops=2 * steps * per_owner * heads * slots * (width + latent),
            bytes_accessed=2 * steps * per_owner * heads * (width + latent),
            transcendentals=steps * per_owner * heads * slots,
        ),
        name="attend",
    )(queries, new_kv, tags, *arrived, *crossed)


def kept_kernel(orders, pieces, tiles, down_ref, *refs):
    arrived_refs, out_refs, sorted_ref = refs[:pieces], refs[pieces:-1], refs[-1]
    width = out_refs[0].shape[1]
    hidden_width = sorted_ref.shape[1]
    for part, (bits, out_ref) in enumerate(zip(orders, out_refs)):
        for place in range(pieces):
            ref, start, _ = blocks_of(apart_of(place, bits), arrived_refs, (None,) * 2, tiles)[0]
            copy_tiles(ref, start, 0, hidden_width // LANES, sorted_ref, place)
        out_ref[...] = jnp.dot(
            sorted_ref[...],
            down_ref[0, :, part * width : (part + 1) * width],
            preferred_element_type=jnp.float32,
        )


def sent_kernel(
    bits, first, pieces, tiles, down_ref, early_ref, late_ref, out_ref, sorted_ref
):
    width = out_ref.shape[1]
    hidden_width = sorted_ref.shape[1]
    for place in range(pieces):
        ref, start, _ = blocks_of(
            apart_of(place, bits), (None,) * pieces, (early_ref, late_ref), tiles
        )[1]
        copy_tiles(ref, start, 0, hidden_width // LANES, sorted_ref, place)
    result = jnp.dot(
        sorted_ref[...],
        down_ref[0, :, first : first + width],
        preferred_element_type=jnp.float32,
    )
    out_ref[...] = result.astype(jnp.bfloat16)


def expert_call(kernel, expert_down, arrays, pieces, outs, name):
    _, hidden_width, model_width = expert_down.shape
    slots = BLOCK * pieces
    vmem = pl.BlockSpec(memory_space=pltpu.VMEM)
    return pl.pallas_call(
        kernel,
        in_specs=[vmem] * (1 + len(arrays)),
        out_specs=[vmem] * len(outs),
        out_shape=outs,
        scratch_shapes=[pltpu.VMEM((slots, hidden_width), jnp.bfloat16)],
        compiler_params=pltpu.CompilerParams(vmem_limit_bytes=SCOPED_BYTES),
        cost_estimate=pl.CostEstimate(
            flops=2 * slots * hidden_width * sum(out.shape[1] for out in outs),
            bytes_accessed=2 * hidden_width * sum(out.shape[1] for out in outs),
            transcendentals=0,
        ),
        name=name,
    )(expert_down, *arrays)


after = lax.optimization_barrier


def swap(values, bit, devices):
    return lax.ppermute(values, "seq", [(i, i ^ bit) for i in range(devices)])


def fold(kept, received):
    total = kept + received.astype(jnp.float32)
    half = total.shape[0] // 2
    return total[:half], total[half:].astype(jnp.bfloat16)


def per_device_dense(
    prefill_kv,
    lengths,
    assignment,
    queries,
    new_kv,
    expert_hidden,
    routes,
    route_weights,
    expert_down,
):
    devices = lax.axis_size("seq")
    steps, per_owner = queries.shape[:2]
    rows, _, top, hidden_width = expert_hidden.shape
    model_width = expert_down.shape[2]
    outboxes = pack_outboxes(
        routes, route_weights, expert_hidden, lengths, assignment, prefill_kv, devices
    )
    chips = devices // 2
    tiles = (hidden_width + prefill_kv.shape[1]) // LANES
    arrived = [
        swap(outboxes[apart], 2 * apart, devices) if apart else outboxes[apart]
        for apart in CHIP_ORDER
    ]
    late_lengths, _ = after((lengths, arrived[1]))
    tags, down = load_down(
        late_lengths, assignment, expert_down, devices, per_owner, devices * BLOCK
    )
    late, _ = after((arrived[EARLY:], tags))
    crossed = [
        swap(jnp.concatenate([rows[tiles * BLOCK :] for rows in group], axis=0), 1, devices)
        for group in (arrived[:EARLY], late)
    ]

    orders = ((1, 2, 4), (2, 1, 4))
    width = model_width // len(orders)
    half = devices * BLOCK // 2
    kept = expert_call(
        functools.partial(kept_kernel, orders, chips, tiles),
        down,
        arrived,
        chips,
        (jax.ShapeDtypeStruct((half, width), jnp.float32),) * len(orders),
        "expert_kept",
    )
    crossed, kept = after((crossed, kept))
    flows = []
    for part, bits in enumerate(orders):
        (sent,) = expert_call(
            functools.partial(sent_kernel, bits, part * width, chips, tiles),
            down,
            crossed,
            chips,
            (jax.ShapeDtypeStruct((half, width), jnp.bfloat16),),
            "expert_sent",
        )
        flows.append((kept[part], swap(sent, 1, devices)))
    flows = [fold(kept, received) for kept, received in flows]
    received = [swap(sent, 2 * bits[0], devices) for (_, sent), bits in zip(flows, orders)]
    late_tags, _ = after((tags, [sent for _, sent in flows]))
    context = attend(queries, new_kv, arrived, crossed, hidden_width, late_tags)
    received[1], _ = after((received[1], context))
    flows = [fold(kept, got) for (kept, _), got in zip(flows, received)]
    received = [swap(sent, 2 * bits[1], devices) for (_, sent), bits in zip(flows, orders)]
    flows = [fold(kept, got) for (kept, _), got in zip(flows, received)]
    kept = jnp.concatenate([kept for kept, _ in flows], axis=1)
    sent = jnp.concatenate([sent for _, sent in flows], axis=1)
    received = swap(sent, 2 * orders[0][-1], devices)
    moe_out = (kept + received.astype(jnp.float32)).astype(jnp.bfloat16)
    return context, moe_out.reshape(rows, steps, model_width)


def per_device(*arrays):
    expert_hidden, expert_down = arrays[5], arrays[8]
    devices = lax.axis_size("seq")
    rows, steps, top = expert_hidden.shape[:3]
    tokens = rows * steps
    experts = expert_down.shape[0] * devices
    bound = max(2, 2 * tokens * top // experts)
    whole = expert_hidden.shape[3] % LANES == 0 and 2 * arrays[0].shape[1] % LANES == 0
    if whole and devices == 16 and experts == devices and tokens == BLOCK == bound:
        return per_device_dense(*arrays)
    return per_device_general(*arrays)


def solution(mesh):
    placed = (
        P(("groups", "seq"), None),
        P("groups"),
        P("groups"),
        P(None, ("groups", "seq"), None, None),
        P(None, ("groups", "seq"), None),
        P(("groups", "seq"), None, None, None),
        P(("groups", "seq"), None, None),
        P(("groups", "seq"), None, None),
        P("seq", None, None),
    )
    return jax.shard_map(
        per_device,
        mesh=mesh,
        in_specs=placed,
        out_specs=(P(None, ("groups", "seq"), None, None), P(("groups", "seq"), None, None)),
        check_vma=False,
    )
```

```python
import functools

import jax
import jax.numpy as jnp
from jax import lax
from jax.experimental import pallas as pl
from jax.experimental.pallas import tpu as pltpu
from jax.sharding import PartitionSpec as P

ROPE = 64
HALF = 2


score_scale = 192.0 ** (-0.5)
masked_score = -1e30


def slot_sources(slot_ids, slot_total):
    source_rows = jnp.arange(slot_ids.shape[0], dtype=jnp.int32)
    matched = slot_ids[None, :] == jnp.arange(slot_total, dtype=jnp.int32)[:, None]
    return jnp.max(jnp.where(matched, source_rows[None, :], -1), axis=1)


def fill_slots(values, sources, filler):
    taken = jnp.take(values, jnp.maximum(sources, 0), axis=0)
    valid = (sources >= 0).reshape((-1,) + (1,) * (values.ndim - 1))
    return jnp.where(valid, taken, jnp.asarray(filler, values.dtype))


def hand_over(prefill_kv, lengths, assignment, per_owner):
    device_count = lax.axis_size("seq")
    own_index = lax.axis_index("seq")
    ctx_here, kv_width = prefill_kv.shape
    position = jnp.arange(ctx_here, dtype=jnp.int32) * device_count + own_index
    request_ends = jnp.cumsum(lengths)
    request = jnp.sum((position[:, None] >= request_ends[None, :]).astype(jnp.int32), axis=1)
    total_rows = assignment.shape[0]
    row_numbers = jnp.arange(total_rows, dtype=jnp.int32)
    serving = jnp.sum(
        jnp.where(assignment[None, :] == row_numbers[:, None], row_numbers[None, :], 0), axis=1
    )
    decode_row = jnp.sum(
        jnp.where(request[:, None] == row_numbers[None, :], serving[None, :], 0), axis=1
    )
    owner_index = decode_row // per_owner
    local_request = decode_row % per_owner
    onehot = (owner_index[:, None] == jnp.arange(device_count, dtype=jnp.int32)[None, :]).astype(
        jnp.int32
    )
    slot_rank = jnp.sum((jnp.cumsum(onehot, axis=0) - onehot) * onehot, axis=1)
    slot_count = 2 * HALF * per_owner
    sources = slot_sources(owner_index * slot_count + slot_rank, device_count * slot_count)
    outbox = fill_slots(prefill_kv, sources, 0).reshape(device_count, slot_count, kv_width)
    labels = fill_slots(local_request, sources, -1).reshape(device_count, slot_count)
    kv_cache, cache_tags = (
        lax.all_to_all(outbox, "seq", split_axis=0, concat_axis=0, tiled=True),
        lax.all_to_all(labels, "seq", split_axis=0, concat_axis=0, tiled=True),
    )
    return (kv_cache.reshape(device_count * slot_count, kv_width), cache_tags.reshape(-1))


def fresh_part(queries, new_kv):
    step_count = queries.shape[0]
    fresh_scores = (
        jnp.einsum("sqhk,uqk->sqhu", queries, new_kv, preferred_element_type=jnp.float32)
        * score_scale
    )
    causal = jnp.arange(step_count)[:, None] >= jnp.arange(step_count)[None, :]
    return jnp.where(causal[:, None, None, :], fresh_scores, masked_score)


def attend_dense(queries, new_kv, kv_cache, cache_tags):
    step_count, per_owner, head_count, kv_width = queries.shape
    latent = kv_width - ROPE
    query_rows = queries.reshape(step_count * per_owner * head_count, kv_width)
    scores = (
        jnp.einsum("rk,ck->rc", query_rows, kv_cache, preferred_element_type=jnp.float32)
        * score_scale
    )
    row_request = jnp.broadcast_to(
        jnp.arange(per_owner, dtype=jnp.int32)[None, :, None], (step_count, per_owner, head_count)
    ).reshape(-1)
    allowed = cache_tags[None, :] == row_request[:, None]
    scores = jnp.where(allowed, scores, masked_score).reshape(step_count, per_owner, head_count, -1)
    fresh_scores = fresh_part(queries, new_kv)
    top_score = jnp.maximum(jnp.max(scores, axis=-1), jnp.max(fresh_scores, axis=-1))
    weights = jnp.exp(scores - top_score[..., None])
    fresh_weights = jnp.exp(fresh_scores - top_score[..., None])
    denominator = jnp.sum(weights, axis=-1) + jnp.sum(fresh_weights, axis=-1)
    summed = jnp.einsum(
        "sqhc,cl->sqhl",
        weights.astype(jnp.bfloat16),
        kv_cache[:, :latent],
        preferred_element_type=jnp.float32,
    )
    summed = summed + jnp.einsum(
        "sqhu,uql->sqhl",
        fresh_weights.astype(jnp.bfloat16),
        new_kv[..., :latent],
        preferred_element_type=jnp.float32,
    )
    return (summed / denominator[..., None]).astype(jnp.bfloat16)


def expert_layer(expert_hidden, routes, route_weights, expert_down):
    device_count = lax.axis_size("seq")
    rows_here, step_count, top_count, hidden_width = expert_hidden.shape
    per_dev = expert_down.shape[0]
    experts = per_dev * device_count
    capacity = max(2, 2 * step_count * rows_here * top_count // experts)
    flat_routes = routes.reshape(-1)
    route_count = flat_routes.shape[0]
    onehot = (flat_routes[:, None] == jnp.arange(experts, dtype=jnp.int32)[None, :]).astype(
        jnp.int32
    )
    slot_index = jnp.sum((jnp.cumsum(onehot, axis=0) - onehot) * onehot, axis=1)
    flat_hidden = expert_hidden.reshape(route_count, hidden_width)
    slot_ids = flat_routes * capacity + slot_index
    sources = slot_sources(slot_ids, experts * capacity)
    outbox = fill_slots(flat_hidden, sources, 0).reshape(
        device_count, per_dev, capacity, hidden_width
    )
    expert_out = jnp.einsum(
        "dekh,ehm->dekm",
        lax.all_to_all(outbox, "seq", split_axis=0, concat_axis=0, tiled=True),
        expert_down,
        preferred_element_type=jnp.float32,
    ).astype(jnp.bfloat16)
    returned = lax.all_to_all(expert_out, "seq", split_axis=0, concat_axis=0, tiled=True)
    returned = returned.reshape(experts * capacity, returned.shape[-1])
    picked = jnp.take(returned, slot_ids, axis=0).astype(jnp.float32)
    weighted = picked * route_weights.reshape(route_count, 1)
    moe_out = jnp.sum(weighted.reshape(rows_here, step_count, top_count, -1), axis=2)
    return moe_out.astype(jnp.bfloat16)


def per_device_general(
    prefill_kv,
    lengths,
    assignment,
    queries,
    new_kv,
    expert_hidden,
    routes,
    route_weights,
    expert_down,
):
    kv_cache, cache_tags = hand_over(prefill_kv, lengths, assignment, queries.shape[1])
    context = attend_dense(queries, new_kv, kv_cache, cache_tags)
    moe_out = expert_layer(expert_hidden, routes, route_weights, expert_down)
    return (context, moe_out)


BLOCK = 16
LANES = 128
CHIP_ORDER = (0, 6, 1, 4, 2, 5, 3, 7)
EARLY = 5
SOONER = (6, 4)
SCOPED_BYTES = 16 * 2**20


def as_column(row):
    size = row.shape[1]
    eye = lax.broadcasted_iota(jnp.int32, (size, size), 0) == lax.broadcasted_iota(
        jnp.int32, (size, size), 1
    )
    return jnp.sum(jnp.where(eye, row, 0), axis=1, keepdims=True)


def flat_row(table, tokens, top, precision):
    lanes = tokens * top
    place = lax.broadcasted_iota(jnp.int32, (top, lanes), 1) % top
    spread = (place == lax.broadcasted_iota(jnp.int32, (top, lanes), 0)).astype(jnp.float32)
    wide = jnp.dot(
        table, spread, precision=precision, preferred_element_type=jnp.float32
    )
    owner = lax.broadcasted_iota(jnp.int32, (tokens, lanes), 1) // top
    mine = owner == lax.broadcasted_iota(jnp.int32, (tokens, lanes), 0)
    return jnp.sum(jnp.where(mine, wide, 0.0), axis=0, keepdims=True)


def ceil_rows(position, source, devices):
    return (position + (devices - 1) - source) // devices


def request_spans(lengths_ref, assignment_ref):
    requests = lengths_ref.shape[1]
    length_column = as_column(lengths_ref[...])
    assignment = assignment_ref[...]
    number = lax.broadcasted_iota(jnp.int32, (requests, requests), 0)
    before = jnp.sum(jnp.where(number < assignment, length_column, 0), axis=0, keepdims=True)
    own = jnp.sum(jnp.where(number == assignment, length_column, 0), axis=0, keepdims=True)
    return before, before + own


def apart_of(place, bits):
    apart = place * 0
    for i, bit in enumerate(bits):
        digit = (place // (1 << (len(bits) - 1 - i))) % 2
        apart = apart + digit * bit
    return apart


def distance_of(block, chips):
    distance = block * 0
    for i, chip in enumerate(chips):
        distance = jnp.where(block // 2 == i, 2 * chip + block % 2, distance)
    return distance


def outbox_kernel(
    chosen_chips,
    devices,
    per_owner,
    routes_ref,
    weights_ref,
    hidden_ref,
    lengths_ref,
    assignment_ref,
    kv_ref,
    *out_refs,
):
    me = lax.axis_index("seq")
    room = BLOCK
    slots = 2 * room * len(chosen_chips)
    rows, steps, top = routes_ref.shape
    tokens = rows * steps
    lanes = tokens * top
    hidden_width = hidden_ref.shape[1]
    routes = jnp.concatenate([routes_ref[i] for i in range(rows)], axis=0).astype(jnp.float32)
    weights = jnp.concatenate([weights_ref[i] for i in range(rows)], axis=0)
    route_row = flat_row(routes, tokens, top, lax.Precision.DEFAULT).astype(jnp.int32)
    weight_row = flat_row(weights, tokens, top, lax.Precision.HIGHEST)
    slot = lax.broadcasted_iota(jnp.int32, (slots, lanes), 0)
    lane = lax.broadcasted_iota(jnp.int32, (slots, lanes), 1)
    target = me ^ distance_of(slot // room, chosen_chips)
    pick = (lane // top == slot % room) & (route_row == target)
    scale = jnp.sum(jnp.where(pick, weight_row, 0.0), axis=1, keepdims=True)
    chosen = jnp.where(pick, 1.0, 0.0).astype(jnp.bfloat16)
    moved = jnp.dot(chosen, hidden_ref[...], preferred_element_type=jnp.float32)
    moved = (moved * scale).astype(jnp.bfloat16)
    kv_width, here = kv_ref.shape
    tiles = (hidden_width + kv_width) // LANES
    for chip, out_ref in enumerate(out_refs):
        for block in range(2):
            start = (2 * chip + block) * room
            for tile in range(hidden_width // LANES):
                out_ref[(block * tiles + tile) * room : (block * tiles + tile + 1) * room, :] = (
                    moved[start : start + room, tile * LANES : (tile + 1) * LANES]
                )

    requests = lengths_ref.shape[1]
    before, after_last = request_spans(lengths_ref, assignment_ref)
    low = ceil_rows(before, me, devices)
    count = ceil_rows(after_last, me, devices) - low
    number = lax.broadcasted_iota(jnp.int32, (requests, requests), 0)
    line = lax.broadcasted_iota(jnp.int32, (requests, requests), 1)
    same = (number // per_owner == line // per_owner) & (number < line)
    offset = jnp.sum(jnp.where(same, as_column(count), 0), axis=0, keepdims=True)
    slot = lax.broadcasted_iota(jnp.int32, (slots, requests), 0)
    decode = lax.broadcasted_iota(jnp.int32, (slots, requests), 1)
    target = me ^ distance_of(slot // room, chosen_chips)
    rank = slot % room - offset
    held = (target == decode // per_owner) & (rank >= 0) & (rank < count)
    source = jnp.sum(jnp.where(held, low + rank + 1, 0), axis=1, keepdims=True) - 1
    pick = source == lax.broadcasted_iota(jnp.int32, (slots, here), 1)
    moved = lax.dot_general(
        jnp.where(pick, 1.0, 0.0).astype(jnp.bfloat16),
        kv_ref[...],
        (((1,), (1,)), ((), ())),
        preferred_element_type=jnp.float32,
    ).astype(jnp.bfloat16)
    whole = kv_width // LANES
    for chip, out_ref in enumerate(out_refs):
        ends = []
        for block in range(2):
            start = (2 * chip + block) * room
            for tile in range(whole):
                place = (block + 1) * tiles - whole + tile
                out_ref[place * room : (place + 1) * room, :] = moved[
                    start : start + room, tile * LANES : (tile + 1) * LANES
                ]
            ends.append(moved[start : start + room, whole * LANES :])
        out_ref[2 * tiles * room :, :] = jnp.concatenate(ends, axis=1)


def pack_outboxes(
    routes, route_weights, expert_hidden, lengths, assignment, prefill_kv, devices, chips
):
    rows, steps, top, hidden_width = expert_hidden.shape
    here, kv_width = prefill_kv.shape
    tokens = rows * steps
    slots = 2 * tokens * len(chips)
    tiles = (hidden_width + kv_width) // LANES
    operands = (
        routes,
        route_weights,
        expert_hidden.reshape(tokens * top, hidden_width),
        lengths.reshape(1, -1),
        assignment.reshape(1, -1),
        prefill_kv.T,
    )
    return pl.pallas_call(
        functools.partial(outbox_kernel, chips, devices, rows),
        out_shape=(jax.ShapeDtypeStruct(((2 * tiles + 1) * tokens, LANES), jnp.bfloat16),)
        * len(chips),
        compiler_params=pltpu.CompilerParams(vmem_limit_bytes=SCOPED_BYTES),
        cost_estimate=pl.CostEstimate(
            flops=2 * slots * (tokens * top * hidden_width + here * kv_width),
            bytes_accessed=4 * slots * (hidden_width + kv_width),
            transcendentals=0,
        ),
        name="pack_outboxes",
    )(*(pltpu.with_memory_space_constraint(x, pltpu.HBM) for x in operands))


def load_kernel(
    devices, per_owner, lengths_ref, assignment_ref, down_ref, tags_ref, held_ref, sem
):
    copy = pltpu.make_async_copy(down_ref, held_ref, sem)
    copy.start()
    me = lax.axis_index("seq")
    requests = lengths_ref.shape[1]
    slots = tags_ref.shape[1]
    room = slots // devices
    before, after = request_spans(lengths_ref, assignment_ref)
    place = lax.broadcasted_iota(jnp.int32, (1, slots), 1)
    sender, rank = me ^ (place // room), place % room
    tags = jnp.full((1, slots), -1, jnp.int32)
    decode = lax.broadcasted_iota(jnp.int32, (1, requests), 1)
    taken = jnp.zeros((1, slots), jnp.int32)
    for q in range(per_owner):
        mine = decode == me * per_owner + q
        first = jnp.sum(jnp.where(mine, before, 0), axis=1, keepdims=True)
        last = jnp.sum(jnp.where(mine, after, 0), axis=1, keepdims=True)
        arriving = ceil_rows(last, sender, devices) - ceil_rows(first, sender, devices)
        tags = jnp.where((rank >= taken) & (rank < taken + arriving), q, tags)
        taken = taken + arriving
    tags_ref[...] = tags
    copy.wait()


def load_down(lengths, assignment, expert_down, devices, per_owner, slots):
    vmem = pl.BlockSpec(memory_space=pltpu.VMEM)
    return pl.pallas_call(
        functools.partial(load_kernel, devices, per_owner),
        in_specs=[vmem, vmem, pl.BlockSpec(memory_space=pltpu.HBM)],
        out_specs=[vmem, vmem],
        out_shape=(
            jax.ShapeDtypeStruct((1, slots), jnp.int32),
            pltpu.VMEM(expert_down.shape, expert_down.dtype),
        ),
        scratch_shapes=[pltpu.SemaphoreType.DMA],
        compiler_params=pltpu.CompilerParams(vmem_limit_bytes=SCOPED_BYTES),
        cost_estimate=pl.CostEstimate(
            flops=0, bytes_accessed=2 * expert_down.size, transcendentals=0
        ),
        name="load_down",
    )(
        pltpu.with_memory_space_constraint(lengths.reshape(1, -1), pltpu.HBM),
        pltpu.with_memory_space_constraint(assignment.reshape(1, -1), pltpu.HBM),
        pltpu.with_memory_space_constraint(expert_down, pltpu.HBM),
    )


def blocks_of(chip, arrived_refs, crossed_refs, tiles):
    place = CHIP_ORDER.index(chip)
    late = place >= EARLY
    start = (place - EARLY * late) * (tiles + 1) * BLOCK
    return (arrived_refs[place], 0, tiles * BLOCK), (crossed_refs[late], start, 0)


def copy_tiles(ref, start, first, count, to_ref, place):
    for tile in range(count):
        at = start + (first + tile) * BLOCK
        to_ref[place * BLOCK : (place + 1) * BLOCK, tile * LANES : (tile + 1) * LANES] = ref[
            at : at + BLOCK, :
        ]


def attend_kernel(first, pieces, queries_ref, fresh_ref, tags_ref, *refs):
    arrived_refs, crossed_refs = refs[:pieces], refs[pieces:-2]
    out_ref, cache_ref = refs[-2:]
    mine = pl.program_id(0)
    kv_width = cache_ref.shape[1]
    whole = kv_width // LANES
    tiles = first // LANES + whole

    @pl.when(mine == 0)
    def _():
        for chip in range(pieces):
            for block, (ref, start, gap) in enumerate(
                blocks_of(chip, arrived_refs, crossed_refs, tiles)
            ):
                place = 2 * chip + block
                copy_tiles(ref, start, tiles - whole, whole, cache_ref, place)
                end = start + tiles * BLOCK + gap
                side = block * (kv_width - whole * LANES)
                cache_ref[place * BLOCK : (place + 1) * BLOCK, whole * LANES :] = ref[
                    end : end + BLOCK, side : side + kv_width - whole * LANES
                ]

    steps, _, heads, width = queries_ref.shape
    latent = out_ref.shape[3]
    per_owner = fresh_ref.shape[1]
    rows = steps * heads
    queries = queries_ref[...].reshape(rows, width)
    cache = cache_ref[...]
    fresh = jnp.concatenate([fresh_ref[u].astype(jnp.float32) for u in range(steps)], axis=0)
    fresh = fresh.astype(jnp.bfloat16)
    contract = (((1,), (1,)), ((), ()))
    scores = (
        lax.dot_general(queries, cache, contract, preferred_element_type=jnp.float32)
        * score_scale
    )
    scores = jnp.where(tags_ref[...] == mine, scores, masked_score)
    fresh_scores = (
        lax.dot_general(queries, fresh, contract, preferred_element_type=jnp.float32)
        * score_scale
    )
    step = lax.broadcasted_iota(jnp.int32, (rows, steps * per_owner), 0) // heads
    other = lax.broadcasted_iota(jnp.int32, (rows, steps * per_owner), 1)
    seen = (other % per_owner == mine) & (other // per_owner <= step)
    fresh_scores = jnp.where(seen, fresh_scores, masked_score)
    top_score = jnp.maximum(
        jnp.max(scores, axis=1, keepdims=True), jnp.max(fresh_scores, axis=1, keepdims=True)
    )
    weights = jnp.exp(scores - top_score)
    fresh_weights = jnp.exp(fresh_scores - top_score)
    denominator = jnp.sum(weights, axis=1, keepdims=True) + jnp.sum(
        fresh_weights, axis=1, keepdims=True
    )
    summed = jnp.dot(
        weights.astype(jnp.bfloat16), cache[:, :latent], preferred_element_type=jnp.float32
    ) + jnp.dot(
        fresh_weights.astype(jnp.bfloat16),
        fresh[:, :latent],
        preferred_element_type=jnp.float32,
    )
    context = (summed / denominator).astype(jnp.bfloat16)
    out_ref[...] = context.reshape(steps, 1, heads, latent)


def attend(queries, new_kv, arrived, crossed, first, tags):
    steps, per_owner, heads, width = queries.shape
    slots = tags.shape[1]
    latent = width - ROPE
    return pl.pallas_call(
        functools.partial(attend_kernel, first, len(arrived)),
        grid=(per_owner,),
        in_specs=[
            pl.BlockSpec((steps, 1, heads, width), lambda q: (0, q, 0, 0)),
            pl.BlockSpec((steps, per_owner, width), lambda q: (0, 0, 0)),
            pl.BlockSpec((1, slots), lambda q: (0, 0)),
        ]
        + [pl.BlockSpec(piece.shape, lambda q: (0, 0)) for piece in arrived + crossed],
        out_specs=pl.BlockSpec((steps, 1, heads, latent), lambda q: (0, q, 0, 0)),
        out_shape=jax.ShapeDtypeStruct((steps, per_owner, heads, latent), jnp.bfloat16),
        scratch_shapes=[pltpu.VMEM((slots, width), jnp.bfloat16)],
        compiler_params=pltpu.CompilerParams(vmem_limit_bytes=SCOPED_BYTES),
        cost_estimate=pl.CostEstimate(
            flops=2 * steps * per_owner * heads * slots * (width + latent),
            bytes_accessed=2 * steps * per_owner * heads * (width + latent),
            transcendentals=steps * per_owner * heads * slots,
        ),
        name="attend",
    )(queries, new_kv, tags, *arrived, *crossed)


def kept_kernel(orders, pieces, tiles, down_ref, *refs):
    arrived_refs, out_refs, sorted_ref = refs[:pieces], refs[pieces:-1], refs[-1]
    width = out_refs[0].shape[1]
    hidden_width = sorted_ref.shape[1]
    for part, (bits, out_ref) in enumerate(zip(orders, out_refs)):
        for place in range(pieces):
            ref, start, _ = blocks_of(apart_of(place, bits), arrived_refs, (None,) * 2, tiles)[0]
            copy_tiles(ref, start, 0, hidden_width // LANES, sorted_ref, place)
        out_ref[...] = jnp.dot(
            sorted_ref[...],
            down_ref[0, :, part * width : (part + 1) * width],
            preferred_element_type=jnp.float32,
        )


def sent_kernel(
    bits, first, pieces, tiles, down_ref, early_ref, late_ref, out_ref, sorted_ref
):
    width = out_ref.shape[1]
    hidden_width = sorted_ref.shape[1]
    for place in range(pieces):
        ref, start, _ = blocks_of(
            apart_of(place, bits), (None,) * pieces, (early_ref, late_ref), tiles
        )[1]
        copy_tiles(ref, start, 0, hidden_width // LANES, sorted_ref, place)
    result = jnp.dot(
        sorted_ref[...],
        down_ref[0, :, first : first + width],
        preferred_element_type=jnp.float32,
    )
    out_ref[...] = result.astype(jnp.bfloat16)


def expert_call(kernel, expert_down, arrays, pieces, outs, name):
    _, hidden_width, model_width = expert_down.shape
    slots = BLOCK * pieces
    vmem = pl.BlockSpec(memory_space=pltpu.VMEM)
    return pl.pallas_call(
        kernel,
        in_specs=[vmem] * (1 + len(arrays)),
        out_specs=[vmem] * len(outs),
        out_shape=outs,
        scratch_shapes=[pltpu.VMEM((slots, hidden_width), jnp.bfloat16)],
        compiler_params=pltpu.CompilerParams(vmem_limit_bytes=SCOPED_BYTES),
        cost_estimate=pl.CostEstimate(
            flops=2 * slots * hidden_width * sum(out.shape[1] for out in outs),
            bytes_accessed=2 * hidden_width * sum(out.shape[1] for out in outs),
            transcendentals=0,
        ),
        name=name,
    )(expert_down, *arrays)


after = lax.optimization_barrier


def swap(values, bit, devices):
    return lax.ppermute(values, "seq", [(i, i ^ bit) for i in range(devices)])


def fold(kept, received):
    total = kept + received.astype(jnp.float32)
    half = total.shape[0] // 2
    return total[:half], total[half:].astype(jnp.bfloat16)


def last_kernel(*refs):
    kept_refs, received_ref, out_ref = refs[:-2], refs[-2], refs[-1]
    rows, steps, _ = out_ref.shape
    first = 0
    for kept_ref in kept_refs:
        width = kept_ref.shape[1]
        columns = slice(first, first + width)
        total = kept_ref[...] + received_ref[:, columns].astype(jnp.float32)
        out_ref[:, :, columns] = total.reshape(rows, steps, width).astype(jnp.bfloat16)
        first += width


def last_sum(kept, received, rows, steps):
    width = received.shape[1]
    vmem = pl.BlockSpec(memory_space=pltpu.VMEM)
    return pl.pallas_call(
        last_kernel,
        in_specs=[vmem] * (len(kept) + 1),
        out_specs=vmem,
        out_shape=jax.ShapeDtypeStruct((rows, steps, width), jnp.bfloat16),
        compiler_params=pltpu.CompilerParams(vmem_limit_bytes=SCOPED_BYTES),
        cost_estimate=pl.CostEstimate(
            flops=rows * steps * width, bytes_accessed=8 * rows * steps * width, transcendentals=0
        ),
        name="last_sum",
    )(*kept, received)


def per_device_dense(
    prefill_kv,
    lengths,
    assignment,
    queries,
    new_kv,
    expert_hidden,
    routes,
    route_weights,
    expert_down,
):
    devices = lax.axis_size("seq")
    steps, per_owner = queries.shape[:2]
    rows, _, top, hidden_width = expert_hidden.shape
    model_width = expert_down.shape[2]
    outboxes = {}
    for group in (SOONER, tuple(chip for chip in sorted(CHIP_ORDER) if chip not in SOONER)):
        packed = pack_outboxes(
            routes, route_weights, expert_hidden, lengths, assignment, prefill_kv, devices, group
        )
        outboxes.update(zip(group, packed))
    chips = devices // 2
    tiles = (hidden_width + prefill_kv.shape[1]) // LANES
    arrived = [
        swap(outboxes[apart], 2 * apart, devices) if apart else outboxes[apart]
        for apart in CHIP_ORDER
    ]
    late_lengths, _ = after((lengths, arrived[1]))
    tags, down = load_down(
        late_lengths, assignment, expert_down, devices, per_owner, devices * BLOCK
    )
    late, _ = after((arrived[EARLY:], tags))
    crossed = [
        swap(jnp.concatenate([rows[tiles * BLOCK :] for rows in group], axis=0), 1, devices)
        for group in (arrived[:EARLY], late)
    ]

    orders = ((1, 2, 4), (2, 1, 4))
    width = model_width // len(orders)
    half = devices * BLOCK // 2
    kept = expert_call(
        functools.partial(kept_kernel, orders, chips, tiles),
        down,
        arrived,
        chips,
        (jax.ShapeDtypeStruct((half, width), jnp.float32),) * len(orders),
        "expert_kept",
    )
    crossed, kept = after((crossed, kept))
    flows = []
    for part, bits in enumerate(orders):
        (sent,) = expert_call(
            functools.partial(sent_kernel, bits, part * width, chips, tiles),
            down,
            crossed,
            chips,
            (jax.ShapeDtypeStruct((half, width), jnp.bfloat16),),
            "expert_sent",
        )
        flows.append((kept[part], swap(sent, 1, devices)))
    flows = [fold(kept, received) for kept, received in flows]
    received = [swap(sent, 2 * bits[0], devices) for (_, sent), bits in zip(flows, orders)]
    late_tags, _ = after((tags, [sent for _, sent in flows]))
    context = attend(queries, new_kv, arrived, crossed, hidden_width, late_tags)
    received[1], _ = after((received[1], context))
    flows = [fold(kept, got) for (kept, _), got in zip(flows, received)]
    received = [swap(sent, 2 * bits[1], devices) for (_, sent), bits in zip(flows, orders)]
    flows = [fold(kept, got) for (kept, _), got in zip(flows, received)]
    sent = jnp.concatenate([sent for _, sent in flows], axis=1)
    received = swap(sent, 2 * orders[0][-1], devices)
    moe_out = last_sum([kept for kept, _ in flows], received, rows, steps)
    return context, moe_out


def per_device(*arrays):
    expert_hidden, expert_down = arrays[5], arrays[8]
    devices = lax.axis_size("seq")
    rows, steps, top = expert_hidden.shape[:3]
    tokens = rows * steps
    experts = expert_down.shape[0] * devices
    bound = max(2, 2 * tokens * top // experts)
    whole = expert_hidden.shape[3] % LANES == 0 and 2 * arrays[0].shape[1] % LANES == 0
    if whole and devices == 16 and experts == devices and tokens == BLOCK == bound:
        return per_device_dense(*arrays)
    return per_device_general(*arrays)


def solution(mesh):
    placed = (
        P(("groups", "seq"), None),
        P("groups"),
        P("groups"),
        P(None, ("groups", "seq"), None, None),
        P(None, ("groups", "seq"), None),
        P(("groups", "seq"), None, None, None),
        P(("groups", "seq"), None, None),
        P(("groups", "seq"), None, None),
        P("seq", None, None),
    )
    return jax.shard_map(
        per_device,
        mesh=mesh,
        in_specs=placed,
        out_specs=(P(None, ("groups", "seq"), None, None), P(("groups", "seq"), None, None)),
        check_vma=False,
    )
```

```python
import functools

import jax
import jax.numpy as jnp
from jax import lax
from jax.experimental import pallas as pl
from jax.experimental.pallas import tpu as pltpu
from jax.sharding import PartitionSpec as P

ROPE = 64
HALF = 2


score_scale = 192.0 ** (-0.5)
masked_score = -1e30


def slot_sources(slot_ids, slot_total):
    source_rows = jnp.arange(slot_ids.shape[0], dtype=jnp.int32)
    matched = slot_ids[None, :] == jnp.arange(slot_total, dtype=jnp.int32)[:, None]
    return jnp.max(jnp.where(matched, source_rows[None, :], -1), axis=1)


def fill_slots(values, sources, filler):
    taken = jnp.take(values, jnp.maximum(sources, 0), axis=0)
    valid = (sources >= 0).reshape((-1,) + (1,) * (values.ndim - 1))
    return jnp.where(valid, taken, jnp.asarray(filler, values.dtype))


def hand_over(prefill_kv, lengths, assignment, per_owner):
    device_count = lax.axis_size("seq")
    own_index = lax.axis_index("seq")
    ctx_here, kv_width = prefill_kv.shape
    position = jnp.arange(ctx_here, dtype=jnp.int32) * device_count + own_index
    request_ends = jnp.cumsum(lengths)
    request = jnp.sum((position[:, None] >= request_ends[None, :]).astype(jnp.int32), axis=1)
    total_rows = assignment.shape[0]
    row_numbers = jnp.arange(total_rows, dtype=jnp.int32)
    serving = jnp.sum(
        jnp.where(assignment[None, :] == row_numbers[:, None], row_numbers[None, :], 0), axis=1
    )
    decode_row = jnp.sum(
        jnp.where(request[:, None] == row_numbers[None, :], serving[None, :], 0), axis=1
    )
    owner_index = decode_row // per_owner
    local_request = decode_row % per_owner
    onehot = (owner_index[:, None] == jnp.arange(device_count, dtype=jnp.int32)[None, :]).astype(
        jnp.int32
    )
    slot_rank = jnp.sum((jnp.cumsum(onehot, axis=0) - onehot) * onehot, axis=1)
    slot_count = 2 * HALF * per_owner
    sources = slot_sources(owner_index * slot_count + slot_rank, device_count * slot_count)
    outbox = fill_slots(prefill_kv, sources, 0).reshape(device_count, slot_count, kv_width)
    labels = fill_slots(local_request, sources, -1).reshape(device_count, slot_count)
    kv_cache, cache_tags = (
        lax.all_to_all(outbox, "seq", split_axis=0, concat_axis=0, tiled=True),
        lax.all_to_all(labels, "seq", split_axis=0, concat_axis=0, tiled=True),
    )
    return (kv_cache.reshape(device_count * slot_count, kv_width), cache_tags.reshape(-1))


def fresh_part(queries, new_kv):
    step_count = queries.shape[0]
    fresh_scores = (
        jnp.einsum("sqhk,uqk->sqhu", queries, new_kv, preferred_element_type=jnp.float32)
        * score_scale
    )
    causal = jnp.arange(step_count)[:, None] >= jnp.arange(step_count)[None, :]
    return jnp.where(causal[:, None, None, :], fresh_scores, masked_score)


def attend_dense(queries, new_kv, kv_cache, cache_tags):
    step_count, per_owner, head_count, kv_width = queries.shape
    latent = kv_width - ROPE
    query_rows = queries.reshape(step_count * per_owner * head_count, kv_width)
    scores = (
        jnp.einsum("rk,ck->rc", query_rows, kv_cache, preferred_element_type=jnp.float32)
        * score_scale
    )
    row_request = jnp.broadcast_to(
        jnp.arange(per_owner, dtype=jnp.int32)[None, :, None], (step_count, per_owner, head_count)
    ).reshape(-1)
    allowed = cache_tags[None, :] == row_request[:, None]
    scores = jnp.where(allowed, scores, masked_score).reshape(step_count, per_owner, head_count, -1)
    fresh_scores = fresh_part(queries, new_kv)
    top_score = jnp.maximum(jnp.max(scores, axis=-1), jnp.max(fresh_scores, axis=-1))
    weights = jnp.exp(scores - top_score[..., None])
    fresh_weights = jnp.exp(fresh_scores - top_score[..., None])
    denominator = jnp.sum(weights, axis=-1) + jnp.sum(fresh_weights, axis=-1)
    summed = jnp.einsum(
        "sqhc,cl->sqhl",
        weights.astype(jnp.bfloat16),
        kv_cache[:, :latent],
        preferred_element_type=jnp.float32,
    )
    summed = summed + jnp.einsum(
        "sqhu,uql->sqhl",
        fresh_weights.astype(jnp.bfloat16),
        new_kv[..., :latent],
        preferred_element_type=jnp.float32,
    )
    return (summed / denominator[..., None]).astype(jnp.bfloat16)


def expert_layer(expert_hidden, routes, route_weights, expert_down):
    device_count = lax.axis_size("seq")
    rows_here, step_count, top_count, hidden_width = expert_hidden.shape
    per_dev = expert_down.shape[0]
    experts = per_dev * device_count
    capacity = max(2, 2 * step_count * rows_here * top_count // experts)
    flat_routes = routes.reshape(-1)
    route_count = flat_routes.shape[0]
    onehot = (flat_routes[:, None] == jnp.arange(experts, dtype=jnp.int32)[None, :]).astype(
        jnp.int32
    )
    slot_index = jnp.sum((jnp.cumsum(onehot, axis=0) - onehot) * onehot, axis=1)
    flat_hidden = expert_hidden.reshape(route_count, hidden_width)
    slot_ids = flat_routes * capacity + slot_index
    sources = slot_sources(slot_ids, experts * capacity)
    outbox = fill_slots(flat_hidden, sources, 0).reshape(
        device_count, per_dev, capacity, hidden_width
    )
    expert_out = jnp.einsum(
        "dekh,ehm->dekm",
        lax.all_to_all(outbox, "seq", split_axis=0, concat_axis=0, tiled=True),
        expert_down,
        preferred_element_type=jnp.float32,
    ).astype(jnp.bfloat16)
    returned = lax.all_to_all(expert_out, "seq", split_axis=0, concat_axis=0, tiled=True)
    returned = returned.reshape(experts * capacity, returned.shape[-1])
    picked = jnp.take(returned, slot_ids, axis=0).astype(jnp.float32)
    weighted = picked * route_weights.reshape(route_count, 1)
    moe_out = jnp.sum(weighted.reshape(rows_here, step_count, top_count, -1), axis=2)
    return moe_out.astype(jnp.bfloat16)


def per_device_general(
    prefill_kv,
    lengths,
    assignment,
    queries,
    new_kv,
    expert_hidden,
    routes,
    route_weights,
    expert_down,
):
    kv_cache, cache_tags = hand_over(prefill_kv, lengths, assignment, queries.shape[1])
    context = attend_dense(queries, new_kv, kv_cache, cache_tags)
    moe_out = expert_layer(expert_hidden, routes, route_weights, expert_down)
    return (context, moe_out)


BLOCK = 16
LANES = 128
CHIP_ORDER = (0, 6, 1, 4, 2, 5, 3, 7)
EARLY = 5
SOONER = (6, 4)
SCOPED_BYTES = 16 * 2**20


def as_column(row):
    size = row.shape[1]
    eye = lax.broadcasted_iota(jnp.int32, (size, size), 0) == lax.broadcasted_iota(
        jnp.int32, (size, size), 1
    )
    return jnp.sum(jnp.where(eye, row, 0), axis=1, keepdims=True)


def flat_row(table, tokens, top, precision):
    lanes = tokens * top
    place = lax.broadcasted_iota(jnp.int32, (top, lanes), 1) % top
    spread = (place == lax.broadcasted_iota(jnp.int32, (top, lanes), 0)).astype(jnp.float32)
    wide = jnp.dot(
        table, spread, precision=precision, preferred_element_type=jnp.float32
    )
    owner = lax.broadcasted_iota(jnp.int32, (tokens, lanes), 1) // top
    mine = owner == lax.broadcasted_iota(jnp.int32, (tokens, lanes), 0)
    return jnp.sum(jnp.where(mine, wide, 0.0), axis=0, keepdims=True)


def ceil_rows(position, source, devices):
    return (position + (devices - 1) - source) // devices


def request_spans(lengths_ref, assignment_ref):
    requests = lengths_ref.shape[1]
    length_column = as_column(lengths_ref[...])
    assignment = assignment_ref[...]
    number = lax.broadcasted_iota(jnp.int32, (requests, requests), 0)
    before = jnp.sum(jnp.where(number < assignment, length_column, 0), axis=0, keepdims=True)
    own = jnp.sum(jnp.where(number == assignment, length_column, 0), axis=0, keepdims=True)
    return before, before + own


def apart_of(place, bits):
    apart = place * 0
    for i, bit in enumerate(bits):
        digit = (place // (1 << (len(bits) - 1 - i))) % 2
        apart = apart + digit * bit
    return apart


def distance_of(block, chips):
    distance = block * 0
    for i, chip in enumerate(chips):
        distance = jnp.where(block // 2 == i, 2 * chip + block % 2, distance)
    return distance


def outbox_kernel(
    chosen_chips,
    devices,
    per_owner,
    routes_ref,
    weights_ref,
    hidden_ref,
    lengths_ref,
    assignment_ref,
    kv_ref,
    *out_refs,
):
    me = lax.axis_index("seq")
    room = BLOCK
    slots = 2 * room * len(chosen_chips)
    rows, steps, top = routes_ref.shape
    tokens = rows * steps
    lanes = tokens * top
    hidden_width = hidden_ref.shape[1]
    routes = jnp.concatenate([routes_ref[i] for i in range(rows)], axis=0).astype(jnp.float32)
    weights = jnp.concatenate([weights_ref[i] for i in range(rows)], axis=0)
    route_row = flat_row(routes, tokens, top, lax.Precision.DEFAULT).astype(jnp.int32)
    weight_row = flat_row(weights, tokens, top, lax.Precision.HIGHEST)
    slot = lax.broadcasted_iota(jnp.int32, (slots, lanes), 0)
    lane = lax.broadcasted_iota(jnp.int32, (slots, lanes), 1)
    target = me ^ distance_of(slot // room, chosen_chips)
    pick = (lane // top == slot % room) & (route_row == target)
    scale = jnp.sum(jnp.where(pick, weight_row, 0.0), axis=1, keepdims=True)
    chosen = jnp.where(pick, 1.0, 0.0).astype(jnp.bfloat16)
    moved = jnp.dot(chosen, hidden_ref[...], preferred_element_type=jnp.float32)
    moved = (moved * scale).astype(jnp.bfloat16)
    kv_width, here = kv_ref.shape
    tiles = (hidden_width + kv_width) // LANES
    for chip, out_ref in enumerate(out_refs):
        for block in range(2):
            start = (2 * chip + block) * room
            for tile in range(hidden_width // LANES):
                out_ref[(block * tiles + tile) * room : (block * tiles + tile + 1) * room, :] = (
                    moved[start : start + room, tile * LANES : (tile + 1) * LANES]
                )

    requests = lengths_ref.shape[1]
    before, after_last = request_spans(lengths_ref, assignment_ref)
    low = ceil_rows(before, me, devices)
    count = ceil_rows(after_last, me, devices) - low
    number = lax.broadcasted_iota(jnp.int32, (requests, requests), 0)
    line = lax.broadcasted_iota(jnp.int32, (requests, requests), 1)
    same = (number // per_owner == line // per_owner) & (number < line)
    offset = jnp.sum(jnp.where(same, as_column(count), 0), axis=0, keepdims=True)
    slot = lax.broadcasted_iota(jnp.int32, (slots, requests), 0)
    decode = lax.broadcasted_iota(jnp.int32, (slots, requests), 1)
    target = me ^ distance_of(slot // room, chosen_chips)
    rank = slot % room - offset
    held = (target == decode // per_owner) & (rank >= 0) & (rank < count)
    source = jnp.sum(jnp.where(held, low + rank + 1, 0), axis=1, keepdims=True) - 1
    pick = source == lax.broadcasted_iota(jnp.int32, (slots, here), 1)
    moved = lax.dot_general(
        jnp.where(pick, 1.0, 0.0).astype(jnp.bfloat16),
        kv_ref[...],
        (((1,), (1,)), ((), ())),
        preferred_element_type=jnp.float32,
    ).astype(jnp.bfloat16)
    whole = kv_width // LANES
    for chip, out_ref in enumerate(out_refs):
        ends = []
        for block in range(2):
            start = (2 * chip + block) * room
            for tile in range(whole):
                place = (block + 1) * tiles - whole + tile
                out_ref[place * room : (place + 1) * room, :] = moved[
                    start : start + room, tile * LANES : (tile + 1) * LANES
                ]
            ends.append(moved[start : start + room, whole * LANES :])
        out_ref[2 * tiles * room :, :] = jnp.concatenate(ends, axis=1)


def pack_outboxes(
    routes, route_weights, expert_hidden, lengths, assignment, prefill_kv, devices, chips
):
    rows, steps, top, hidden_width = expert_hidden.shape
    here, kv_width = prefill_kv.shape
    tokens = rows * steps
    slots = 2 * tokens * len(chips)
    tiles = (hidden_width + kv_width) // LANES
    operands = (
        routes,
        route_weights,
        expert_hidden.reshape(tokens * top, hidden_width),
        lengths.reshape(1, -1),
        assignment.reshape(1, -1),
        prefill_kv.T,
    )
    return pl.pallas_call(
        functools.partial(outbox_kernel, chips, devices, rows),
        out_shape=(jax.ShapeDtypeStruct(((2 * tiles + 1) * tokens, LANES), jnp.bfloat16),)
        * len(chips),
        compiler_params=pltpu.CompilerParams(vmem_limit_bytes=SCOPED_BYTES),
        cost_estimate=pl.CostEstimate(
            flops=2 * slots * (tokens * top * hidden_width + here * kv_width),
            bytes_accessed=4 * slots * (hidden_width + kv_width),
            transcendentals=0,
        ),
        name="pack_outboxes",
    )(*(pltpu.with_memory_space_constraint(x, pltpu.HBM) for x in operands))


def load_kernel(
    devices, per_owner, lengths_ref, assignment_ref, down_ref, tags_ref, held_ref, sem
):
    copy = pltpu.make_async_copy(down_ref, held_ref, sem)
    copy.start()
    me = lax.axis_index("seq")
    requests = lengths_ref.shape[1]
    slots = tags_ref.shape[1]
    room = slots // devices
    before, after = request_spans(lengths_ref, assignment_ref)
    place = lax.broadcasted_iota(jnp.int32, (1, slots), 1)
    sender, rank = me ^ (place // room), place % room
    tags = jnp.full((1, slots), -1, jnp.int32)
    decode = lax.broadcasted_iota(jnp.int32, (1, requests), 1)
    taken = jnp.zeros((1, slots), jnp.int32)
    for q in range(per_owner):
        mine = decode == me * per_owner + q
        first = jnp.sum(jnp.where(mine, before, 0), axis=1, keepdims=True)
        last = jnp.sum(jnp.where(mine, after, 0), axis=1, keepdims=True)
        arriving = ceil_rows(last, sender, devices) - ceil_rows(first, sender, devices)
        tags = jnp.where((rank >= taken) & (rank < taken + arriving), q, tags)
        taken = taken + arriving
    tags_ref[...] = tags
    copy.wait()


def load_down(lengths, assignment, expert_down, devices, per_owner, slots):
    vmem = pl.BlockSpec(memory_space=pltpu.VMEM)
    return pl.pallas_call(
        functools.partial(load_kernel, devices, per_owner),
        in_specs=[vmem, vmem, pl.BlockSpec(memory_space=pltpu.HBM)],
        out_specs=[vmem, vmem],
        out_shape=(
            jax.ShapeDtypeStruct((1, slots), jnp.int32),
            pltpu.VMEM(expert_down.shape, expert_down.dtype),
        ),
        scratch_shapes=[pltpu.SemaphoreType.DMA],
        compiler_params=pltpu.CompilerParams(vmem_limit_bytes=SCOPED_BYTES),
        cost_estimate=pl.CostEstimate(
            flops=0, bytes_accessed=2 * expert_down.size, transcendentals=0
        ),
        name="load_down",
    )(
        pltpu.with_memory_space_constraint(lengths.reshape(1, -1), pltpu.HBM),
        pltpu.with_memory_space_constraint(assignment.reshape(1, -1), pltpu.HBM),
        pltpu.with_memory_space_constraint(expert_down, pltpu.HBM),
    )


def blocks_of(chip, arrived_refs, crossed_refs, tiles):
    place = CHIP_ORDER.index(chip)
    late = place >= EARLY
    start = (place - EARLY * late) * (tiles + 1) * BLOCK
    return (arrived_refs[place], 0, tiles * BLOCK), (crossed_refs[late], start, 0)


def copy_tiles(ref, start, first, count, to_ref, place):
    for tile in range(count):
        at = start + (first + tile) * BLOCK
        to_ref[place * BLOCK : (place + 1) * BLOCK, tile * LANES : (tile + 1) * LANES] = ref[
            at : at + BLOCK, :
        ]


def attend_kernel(first, pieces, queries_ref, fresh_ref, tags_ref, *refs):
    arrived_refs, crossed_refs = refs[:pieces], refs[pieces:-2]
    out_ref, cache_ref = refs[-2:]
    mine = pl.program_id(0)
    kv_width = cache_ref.shape[1]
    whole = kv_width // LANES
    tiles = first // LANES + whole

    @pl.when(mine == 0)
    def _():
        for chip in range(pieces):
            for block, (ref, start, gap) in enumerate(
                blocks_of(chip, arrived_refs, crossed_refs, tiles)
            ):
                place = 2 * chip + block
                copy_tiles(ref, start, tiles - whole, whole, cache_ref, place)
                end = start + tiles * BLOCK + gap
                side = block * (kv_width - whole * LANES)
                cache_ref[place * BLOCK : (place + 1) * BLOCK, whole * LANES :] = ref[
                    end : end + BLOCK, side : side + kv_width - whole * LANES
                ]

    steps, _, heads, width = queries_ref.shape
    latent = out_ref.shape[3]
    per_owner = fresh_ref.shape[1]
    rows = steps * heads
    queries = queries_ref[...].reshape(rows, width)
    cache = cache_ref[...]
    fresh = jnp.concatenate([fresh_ref[u].astype(jnp.float32) for u in range(steps)], axis=0)
    fresh = fresh.astype(jnp.bfloat16)
    contract = (((1,), (1,)), ((), ()))
    scores = (
        lax.dot_general(queries, cache, contract, preferred_element_type=jnp.float32)
        * score_scale
    )
    scores = jnp.where(tags_ref[...] == mine, scores, masked_score)
    fresh_scores = (
        lax.dot_general(queries, fresh, contract, preferred_element_type=jnp.float32)
        * score_scale
    )
    step = lax.broadcasted_iota(jnp.int32, (rows, steps * per_owner), 0) // heads
    other = lax.broadcasted_iota(jnp.int32, (rows, steps * per_owner), 1)
    seen = (other % per_owner == mine) & (other // per_owner <= step)
    fresh_scores = jnp.where(seen, fresh_scores, masked_score)
    top_score = jnp.maximum(
        jnp.max(scores, axis=1, keepdims=True), jnp.max(fresh_scores, axis=1, keepdims=True)
    )
    weights = jnp.exp(scores - top_score)
    fresh_weights = jnp.exp(fresh_scores - top_score)
    denominator = jnp.sum(weights, axis=1, keepdims=True) + jnp.sum(
        fresh_weights, axis=1, keepdims=True
    )
    summed = jnp.dot(
        weights.astype(jnp.bfloat16), cache[:, :latent], preferred_element_type=jnp.float32
    ) + jnp.dot(
        fresh_weights.astype(jnp.bfloat16),
        fresh[:, :latent],
        preferred_element_type=jnp.float32,
    )
    context = (summed / denominator).astype(jnp.bfloat16)
    out_ref[...] = context.reshape(steps, 1, heads, latent)


def attend(queries, new_kv, arrived, crossed, first, tags):
    steps, per_owner, heads, width = queries.shape
    slots = tags.shape[1]
    latent = width - ROPE
    return pl.pallas_call(
        functools.partial(attend_kernel, first, len(arrived)),
        grid=(per_owner,),
        in_specs=[
            pl.BlockSpec((steps, 1, heads, width), lambda q: (0, q, 0, 0)),
            pl.BlockSpec((steps, per_owner, width), lambda q: (0, 0, 0)),
            pl.BlockSpec((1, slots), lambda q: (0, 0)),
        ]
        + [pl.BlockSpec(piece.shape, lambda q: (0, 0)) for piece in arrived + crossed],
        out_specs=pl.BlockSpec((steps, 1, heads, latent), lambda q: (0, q, 0, 0)),
        out_shape=jax.ShapeDtypeStruct((steps, per_owner, heads, latent), jnp.bfloat16),
        scratch_shapes=[pltpu.VMEM((slots, width), jnp.bfloat16)],
        compiler_params=pltpu.CompilerParams(vmem_limit_bytes=SCOPED_BYTES),
        cost_estimate=pl.CostEstimate(
            flops=2 * steps * per_owner * heads * slots * (width + latent),
            bytes_accessed=2 * steps * per_owner * heads * (width + latent),
            transcendentals=steps * per_owner * heads * slots,
        ),
        name="attend",
    )(queries, new_kv, tags, *arrived, *crossed)


def kept_kernel(orders, pieces, tiles, down_ref, *refs):
    arrived_refs, out_refs, sorted_ref = refs[:pieces], refs[pieces:-1], refs[-1]
    width = out_refs[0].shape[1]
    hidden_width = sorted_ref.shape[1]
    for part, (bits, out_ref) in enumerate(zip(orders, out_refs)):
        for place in range(pieces):
            ref, start, _ = blocks_of(apart_of(place, bits), arrived_refs, (None,) * 2, tiles)[0]
            copy_tiles(ref, start, 0, hidden_width // LANES, sorted_ref, place)
        out_ref[...] = jnp.dot(
            sorted_ref[...],
            down_ref[0, :, part * width : (part + 1) * width],
            preferred_element_type=jnp.float32,
        )


def sent_kernel(
    bits, first, pieces, tiles, down_ref, early_ref, late_ref, out_ref, sorted_ref
):
    width = out_ref.shape[1]
    hidden_width = sorted_ref.shape[1]
    for place in range(pieces):
        ref, start, _ = blocks_of(
            apart_of(place, bits), (None,) * pieces, (early_ref, late_ref), tiles
        )[1]
        copy_tiles(ref, start, 0, hidden_width // LANES, sorted_ref, place)
    result = jnp.dot(
        sorted_ref[...],
        down_ref[0, :, first : first + width],
        preferred_element_type=jnp.float32,
    )
    out_ref[...] = result.astype(jnp.bfloat16)


def expert_call(kernel, expert_down, arrays, pieces, outs, name):
    _, hidden_width, model_width = expert_down.shape
    slots = BLOCK * pieces
    vmem = pl.BlockSpec(memory_space=pltpu.VMEM)
    return pl.pallas_call(
        kernel,
        in_specs=[vmem] * (1 + len(arrays)),
        out_specs=[vmem] * len(outs),
        out_shape=outs,
        scratch_shapes=[pltpu.VMEM((slots, hidden_width), jnp.bfloat16)],
        compiler_params=pltpu.CompilerParams(vmem_limit_bytes=SCOPED_BYTES),
        cost_estimate=pl.CostEstimate(
            flops=2 * slots * hidden_width * sum(out.shape[1] for out in outs),
            bytes_accessed=2 * hidden_width * sum(out.shape[1] for out in outs),
            transcendentals=0,
        ),
        name=name,
    )(expert_down, *arrays)


after = lax.optimization_barrier


def swap(values, bit, devices):
    return lax.ppermute(values, "seq", [(i, i ^ bit) for i in range(devices)])


def fold(kept, received):
    total = kept + received.astype(jnp.float32)
    half = total.shape[0] // 2
    return total[:half], total[half:].astype(jnp.bfloat16)


def last_kernel(*refs):
    kept_refs, received_ref, out_ref = refs[:-2], refs[-2], refs[-1]
    rows, steps, _ = out_ref.shape
    first = 0
    for kept_ref in kept_refs:
        width = kept_ref.shape[1]
        columns = slice(first, first + width)
        total = kept_ref[...] + received_ref[:, columns].astype(jnp.float32)
        out_ref[:, :, columns] = total.reshape(rows, steps, width).astype(jnp.bfloat16)
        first += width


def last_sum(kept, received, rows, steps):
    width = received.shape[1]
    vmem = pl.BlockSpec(memory_space=pltpu.VMEM)
    return pl.pallas_call(
        last_kernel,
        in_specs=[vmem] * (len(kept) + 1),
        out_specs=vmem,
        out_shape=jax.ShapeDtypeStruct((rows, steps, width), jnp.bfloat16),
        compiler_params=pltpu.CompilerParams(vmem_limit_bytes=SCOPED_BYTES),
        cost_estimate=pl.CostEstimate(
            flops=rows * steps * width, bytes_accessed=8 * rows * steps * width, transcendentals=0
        ),
        name="last_sum",
    )(*kept, received)


def per_device_dense(
    prefill_kv,
    lengths,
    assignment,
    queries,
    new_kv,
    expert_hidden,
    routes,
    route_weights,
    expert_down,
):
    devices = lax.axis_size("seq")
    steps, per_owner = queries.shape[:2]
    rows, _, top, hidden_width = expert_hidden.shape
    model_width = expert_down.shape[2]
    outboxes = {}
    for group in (SOONER, tuple(chip for chip in sorted(CHIP_ORDER) if chip not in SOONER)):
        packed = pack_outboxes(
            routes, route_weights, expert_hidden, lengths, assignment, prefill_kv, devices, group
        )
        outboxes.update(zip(group, packed))
    chips = devices // 2
    tiles = (hidden_width + prefill_kv.shape[1]) // LANES
    arrived = [
        swap(outboxes[apart], 2 * apart, devices) if apart else outboxes[apart]
        for apart in CHIP_ORDER
    ]
    late_lengths, _ = after((lengths, arrived[1]))
    tags, down = load_down(
        late_lengths, assignment, expert_down, devices, per_owner, devices * BLOCK
    )
    late, _ = after((arrived[EARLY:], tags))
    crossed = [
        swap(jnp.concatenate([rows[tiles * BLOCK :] for rows in group], axis=0), 1, devices)
        for group in (arrived[:EARLY], late)
    ]

    orders = ((2, 1, 4), (1, 2, 4))
    width = model_width // len(orders)
    half = devices * BLOCK // 2
    kept = expert_call(
        functools.partial(kept_kernel, orders, chips, tiles),
        down,
        arrived,
        chips,
        (jax.ShapeDtypeStruct((half, width), jnp.float32),) * len(orders),
        "expert_kept",
    )
    crossed, kept = after((crossed, kept))
    flows = []
    for part, bits in enumerate(orders):
        (sent,) = expert_call(
            functools.partial(sent_kernel, bits, part * width, chips, tiles),
            down,
            crossed,
            chips,
            (jax.ShapeDtypeStruct((half, width), jnp.bfloat16),),
            "expert_sent",
        )
        flows.append((kept[part], swap(sent, 1, devices)))
    flows = [fold(kept, received) for kept, received in flows]
    received = [swap(sent, 2 * bits[0], devices) for (_, sent), bits in zip(flows, orders)]
    late_tags, _ = after((tags, [sent for _, sent in flows]))
    context = attend(queries, new_kv, arrived, crossed, hidden_width, late_tags)
    received[1], _ = after((received[1], context))
    flows = [fold(kept, got) for (kept, _), got in zip(flows, received)]
    received = [swap(sent, 2 * bits[1], devices) for (_, sent), bits in zip(flows, orders)]
    flows = [fold(kept, got) for (kept, _), got in zip(flows, received)]
    sent = jnp.concatenate([sent for _, sent in flows], axis=1)
    received = swap(sent, 2 * orders[0][-1], devices)
    moe_out = last_sum([kept for kept, _ in flows], received, rows, steps)
    return context, moe_out


def per_device(*arrays):
    expert_hidden, expert_down = arrays[5], arrays[8]
    devices = lax.axis_size("seq")
    rows, steps, top = expert_hidden.shape[:3]
    tokens = rows * steps
    experts = expert_down.shape[0] * devices
    bound = max(2, 2 * tokens * top // experts)
    whole = expert_hidden.shape[3] % LANES == 0 and 2 * arrays[0].shape[1] % LANES == 0
    if whole and devices == 16 and experts == devices and tokens == BLOCK == bound:
        return per_device_dense(*arrays)
    return per_device_general(*arrays)


def solution(mesh):
    placed = (
        P(("groups", "seq"), None),
        P("groups"),
        P("groups"),
        P(None, ("groups", "seq"), None, None),
        P(None, ("groups", "seq"), None),
        P(("groups", "seq"), None, None, None),
        P(("groups", "seq"), None, None),
        P(("groups", "seq"), None, None),
        P("seq", None, None),
    )
    return jax.shard_map(
        per_device,
        mesh=mesh,
        in_specs=placed,
        out_specs=(P(None, ("groups", "seq"), None, None), P(("groups", "seq"), None, None)),
        check_vma=False,
    )
```

```python
import functools

import jax
import jax.numpy as jnp
from jax import lax
from jax.experimental import pallas as pl
from jax.experimental.pallas import tpu as pltpu
from jax.sharding import PartitionSpec as P

ROPE = 64
HALF = 2


score_scale = 192.0 ** (-0.5)
masked_score = -1e30


def slot_sources(slot_ids, slot_total):
    source_rows = jnp.arange(slot_ids.shape[0], dtype=jnp.int32)
    matched = slot_ids[None, :] == jnp.arange(slot_total, dtype=jnp.int32)[:, None]
    return jnp.max(jnp.where(matched, source_rows[None, :], -1), axis=1)


def fill_slots(values, sources, filler):
    taken = jnp.take(values, jnp.maximum(sources, 0), axis=0)
    valid = (sources >= 0).reshape((-1,) + (1,) * (values.ndim - 1))
    return jnp.where(valid, taken, jnp.asarray(filler, values.dtype))


def hand_over(prefill_kv, lengths, assignment, per_owner):
    device_count = lax.axis_size("seq")
    own_index = lax.axis_index("seq")
    ctx_here, kv_width = prefill_kv.shape
    position = jnp.arange(ctx_here, dtype=jnp.int32) * device_count + own_index
    request_ends = jnp.cumsum(lengths)
    request = jnp.sum((position[:, None] >= request_ends[None, :]).astype(jnp.int32), axis=1)
    total_rows = assignment.shape[0]
    row_numbers = jnp.arange(total_rows, dtype=jnp.int32)
    serving = jnp.sum(
        jnp.where(assignment[None, :] == row_numbers[:, None], row_numbers[None, :], 0), axis=1
    )
    decode_row = jnp.sum(
        jnp.where(request[:, None] == row_numbers[None, :], serving[None, :], 0), axis=1
    )
    owner_index = decode_row // per_owner
    local_request = decode_row % per_owner
    onehot = (owner_index[:, None] == jnp.arange(device_count, dtype=jnp.int32)[None, :]).astype(
        jnp.int32
    )
    slot_rank = jnp.sum((jnp.cumsum(onehot, axis=0) - onehot) * onehot, axis=1)
    slot_count = 2 * HALF * per_owner
    sources = slot_sources(owner_index * slot_count + slot_rank, device_count * slot_count)
    outbox = fill_slots(prefill_kv, sources, 0).reshape(device_count, slot_count, kv_width)
    labels = fill_slots(local_request, sources, -1).reshape(device_count, slot_count)
    kv_cache, cache_tags = (
        lax.all_to_all(outbox, "seq", split_axis=0, concat_axis=0, tiled=True),
        lax.all_to_all(labels, "seq", split_axis=0, concat_axis=0, tiled=True),
    )
    return (kv_cache.reshape(device_count * slot_count, kv_width), cache_tags.reshape(-1))


def fresh_part(queries, new_kv):
    step_count = queries.shape[0]
    fresh_scores = (
        jnp.einsum("sqhk,uqk->sqhu", queries, new_kv, preferred_element_type=jnp.float32)
        * score_scale
    )
    causal = jnp.arange(step_count)[:, None] >= jnp.arange(step_count)[None, :]
    return jnp.where(causal[:, None, None, :], fresh_scores, masked_score)


def attend_dense(queries, new_kv, kv_cache, cache_tags):
    step_count, per_owner, head_count, kv_width = queries.shape
    latent = kv_width - ROPE
    query_rows = queries.reshape(step_count * per_owner * head_count, kv_width)
    scores = (
        jnp.einsum("rk,ck->rc", query_rows, kv_cache, preferred_element_type=jnp.float32)
        * score_scale
    )
    row_request = jnp.broadcast_to(
        jnp.arange(per_owner, dtype=jnp.int32)[None, :, None], (step_count, per_owner, head_count)
    ).reshape(-1)
    allowed = cache_tags[None, :] == row_request[:, None]
    scores = jnp.where(allowed, scores, masked_score).reshape(step_count, per_owner, head_count, -1)
    fresh_scores = fresh_part(queries, new_kv)
    top_score = jnp.maximum(jnp.max(scores, axis=-1), jnp.max(fresh_scores, axis=-1))
    weights = jnp.exp(scores - top_score[..., None])
    fresh_weights = jnp.exp(fresh_scores - top_score[..., None])
    denominator = jnp.sum(weights, axis=-1) + jnp.sum(fresh_weights, axis=-1)
    summed = jnp.einsum(
        "sqhc,cl->sqhl",
        weights.astype(jnp.bfloat16),
        kv_cache[:, :latent],
        preferred_element_type=jnp.float32,
    )
    summed = summed + jnp.einsum(
        "sqhu,uql->sqhl",
        fresh_weights.astype(jnp.bfloat16),
        new_kv[..., :latent],
        preferred_element_type=jnp.float32,
    )
    return (summed / denominator[..., None]).astype(jnp.bfloat16)


def expert_layer(expert_hidden, routes, route_weights, expert_down):
    device_count = lax.axis_size("seq")
    rows_here, step_count, top_count, hidden_width = expert_hidden.shape
    per_dev = expert_down.shape[0]
    experts = per_dev * device_count
    capacity = max(2, 2 * step_count * rows_here * top_count // experts)
    flat_routes = routes.reshape(-1)
    route_count = flat_routes.shape[0]
    onehot = (flat_routes[:, None] == jnp.arange(experts, dtype=jnp.int32)[None, :]).astype(
        jnp.int32
    )
    slot_index = jnp.sum((jnp.cumsum(onehot, axis=0) - onehot) * onehot, axis=1)
    flat_hidden = expert_hidden.reshape(route_count, hidden_width)
    slot_ids = flat_routes * capacity + slot_index
    sources = slot_sources(slot_ids, experts * capacity)
    outbox = fill_slots(flat_hidden, sources, 0).reshape(
        device_count, per_dev, capacity, hidden_width
    )
    expert_out = jnp.einsum(
        "dekh,ehm->dekm",
        lax.all_to_all(outbox, "seq", split_axis=0, concat_axis=0, tiled=True),
        expert_down,
        preferred_element_type=jnp.float32,
    ).astype(jnp.bfloat16)
    returned = lax.all_to_all(expert_out, "seq", split_axis=0, concat_axis=0, tiled=True)
    returned = returned.reshape(experts * capacity, returned.shape[-1])
    picked = jnp.take(returned, slot_ids, axis=0).astype(jnp.float32)
    weighted = picked * route_weights.reshape(route_count, 1)
    moe_out = jnp.sum(weighted.reshape(rows_here, step_count, top_count, -1), axis=2)
    return moe_out.astype(jnp.bfloat16)


def per_device_general(
    prefill_kv,
    lengths,
    assignment,
    queries,
    new_kv,
    expert_hidden,
    routes,
    route_weights,
    expert_down,
):
    kv_cache, cache_tags = hand_over(prefill_kv, lengths, assignment, queries.shape[1])
    context = attend_dense(queries, new_kv, kv_cache, cache_tags)
    moe_out = expert_layer(expert_hidden, routes, route_weights, expert_down)
    return (context, moe_out)


BLOCK = 16
LANES = 128
CHIP_ORDER = (0, 6, 1, 4, 2, 5, 3, 7)
EARLY = 5
SOONER = (6, 4)
SCOPED_BYTES = 16 * 2**20


def as_column(row):
    size = row.shape[1]
    eye = lax.broadcasted_iota(jnp.int32, (size, size), 0) == lax.broadcasted_iota(
        jnp.int32, (size, size), 1
    )
    return jnp.sum(jnp.where(eye, row, 0), axis=1, keepdims=True)


def flat_row(table, tokens, top, precision):
    lanes = tokens * top
    place = lax.broadcasted_iota(jnp.int32, (top, lanes), 1) % top
    spread = (place == lax.broadcasted_iota(jnp.int32, (top, lanes), 0)).astype(jnp.float32)
    wide = jnp.dot(
        table, spread, precision=precision, preferred_element_type=jnp.float32
    )
    owner = lax.broadcasted_iota(jnp.int32, (tokens, lanes), 1) // top
    mine = owner == lax.broadcasted_iota(jnp.int32, (tokens, lanes), 0)
    return jnp.sum(jnp.where(mine, wide, 0.0), axis=0, keepdims=True)


def ceil_rows(position, source, devices):
    return (position + (devices - 1) - source) // devices


def request_spans(lengths_ref, assignment_ref):
    requests = lengths_ref.shape[1]
    length_column = as_column(lengths_ref[...])
    assignment = assignment_ref[...]
    number = lax.broadcasted_iota(jnp.int32, (requests, requests), 0)
    before = jnp.sum(jnp.where(number < assignment, length_column, 0), axis=0, keepdims=True)
    own = jnp.sum(jnp.where(number == assignment, length_column, 0), axis=0, keepdims=True)
    return before, before + own


def apart_of(place, bits):
    apart = place * 0
    for i, bit in enumerate(bits):
        digit = (place // (1 << (len(bits) - 1 - i))) % 2
        apart = apart + digit * bit
    return apart


def distance_of(block, chips):
    distance = block * 0
    for i, chip in enumerate(chips):
        distance = jnp.where(block // 2 == i, 2 * chip + block % 2, distance)
    return distance


def outbox_kernel(
    chosen_chips,
    devices,
    per_owner,
    routes_ref,
    weights_ref,
    hidden_ref,
    lengths_ref,
    assignment_ref,
    kv_ref,
    *out_refs,
):
    me = lax.axis_index("seq")
    room = BLOCK
    slots = 2 * room * len(chosen_chips)
    rows, steps, top = routes_ref.shape
    tokens = rows * steps
    lanes = tokens * top
    hidden_width = hidden_ref.shape[1]
    routes = jnp.concatenate([routes_ref[i] for i in range(rows)], axis=0).astype(jnp.float32)
    weights = jnp.concatenate([weights_ref[i] for i in range(rows)], axis=0)
    route_row = flat_row(routes, tokens, top, lax.Precision.DEFAULT).astype(jnp.int32)
    weight_row = flat_row(weights, tokens, top, lax.Precision.HIGHEST)
    slot = lax.broadcasted_iota(jnp.int32, (slots, lanes), 0)
    lane = lax.broadcasted_iota(jnp.int32, (slots, lanes), 1)
    target = me ^ distance_of(slot // room, chosen_chips)
    pick = (lane // top == slot % room) & (route_row == target)
    scale = jnp.sum(jnp.where(pick, weight_row, 0.0), axis=1, keepdims=True)
    chosen = jnp.where(pick, 1.0, 0.0).astype(jnp.bfloat16)
    moved = jnp.dot(chosen, hidden_ref[...], preferred_element_type=jnp.float32)
    moved = (moved * scale).astype(jnp.bfloat16)
    kv_width, here = kv_ref.shape
    tiles = (hidden_width + kv_width) // LANES
    for chip, out_ref in enumerate(out_refs):
        for block in range(2):
            start = (2 * chip + block) * room
            for tile in range(hidden_width // LANES):
                out_ref[(block * tiles + tile) * room : (block * tiles + tile + 1) * room, :] = (
                    moved[start : start + room, tile * LANES : (tile + 1) * LANES]
                )

    requests = lengths_ref.shape[1]
    before, after_last = request_spans(lengths_ref, assignment_ref)
    low = ceil_rows(before, me, devices)
    count = ceil_rows(after_last, me, devices) - low
    number = lax.broadcasted_iota(jnp.int32, (requests, requests), 0)
    line = lax.broadcasted_iota(jnp.int32, (requests, requests), 1)
    same = (number // per_owner == line // per_owner) & (number < line)
    offset = jnp.sum(jnp.where(same, as_column(count), 0), axis=0, keepdims=True)
    slot = lax.broadcasted_iota(jnp.int32, (slots, requests), 0)
    decode = lax.broadcasted_iota(jnp.int32, (slots, requests), 1)
    target = me ^ distance_of(slot // room, chosen_chips)
    rank = slot % room - offset
    held = (target == decode // per_owner) & (rank >= 0) & (rank < count)
    source = jnp.sum(jnp.where(held, low + rank + 1, 0), axis=1, keepdims=True) - 1
    pick = source == lax.broadcasted_iota(jnp.int32, (slots, here), 1)
    moved = lax.dot_general(
        jnp.where(pick, 1.0, 0.0).astype(jnp.bfloat16),
        kv_ref[...],
        (((1,), (1,)), ((), ())),
        preferred_element_type=jnp.float32,
    ).astype(jnp.bfloat16)
    whole = kv_width // LANES
    for chip, out_ref in enumerate(out_refs):
        ends = []
        for block in range(2):
            start = (2 * chip + block) * room
            for tile in range(whole):
                place = (block + 1) * tiles - whole + tile
                out_ref[place * room : (place + 1) * room, :] = moved[
                    start : start + room, tile * LANES : (tile + 1) * LANES
                ]
            ends.append(moved[start : start + room, whole * LANES :])
        out_ref[2 * tiles * room :, :] = jnp.concatenate(ends, axis=1)


def pack_outboxes(
    routes, route_weights, expert_hidden, lengths, assignment, prefill_kv, devices, chips
):
    rows, steps, top, hidden_width = expert_hidden.shape
    here, kv_width = prefill_kv.shape
    tokens = rows * steps
    slots = 2 * tokens * len(chips)
    tiles = (hidden_width + kv_width) // LANES
    operands = (
        routes,
        route_weights,
        expert_hidden.reshape(tokens * top, hidden_width),
        lengths.reshape(1, -1),
        assignment.reshape(1, -1),
        prefill_kv.T,
    )
    return pl.pallas_call(
        functools.partial(outbox_kernel, chips, devices, rows),
        out_shape=(jax.ShapeDtypeStruct(((2 * tiles + 1) * tokens, LANES), jnp.bfloat16),)
        * len(chips),
        compiler_params=pltpu.CompilerParams(vmem_limit_bytes=SCOPED_BYTES),
        cost_estimate=pl.CostEstimate(
            flops=2 * slots * (tokens * top * hidden_width + here * kv_width),
            bytes_accessed=4 * slots * (hidden_width + kv_width),
            transcendentals=0,
        ),
        name="pack_outboxes",
    )(*(pltpu.with_memory_space_constraint(x, pltpu.HBM) for x in operands))


def load_kernel(
    devices, per_owner, lengths_ref, assignment_ref, down_ref, tags_ref, held_ref, sem
):
    copy = pltpu.make_async_copy(down_ref, held_ref, sem)
    copy.start()
    me = lax.axis_index("seq")
    requests = lengths_ref.shape[1]
    slots = tags_ref.shape[1]
    room = slots // devices
    before, after = request_spans(lengths_ref, assignment_ref)
    place = lax.broadcasted_iota(jnp.int32, (1, slots), 1)
    sender, rank = me ^ (place // room), place % room
    tags = jnp.full((1, slots), -1, jnp.int32)
    decode = lax.broadcasted_iota(jnp.int32, (1, requests), 1)
    taken = jnp.zeros((1, slots), jnp.int32)
    for q in range(per_owner):
        mine = decode == me * per_owner + q
        first = jnp.sum(jnp.where(mine, before, 0), axis=1, keepdims=True)
        last = jnp.sum(jnp.where(mine, after, 0), axis=1, keepdims=True)
        arriving = ceil_rows(last, sender, devices) - ceil_rows(first, sender, devices)
        tags = jnp.where((rank >= taken) & (rank < taken + arriving), q, tags)
        taken = taken + arriving
    tags_ref[...] = tags
    copy.wait()


def load_down(lengths, assignment, expert_down, devices, per_owner, slots):
    vmem = pl.BlockSpec(memory_space=pltpu.VMEM)
    return pl.pallas_call(
        functools.partial(load_kernel, devices, per_owner),
        in_specs=[vmem, vmem, pl.BlockSpec(memory_space=pltpu.HBM)],
        out_specs=[vmem, vmem],
        out_shape=(
            jax.ShapeDtypeStruct((1, slots), jnp.int32),
            pltpu.VMEM(expert_down.shape, expert_down.dtype),
        ),
        scratch_shapes=[pltpu.SemaphoreType.DMA],
        compiler_params=pltpu.CompilerParams(vmem_limit_bytes=SCOPED_BYTES),
        cost_estimate=pl.CostEstimate(
            flops=0, bytes_accessed=2 * expert_down.size, transcendentals=0
        ),
        name="load_down",
    )(
        pltpu.with_memory_space_constraint(lengths.reshape(1, -1), pltpu.HBM),
        pltpu.with_memory_space_constraint(assignment.reshape(1, -1), pltpu.HBM),
        pltpu.with_memory_space_constraint(expert_down, pltpu.HBM),
    )


def blocks_of(chip, arrived_refs, crossed_refs, tiles):
    place = CHIP_ORDER.index(chip)
    late = place >= EARLY
    start = (place - EARLY * late) * (tiles + 1) * BLOCK
    return (arrived_refs[place], 0, tiles * BLOCK), (crossed_refs[late], start, 0)


def copy_tiles(ref, start, first, count, to_ref, place):
    for tile in range(count):
        at = start + (first + tile) * BLOCK
        to_ref[place * BLOCK : (place + 1) * BLOCK, tile * LANES : (tile + 1) * LANES] = ref[
            at : at + BLOCK, :
        ]


def attend_kernel(first, pieces, queries_ref, fresh_ref, tags_ref, *refs):
    arrived_refs, crossed_refs = refs[:pieces], refs[pieces:-2]
    out_ref, cache_ref = refs[-2:]
    mine = pl.program_id(0)
    kv_width = cache_ref.shape[1]
    whole = kv_width // LANES
    tiles = first // LANES + whole

    @pl.when(mine == 0)
    def _():
        for chip in range(pieces):
            for block, (ref, start, gap) in enumerate(
                blocks_of(chip, arrived_refs, crossed_refs, tiles)
            ):
                place = 2 * chip + block
                copy_tiles(ref, start, tiles - whole, whole, cache_ref, place)
                end = start + tiles * BLOCK + gap
                side = block * (kv_width - whole * LANES)
                cache_ref[place * BLOCK : (place + 1) * BLOCK, whole * LANES :] = ref[
                    end : end + BLOCK, side : side + kv_width - whole * LANES
                ]

    steps, _, heads, width = queries_ref.shape
    latent = out_ref.shape[3]
    per_owner = fresh_ref.shape[1]
    rows = steps * heads
    queries = queries_ref[...].reshape(rows, width)
    cache = cache_ref[...]
    fresh = jnp.concatenate([fresh_ref[u].astype(jnp.float32) for u in range(steps)], axis=0)
    fresh = fresh.astype(jnp.bfloat16)
    contract = (((1,), (1,)), ((), ()))
    scores = (
        lax.dot_general(queries, cache, contract, preferred_element_type=jnp.float32)
        * score_scale
    )
    scores = jnp.where(tags_ref[...] == mine, scores, masked_score)
    fresh_scores = (
        lax.dot_general(queries, fresh, contract, preferred_element_type=jnp.float32)
        * score_scale
    )
    step = lax.broadcasted_iota(jnp.int32, (rows, steps * per_owner), 0) // heads
    other = lax.broadcasted_iota(jnp.int32, (rows, steps * per_owner), 1)
    seen = (other % per_owner == mine) & (other // per_owner <= step)
    fresh_scores = jnp.where(seen, fresh_scores, masked_score)
    top_score = jnp.maximum(
        jnp.max(scores, axis=1, keepdims=True), jnp.max(fresh_scores, axis=1, keepdims=True)
    )
    weights = jnp.exp(scores - top_score)
    fresh_weights = jnp.exp(fresh_scores - top_score)
    denominator = jnp.sum(weights, axis=1, keepdims=True) + jnp.sum(
        fresh_weights, axis=1, keepdims=True
    )
    summed = jnp.dot(
        weights.astype(jnp.bfloat16), cache[:, :latent], preferred_element_type=jnp.float32
    ) + jnp.dot(
        fresh_weights.astype(jnp.bfloat16),
        fresh[:, :latent],
        preferred_element_type=jnp.float32,
    )
    context = (summed / denominator).astype(jnp.bfloat16)
    out_ref[...] = context.reshape(steps, 1, heads, latent)


def attend(queries, new_kv, arrived, crossed, first, tags):
    steps, per_owner, heads, width = queries.shape
    slots = tags.shape[1]
    latent = width - ROPE
    return pl.pallas_call(
        functools.partial(attend_kernel, first, len(arrived)),
        grid=(per_owner,),
        in_specs=[
            pl.BlockSpec((steps, 1, heads, width), lambda q: (0, q, 0, 0)),
            pl.BlockSpec((steps, per_owner, width), lambda q: (0, 0, 0)),
            pl.BlockSpec((1, slots), lambda q: (0, 0)),
        ]
        + [pl.BlockSpec(piece.shape, lambda q: (0, 0)) for piece in arrived + crossed],
        out_specs=pl.BlockSpec((steps, 1, heads, latent), lambda q: (0, q, 0, 0)),
        out_shape=jax.ShapeDtypeStruct((steps, per_owner, heads, latent), jnp.bfloat16),
        scratch_shapes=[pltpu.VMEM((slots, width), jnp.bfloat16)],
        compiler_params=pltpu.CompilerParams(vmem_limit_bytes=SCOPED_BYTES),
        cost_estimate=pl.CostEstimate(
            flops=2 * steps * per_owner * heads * slots * (width + latent),
            bytes_accessed=2 * steps * per_owner * heads * (width + latent),
            transcendentals=steps * per_owner * heads * slots,
        ),
        name="attend",
    )(queries, new_kv, tags, *arrived, *crossed)


def kept_kernel(orders, pieces, tiles, down_ref, *refs):
    arrived_refs, out_refs, sorted_ref = refs[:pieces], refs[pieces:-1], refs[-1]
    width = out_refs[0].shape[1]
    hidden_width = sorted_ref.shape[1]
    for part, (bits, out_ref) in enumerate(zip(orders, out_refs)):
        for place in range(pieces):
            ref, start, _ = blocks_of(apart_of(place, bits), arrived_refs, (None,) * 2, tiles)[0]
            copy_tiles(ref, start, 0, hidden_width // LANES, sorted_ref, place)
        out_ref[...] = jnp.dot(
            sorted_ref[...],
            down_ref[0, :, part * width : (part + 1) * width],
            preferred_element_type=jnp.float32,
        )


def sent_kernel(
    bits, first, pieces, tiles, down_ref, early_ref, late_ref, out_ref, sorted_ref
):
    width = out_ref.shape[1]
    hidden_width = sorted_ref.shape[1]
    for place in range(pieces):
        ref, start, _ = blocks_of(
            apart_of(place, bits), (None,) * pieces, (early_ref, late_ref), tiles
        )[1]
        copy_tiles(ref, start, 0, hidden_width // LANES, sorted_ref, place)
    result = jnp.dot(
        sorted_ref[...],
        down_ref[0, :, first : first + width],
        preferred_element_type=jnp.float32,
    )
    out_ref[...] = result.astype(jnp.bfloat16)


def expert_call(kernel, expert_down, arrays, pieces, outs, name):
    _, hidden_width, model_width = expert_down.shape
    slots = BLOCK * pieces
    vmem = pl.BlockSpec(memory_space=pltpu.VMEM)
    return pl.pallas_call(
        kernel,
        in_specs=[vmem] * (1 + len(arrays)),
        out_specs=[vmem] * len(outs),
        out_shape=outs,
        scratch_shapes=[pltpu.VMEM((slots, hidden_width), jnp.bfloat16)],
        compiler_params=pltpu.CompilerParams(vmem_limit_bytes=SCOPED_BYTES),
        cost_estimate=pl.CostEstimate(
            flops=2 * slots * hidden_width * sum(out.shape[1] for out in outs),
            bytes_accessed=2 * hidden_width * sum(out.shape[1] for out in outs),
            transcendentals=0,
        ),
        name=name,
    )(expert_down, *arrays)


after = lax.optimization_barrier


def swap(values, bit, devices):
    return lax.ppermute(values, "seq", [(i, i ^ bit) for i in range(devices)])


def fold(kept, received):
    total = kept + received.astype(jnp.float32)
    half = total.shape[0] // 2
    return total[:half], total[half:].astype(jnp.bfloat16)


def last_kernel(*refs):
    kept_refs, received_ref, out_ref = refs[:-2], refs[-2], refs[-1]
    rows, steps, _ = out_ref.shape
    first = 0
    for kept_ref in kept_refs:
        width = kept_ref.shape[1]
        columns = slice(first, first + width)
        total = kept_ref[...] + received_ref[:, columns].astype(jnp.float32)
        out_ref[:, :, columns] = total.reshape(rows, steps, width).astype(jnp.bfloat16)
        first += width


def last_sum(kept, received, rows, steps):
    width = received.shape[1]
    vmem = pl.BlockSpec(memory_space=pltpu.VMEM)
    return pl.pallas_call(
        last_kernel,
        in_specs=[vmem] * (len(kept) + 1),
        out_specs=vmem,
        out_shape=jax.ShapeDtypeStruct((rows, steps, width), jnp.bfloat16),
        compiler_params=pltpu.CompilerParams(vmem_limit_bytes=SCOPED_BYTES),
        cost_estimate=pl.CostEstimate(
            flops=rows * steps * width, bytes_accessed=8 * rows * steps * width, transcendentals=0
        ),
        name="last_sum",
    )(*kept, received)


def per_device_dense(
    prefill_kv,
    lengths,
    assignment,
    queries,
    new_kv,
    expert_hidden,
    routes,
    route_weights,
    expert_down,
):
    devices = lax.axis_size("seq")
    steps, per_owner = queries.shape[:2]
    rows, _, top, hidden_width = expert_hidden.shape
    model_width = expert_down.shape[2]
    outboxes = {}
    for group in (SOONER, tuple(chip for chip in sorted(CHIP_ORDER) if chip not in SOONER)):
        packed = pack_outboxes(
            routes, route_weights, expert_hidden, lengths, assignment, prefill_kv, devices, group
        )
        outboxes.update(zip(group, packed))
    chips = devices // 2
    tiles = (hidden_width + prefill_kv.shape[1]) // LANES
    arrived = [
        swap(outboxes[apart], 2 * apart, devices) if apart else outboxes[apart]
        for apart in CHIP_ORDER
    ]
    late_lengths, _ = after((lengths, arrived[1]))
    tags, down = load_down(
        late_lengths, assignment, expert_down, devices, per_owner, devices * BLOCK
    )
    late, _ = after((arrived[EARLY:], tags))
    crossed = [
        swap(jnp.concatenate([rows[tiles * BLOCK :] for rows in group], axis=0), 1, devices)
        for group in (arrived[:EARLY], late)
    ]

    orders = ((2, 1, 4), (1, 2, 4))
    width = model_width // len(orders)
    half = devices * BLOCK // 2
    kept = expert_call(
        functools.partial(kept_kernel, orders, chips, tiles),
        down,
        arrived,
        chips,
        (jax.ShapeDtypeStruct((half, width), jnp.float32),) * len(orders),
        "expert_kept",
    )
    crossed, kept = after((crossed, kept))
    flows = []
    for part, bits in enumerate(orders):
        (sent,) = expert_call(
            functools.partial(sent_kernel, bits, part * width, chips, tiles),
            down,
            crossed,
            chips,
            (jax.ShapeDtypeStruct((half, width), jnp.bfloat16),),
            "expert_sent",
        )
        flows.append((kept[part], swap(sent, 1, devices)))
    flows = [fold(kept, received) for kept, received in flows]
    received = [swap(sent, 2 * bits[0], devices) for (_, sent), bits in zip(flows, orders)]
    late_tags, _ = after((tags, [sent for _, sent in flows]))
    context = attend(queries, new_kv, arrived, crossed, hidden_width, late_tags)
    received[0], _ = after((received[0], context))
    flows = [fold(kept, got) for (kept, _), got in zip(flows, received)]
    received = [swap(sent, 2 * bits[1], devices) for (_, sent), bits in zip(flows, orders)]
    flows = [fold(kept, got) for (kept, _), got in zip(flows, received)]
    sent = jnp.concatenate([sent for _, sent in flows], axis=1)
    received = swap(sent, 2 * orders[0][-1], devices)
    moe_out = last_sum([kept for kept, _ in flows], received, rows, steps)
    return context, moe_out


def per_device(*arrays):
    expert_hidden, expert_down = arrays[5], arrays[8]
    devices = lax.axis_size("seq")
    rows, steps, top = expert_hidden.shape[:3]
    tokens = rows * steps
    experts = expert_down.shape[0] * devices
    bound = max(2, 2 * tokens * top // experts)
    whole = expert_hidden.shape[3] % LANES == 0 and 2 * arrays[0].shape[1] % LANES == 0
    if whole and devices == 16 and experts == devices and tokens == BLOCK == bound:
        return per_device_dense(*arrays)
    return per_device_general(*arrays)


def solution(mesh):
    placed = (
        P(("groups", "seq"), None),
        P("groups"),
        P("groups"),
        P(None, ("groups", "seq"), None, None),
        P(None, ("groups", "seq"), None),
        P(("groups", "seq"), None, None, None),
        P(("groups", "seq"), None, None),
        P(("groups", "seq"), None, None),
        P("seq", None, None),
    )
    return jax.shard_map(
        per_device,
        mesh=mesh,
        in_specs=placed,
        out_specs=(P(None, ("groups", "seq"), None, None), P(("groups", "seq"), None, None)),
        check_vma=False,
    )
```
